128 devices in a mesh: role: 2 (over core), dev: 64 (over x, y, z).
Axes of the slice: x: 4, y: 4, z: 4, core: 2. Of those that a mesh axis runs over, the one named last changes fastest.
Arguments:
- initial_realizations: bfloat16 [64, 69, 128, 384], P('dev', None, 'role'), may hold values from -6 to 15, as said below
- diffusivity: float32 [69], replicated, may hold values from 0.05 to 0.24
- w_in: bfloat16 [512, 69], replicated, may hold values from -0.75 to 0.75
- b_in: float32 [512], replicated, may hold values from -4 to 4
- w_out: bfloat16 [69, 512], replicated, may hold values from -0.25 to 0.25
- obs_index: int32 [768, 128], P('role'), may hold values from 0 to 4415
- obs_value: float32 [768, 128], P(('role', 'dev')), may hold values from -8 to 8
- obs_weight: float32 [768, 128], P(('role', 'dev')), may hold values from 0.1 to 1
- climate: float32 [1], replicated, may hold values from -3 to 3
Outputs:
- analysis: bfloat16 [64, 69, 128, 384], P('dev', None, 'role')
The draws below stay inside these ranges and needn't reach their ends.
Inputs may be any that keep to these rules, and one draw needn't show every extreme that they name: `initial_realizations`: field 0 carries a latitude-dependent offset. `obs_index`: entry f * 64 + a * 8 + b of a patch is field f at the cell a rows and b columns from the patch's first corner.
All inputs are finite; a program needn't handle non-finite values.
Results may differ from the reference program's by a relative error of at most 0.0071.
Values may be sent and summed in bfloat16 or wider, within the bound.
No kernel may reach another device: no remote copies, remote signals or barrier semaphores. Data moves between devices by JAX's collectives and lax.ppermute only.
A program may use at most 192 MiB of HBM per device.

```python
import math
import jax
import jax.numpy as jnp
from jax import lax

EVOLVED_VARS = 69
LATENT = 512
LON = 384
TILE_EDGE_POINTS = 8
OBS = 128
STEPS = 2
NS_ITERS = 12
MEMBERSHIP_TALLY = 64
CELLS = 64
NLAT = 128
PATCHES = 768


def draw_initial_realizations(key, part):
    key = jax.random.fold_in(key, 11)
    first = jax.random.fold_in(key, 0)
    shape = (MEMBERSHIP_TALLY, EVOLVED_VARS, NLAT, LON)
    latitude = jnp.arange(NLAT, dtype=jnp.float32)[None, None, :, None] / (NLAT - 1.0)
    reference_profile = jnp.clip(jax.random.normal(first, shape, jnp.float32), -5.0, 5.0)
    grid_displacement = 1.0 + 3.0 * latitude
    thermal_distribution = (jnp.arange(EVOLVED_VARS) == 0)[None, :, None, None]
    return (reference_profile + jnp.where(thermal_distribution, grid_displacement, 0.0)).astype(jnp.bfloat16)


def plant(array, own_key, low, high):
    spot = [jax.random.randint(jax.random.fold_in(own_key, axis), (), 0, length) for axis, length in enumerate(array.shape)]
    main_axis = array.shape.index(max(array.shape))
    neighbour = spot[:main_axis] + [(spot[main_axis] + 1) % array.shape[main_axis]] + spot[main_axis + 1:]
    return array.at[tuple(spot)].set(low).at[tuple(neighbour)].set(high)


def block_scale(stream_key, extent, cuts, least, largest):
    level, own = 1.0, jax.random.fold_in(stream_key, 6)
    for position, blocks in cuts:
        draws = jnp.exp(jax.random.uniform(jax.random.fold_in(own, position), (blocks,), jnp.float32, least / len(cuts), largest / len(cuts)))
        level = level * jnp.repeat(draws, extent[position] // blocks).reshape([-1 if axis == position else 1 for axis in range(len(extent))])
    return level


def noise(stream_key, extent, scale, bound, cuts=(), kind=jnp.bfloat16):
    result = scale * jax.random.normal(stream_key, extent, jnp.float32)
    if cuts:
        result = result * block_scale(stream_key, extent, cuts, -0.22, 0.18)
    return jnp.clip(result, -bound, bound).astype(kind)


def setup_inputs(seed: int = 0) -> dict:
    seeds = jax.random.split(jax.random.key(seed), 10)
    initial_realizations = draw_initial_realizations(jax.random.fold_in(seeds[9], 71), 0)
    diffusivity = jnp.clip(jnp.exp(jax.random.uniform(seeds[1], (EVOLVED_VARS,), jnp.float32, math.log(0.05), math.log(0.24))), 0.05, 0.24)
    w_in = noise(seeds[2], (LATENT, EVOLVED_VARS), EVOLVED_VARS ** -0.5, 0.75)
    b_in = noise(seeds[3], (LATENT,), 1.0, 4.0, (), jnp.float32)
    w_out = noise(seeds[4], (EVOLVED_VARS, LATENT), LATENT ** -0.5, 0.25)
    obs_index = plant(jax.random.randint(seeds[5], (PATCHES, OBS), 0, EVOLVED_VARS * CELLS), jax.random.fold_in(seeds[5], 1), 0, (EVOLVED_VARS * CELLS) - 1).astype(jnp.int32)
    obs_value = noise(seeds[6], (PATCHES, OBS), 1.5, 8.0, ((0, 128),), jnp.float32)
    obs_weight = jnp.clip(jnp.exp(math.log(1.0) - 2.3025851 * jax.random.uniform(seeds[7], (PATCHES, OBS), jnp.float32) ** block_scale(seeds[7], (PATCHES, OBS), ((0, 128),), -0.2, 0.2)), 0.1, 1.0)
    climate = noise(seeds[8], (1,), 1.0, 3.0, (), jnp.float32)
    return {"initial_realizations": initial_realizations, "diffusivity": diffusivity, "w_in": w_in, "b_in": b_in, "w_out": w_out, "obs_index": obs_index, "obs_value": obs_value, "obs_weight": obs_weight, "climate": climate}


HIGH = lax.Precision.HIGHEST

def advance_member(current, diffusivity, w_in, b_in, w_out):
    centre = current.astype(jnp.float32)
    padded = jnp.pad(centre, ((0, 0), (1, 1), (0, 0)))
    laplace = padded[:, 2:] + padded[:, :-2] + jnp.roll(centre, 1, 2) + jnp.roll(centre, -1, 2) - 4.0 * centre
    smooth = (centre + diffusivity[:, None, None] * laplace).astype(jnp.bfloat16)
    flat = smooth.reshape(EVOLVED_VARS, NLAT * LON)
    linear = jnp.dot(w_in, flat, preferred_element_type=jnp.float32) + b_in[:, None]
    hidden = jax.nn.gelu(linear).astype(jnp.bfloat16)
    change = jnp.dot(w_out, hidden, preferred_element_type=jnp.float32).reshape(EVOLVED_VARS, NLAT, LON)
    return (centre + change).astype(jnp.bfloat16)

def analyze_patch(pieces):
    block, index, value, weight = pieces
    values = block.astype(jnp.float32)
    mean = lax.optimization_barrier(jnp.mean(values, axis=0))
    spread = values - mean[None]
    observed = jnp.take(values, index, axis=1)
    obs_mean = lax.optimization_barrier(jnp.mean(observed, axis=0))
    obs_spread = observed - obs_mean[None]
    innovation = value - obs_mean
    weighted = obs_spread * weight[None]
    identity = jnp.eye(MEMBERSHIP_TALLY, dtype=jnp.float32)
    precision_matrix = (MEMBERSHIP_TALLY - 1.0) * identity + jnp.dot(weighted, obs_spread.T, precision=HIGH)
    scale = MEMBERSHIP_TALLY * jnp.trace(precision_matrix)

    def newton(counter, carry):
        iterate, root = carry
        factor = 0.5 * (3.0 * identity - jnp.dot(root, iterate, precision=HIGH))
        return (jnp.dot(iterate, factor, precision=HIGH), jnp.dot(factor, root, precision=HIGH))
    iterate, root = lax.fori_loop(0, NS_ITERS, newton, (precision_matrix / scale, identity))
    transform = jnp.sqrt((MEMBERSHIP_TALLY - 1.0) / scale) * root
    pulled = jnp.dot(weighted, innovation, precision=HIGH)
    shift = jnp.dot(root, jnp.dot(root, pulled, precision=HIGH), precision=HIGH) / scale
    combined = transform + shift[:, None]
    return mean[None] + jnp.dot(combined.T, spread, precision=HIGH)

def reference(initial_realizations, diffusivity, w_in, b_in, w_out, obs_index, obs_value, obs_weight, climate):

    def predict_lone_realization(realization_vector):
        for section in range(STEPS):
            realization_vector = advance_member(realization_vector, diffusivity, w_in, b_in, w_out)
        return realization_vector
    predict_realizations = lax.map(predict_lone_realization, initial_realizations)
    tiles_across_latitude = NLAT // TILE_EDGE_POINTS
    tiles_across_longitude = LON // TILE_EDGE_POINTS
    tile_partition = predict_realizations.reshape(MEMBERSHIP_TALLY, EVOLVED_VARS, tiles_across_latitude, TILE_EDGE_POINTS, tiles_across_longitude, TILE_EDGE_POINTS)
    tile_partition = tile_partition.transpose(2, 4, 0, 1, 3, 5).reshape(PATCHES, MEMBERSHIP_TALLY, EVOLVED_VARS * CELLS)
    updated = lax.map(analyze_patch, (tile_partition, obs_index, obs_value, obs_weight))
    tmean = jnp.sum(updated[:, :, :CELLS]) / (MEMBERSHIP_TALLY * NLAT * LON)
    nudged = updated.at[:, :, :CELLS].add(climate[0] - tmean).astype(jnp.bfloat16)
    nudged = nudged.reshape(tiles_across_latitude, tiles_across_longitude, MEMBERSHIP_TALLY, EVOLVED_VARS, TILE_EDGE_POINTS, TILE_EDGE_POINTS)
    return nudged.transpose(2, 3, 0, 4, 1, 5).reshape(MEMBERSHIP_TALLY, EVOLVED_VARS, NLAT, LON)
```

```python
import jax
import jax.numpy as jnp
from jax import lax
from jax.experimental import pallas as pl
from jax.experimental.pallas import tpu as pltpu
from jax.sharding import PartitionSpec as P

EDGE = 8
NS_ITERS = 12
CELLS = 64
LANES = 128
FIELDS = 69
PADDED = 72
LATENT = 512
LON = 384
TILES = 3
ROWS = 64
MEMBERS = 64
OBS = 128
GROUP = 16
BLOCK = 256
VMEM = 56 * 1024 * 1024
GELU_A = 0.7978845608028654
GELU_B = 0.044715 * 0.7978845608028654
VALUES = MEMBERS * 128 * LON

ANY_VMEM = pl.BlockSpec(memory_space=pltpu.VMEM)
ANY_SMEM = pl.BlockSpec(memory_space=pltpu.SMEM)


def params():
    return pltpu.CompilerParams(vmem_limit_bytes=VMEM)


def mlp(smooth, w_in, w_out):
    total = None
    for part in range(LATENT // BLOCK):
        rows = slice(part * BLOCK, (part + 1) * BLOCK)
        linear = jnp.dot(w_in[rows, :], smooth, preferred_element_type=jnp.float32)
        inner = linear * (GELU_A + GELU_B * (linear * linear))
        hidden = (linear + linear * jnp.tanh(inner)).astype(jnp.bfloat16)
        change = jnp.dot(w_out[:, rows], hidden, preferred_element_type=jnp.float32)
        total = change if total is None else total + change
    return total


def first_kernel(role_ref, x_ref, halo_ref, diff_ref, w_in_ref, w_out_ref, out_ref, turn, state):
    role = role_ref[0]
    turn[...] = jnp.ones_like(turn)

    def take(block, rows, place):
        block = block.astype(jnp.float32)
        for tile in range(TILES):
            lanes = slice(tile * LANES, (tile + 1) * LANES)
            turn[tile, 0 : FIELDS * rows, :] = block[:, :, lanes].reshape(FIELDS * rows, LANES)
        for a in range(rows):
            for tile in range(TILES):
                state[place + a, :, tile * LANES : (tile + 1) * LANES] = turn[
                    tile, pl.ds(a, PADDED, stride=rows), :
                ]

    state[0:8] = jnp.zeros((8, PADDED, LON), jnp.float32)
    state[72:80] = jnp.zeros((8, PADDED, LON), jnp.float32)
    take(halo_ref[...], 8, jnp.where(role == 0, 72, 0))
    turn[...] = jnp.ones_like(turn)

    def load(step, carry):
        rows = pl.ds(pl.multiple_of(step * 16, 16), 16)
        take(x_ref[:, rows, :], 16, 8 + step * 16)
        return carry

    lax.fori_loop(0, ROWS // 16, load, 0)
    diff = diff_ref[...]
    w_in = w_in_ref[...]
    w_out = w_out_ref[...]

    def pair(step, carry):
        smooth = []
        centre = []
        for k in range(2):
            row = step * 2 + k + 7
            c = state[row]
            around = state[row - 1] + state[row + 1] + pltpu.roll(c, 1, 1) + pltpu.roll(c, LON - 1, 1)
            smooth.append((c + diff * (around - 4.0 * c)).astype(jnp.bfloat16))
            centre.append(c)
        smooth = jnp.concatenate(smooth, axis=1)
        centre = jnp.concatenate(centre, axis=1)
        new = []
        for n in range(2 * LON // BLOCK):
            cols = slice(n * BLOCK, (n + 1) * BLOCK)
            new.append(centre[:, cols] + mlp(smooth[:, cols], w_in, w_out))
        new = jnp.concatenate(new, axis=1).astype(jnp.bfloat16)
        out_ref[step * 2] = new[:, :LON]
        out_ref[step * 2 + 1] = new[:, LON:]
        return carry

    lax.fori_loop(0, (ROWS + 2) // 2, pair, 0)

    @pl.when(role == 0)
    def _():
        out_ref[0] = jnp.zeros((PADDED, LON), jnp.bfloat16)

    @pl.when(role == 1)
    def _():
        out_ref[ROWS + 1] = jnp.zeros((PADDED, LON), jnp.bfloat16)


def swap_groups(rows):
    lane = lax.broadcasted_iota(jnp.int32, rows[0].shape, 1)
    for bit in (4, 2, 1):
        shift = bit * GROUP
        high = (lane & shift) != 0
        new = list(rows)
        for a in range(8):
            if a & bit:
                continue
            first, second = rows[a], rows[a + bit]
            new[a] = jnp.where(high, pltpu.roll(second, shift, 1), first)
            new[a + bit] = jnp.where(high, second, pltpu.roll(first, LANES - shift, 1))
        rows = new
    return rows


def second_kernel(tiles, state_ref, diff_ref, w_in_ref, w_out_ref, out_ref):
    diff = diff_ref[...][:, :LANES]
    w_in = w_in_ref[...]
    w_out = w_out_ref[...]
    lane = lax.broadcasted_iota(jnp.int32, (PADDED, LANES), 1)
    first_lane = lane == 0
    last_lane = lane == LANES - 1

    def piece(row, tile):
        return state_ref[row, :, tile * LANES : (tile + 1) * LANES].astype(jnp.float32)

    def block(r, carry):
        pieces = []
        for a in range(8):
            row = r * 8 + a + 1
            for tile in tiles:
                c = piece(row, tile)
                before = piece(row, (tile - 1) % TILES)
                after = piece(row, (tile + 1) % TILES)
                left = pltpu.roll(jnp.where(last_lane, before, c), 1, 1)
                right = pltpu.roll(jnp.where(first_lane, after, c), LANES - 1, 1)
                around = piece(row - 1, tile) + piece(row + 1, tile) + left + right
                pieces.append((c, (c + diff * (around - 4.0 * c)).astype(jnp.bfloat16)))
        new = []
        for first, second in zip(pieces[0::2], pieces[1::2]):
            change = mlp(jnp.concatenate([first[1], second[1]], axis=1), w_in, w_out)
            new.append(first[0] + change[:, :LANES])
            new.append(second[0] + change[:, LANES:])
        for k in range(len(tiles)):
            for t, message in enumerate(swap_groups(new[k :: len(tiles)])):
                out_ref[r * 8 + t, k] = message.astype(jnp.bfloat16)
        return carry

    lax.fori_loop(0, ROWS // 8, block, 0)


def split(a):
    high = a.astype(jnp.bfloat16)
    return high, (a - high.astype(jnp.float32)).astype(jnp.bfloat16)


def dot3(a, b, contract=((1,), (0,))):
    (a_high, a_low), (b_high, b_low) = split(a), split(b)

    left = jnp.concatenate([a_high, a_low, a_high], axis=1)
    right = jnp.concatenate([b_high, b_high, b_low], axis=contract[1][0])
    return lax.dot_general(left, right, (contract, ((), ())), preferred_element_type=jnp.float32)


def weights_of(observed, value, weight):
    eye = jnp.where(
        lax.broadcasted_iota(jnp.int32, (MEMBERS, MEMBERS), 0)
        == lax.broadcasted_iota(jnp.int32, (MEMBERS, MEMBERS), 1),
        1.0,
        0.0,
    )
    obs_mean = jnp.sum(observed, axis=0, keepdims=True) * (1.0 / MEMBERS)
    spread = observed - obs_mean
    innovation = value - obs_mean
    weighted = spread * weight
    precision = (MEMBERS - 1.0) * eye + dot3(weighted, spread, ((1,), (1,)))
    pulled = jnp.sum(weighted * innovation, axis=1, keepdims=True)
    pulled = jnp.broadcast_to(pulled, (MEMBERS, MEMBERS))
    trace = jnp.sum(jnp.sum(precision * eye, axis=0, keepdims=True), axis=1, keepdims=True)
    scale = MEMBERS * trace
    return eye, precision / scale, pulled, scale


def mix_kernel(nt, last, *refs):
    if last:
        (idx_ref, value_ref, weight_ref, part_ref, g_ref, out_ref, picked, turn, back) = refs
    else:
        (idx_ref, value_ref, weight_ref, g_ref, out_ref, part_out, picked, turn, back) = refs
    f32, bf16 = jnp.float32, jnp.bfloat16

    gather_sum = jnp.where(
        lax.broadcasted_iota(jnp.int32, (MEMBERS, MEMBERS * 8), 1) >> 3
        == lax.broadcasted_iota(jnp.int32, (MEMBERS, MEMBERS * 8), 0),
        1.0,
        0.0,
    ).astype(bf16)
    patches = []
    for k in range(nt):
        idx = jnp.concatenate([idx_ref[2 * k : 2 * k + 1, :], idx_ref[2 * k + 1 : 2 * k + 2, :]], axis=1)
        odd = (lax.broadcasted_iota(jnp.int32, (1, 2 * OBS), 1) >= OBS).astype(jnp.int32)
        cell = idx & (CELLS - 1)
        lane = (cell >> 3) * GROUP + odd * EDGE + (cell & 7)
        field = idx >> 6
        hot = jnp.where(lax.broadcasted_iota(jnp.int32, (LANES, 2 * OBS), 0) == lane, 1.0, 0.0).astype(bf16)
        mask = lax.broadcasted_iota(jnp.int32, (PADDED, 2 * OBS), 0) == field

        def pick(step, carry):
            m = pl.multiple_of(step * 8, 8)
            block = g_ref[pl.ds(m, 8), k].astype(f32).reshape(8 * PADDED, LANES)
            turn[k, pl.ds(pl.multiple_of(step * 8 * PADDED, 8), 8 * PADDED), :] = block
            values = jnp.dot(block.astype(bf16), hot, preferred_element_type=f32)
            values = jnp.where(mask[None], values.reshape(8, PADDED, 2 * OBS), 0.0)
            values = jnp.sum(values.reshape(8, PADDED // 8, 8, 2 * OBS), axis=1)
            picked[pl.ds(pl.multiple_of(step * 64, 64), 64), :] = values.reshape(64, 2 * OBS)
            return carry

        lax.fori_loop(0, MEMBERS // 8, pick, 0)
        observed = jnp.dot(gather_sum, picked[...].astype(bf16), preferred_element_type=f32)
        for e in range(2):
            patches.append(
                weights_of(
                    observed[:, e * OBS : (e + 1) * OBS],
                    value_ref[2 * k + e : 2 * k + e + 1, :],
                    weight_ref[2 * k + e : 2 * k + e + 1, :],
                )
            )
    eye = patches[0][0]

    def newton(step, carry):
        new = []
        for iterate, root in carry:
            factor = 0.5 * (3.0 * eye - dot3(root, iterate))
            new.append((dot3(iterate, factor), dot3(factor, root)))
        return tuple(new)

    carry = tuple((iterate, eye) for _, iterate, _, _ in patches)
    carry = lax.fori_loop(0, NS_ITERS, newton, carry)
    mixes = []
    for (_, root), (_, _, pulled, scale) in zip(carry, patches):
        combined = jnp.sqrt((MEMBERS - 1.0) / scale) * root + dot3(root, dot3(root, pulled)) / scale
        rest = (1.0 - jnp.sum(combined, axis=0, keepdims=True)) * (1.0 / MEMBERS)
        mixes.append((combined + rest).T)
    even = (lax.broadcasted_iota(jnp.int32, (MEMBERS, LANES), 1) & EDGE) == 0
    partial = jnp.zeros((1, 1), f32)
    for k in range(nt):
        mix = jnp.concatenate(mixes[2 * k : 2 * k + 2], axis=0).astype(bf16)

        def apply(f):
            x = turn[k, pl.ds(f, MEMBERS, stride=PADDED), :].astype(bf16)
            both = jnp.dot(mix, x, preferred_element_type=f32)
            mixed = jnp.where(even, both[:MEMBERS], both[MEMBERS:])
            back[k, pl.ds(f, MEMBERS, stride=PADDED), :] = mixed
            return mixed

        for f in range(FIELDS):
            mixed = apply(f)
            if f == 0:
                part = jnp.sum(jnp.sum(mixed, axis=0, keepdims=True), axis=1, keepdims=True)
                partial = partial + part
    if last:
        partial = partial + part_ref[0:1, 0:1]
        high = partial.astype(bf16).astype(f32)
        middle = (partial - high).astype(bf16).astype(f32)
        low = partial - high - middle
    else:
        part_out[...] = jnp.broadcast_to(partial, (8, LANES))
    for k in range(nt):
        for row, extra in zip(range(FIELDS, PADDED), (high, middle, low) if last else (partial,) * 3):
            back[k, pl.ds(row, MEMBERS, stride=PADDED), :] = jnp.broadcast_to(extra, (MEMBERS, LANES))

        def give(step, carry):
            m = pl.multiple_of(step * 8, 8)
            block = back[k, pl.ds(pl.multiple_of(step * 8 * PADDED, 8), 8 * PADDED), :]
            out_ref[pl.ds(m, 8), k] = block.reshape(8, PADDED, LANES).astype(bf16)
            return carry

        lax.fori_loop(0, MEMBERS // 8, give, 0)


def last_kernel(offset_ref, *refs):
    sources, out_ref, turn = refs[:-2], refs[-2], refs[-1]
    offset = offset_ref[0]
    first = lax.broadcasted_iota(jnp.int32, (FIELDS, 1, LANES), 0) == 0
    add = jnp.where(first, offset, 0.0)
    places = [(ref, k) for ref in sources for k in range(ref.shape[1])]

    def block(step, carry):
        for tile, (ref, k) in enumerate(places):
            for half in range(2):
                rows = [ref[(step * 2 + half) * 8 + t, k].astype(jnp.float32) for t in range(8)]
                for a, row in enumerate(swap_groups(rows)):
                    turn[tile, pl.ds(half * 8 + a, PADDED, stride=16), :] = row
            values = turn[tile, 0 : FIELDS * 16, :].reshape(FIELDS, 16, LANES) + add
            place = pl.ds(pl.multiple_of(step * 16, 16), 16)
            out_ref[:, place, tile * LANES : (tile + 1) * LANES] = values.astype(jnp.bfloat16)
        return carry

    lax.fori_loop(0, ROWS // 16, block, 0)


def cost(flops, size, tanhs=0):
    return pl.CostEstimate(flops=flops, bytes_accessed=size, transcendentals=tanhs)


def forecast_first(role, x, halo, diff, w_in, w_out):
    cells = (ROWS + 2) * LON
    return pl.pallas_call(
        first_kernel,
        out_shape=jax.ShapeDtypeStruct((ROWS + 2, PADDED, LON), jnp.bfloat16),
        in_specs=[ANY_SMEM] + [ANY_VMEM] * 5,
        out_specs=ANY_VMEM,
        scratch_shapes=[
            pltpu.VMEM((TILES, PADDED * 16, LANES), jnp.float32),
            pltpu.VMEM((ROWS + 16, PADDED, LON), jnp.float32),
        ],
        compiler_params=params(),
        cost_estimate=cost(cells * LATENT * 256 * 4, 7 << 20, cells * LATENT),
        name="forecast_first",
    )(role, x, halo, diff, w_in, w_out)


def forecast_second(tiles, state, diff, w_in, w_out):
    cells = ROWS * LANES * len(tiles)
    return pl.pallas_call(
        lambda *refs: second_kernel(tiles, *refs),
        out_shape=jax.ShapeDtypeStruct((MEMBERS, len(tiles), PADDED, LANES), jnp.bfloat16),
        in_specs=[ANY_VMEM] * 4,
        out_specs=ANY_VMEM,
        compiler_params=params(),
        cost_estimate=cost(cells * LATENT * 256 * 4, 5 << 20, cells * LATENT),
        name="forecast_second",
    )(state, diff, w_in, w_out)


def mix(last, idx, value, weight, g, *part):
    nt = g.shape[1]
    message = jax.ShapeDtypeStruct(g.shape, jnp.bfloat16)
    sums = jax.ShapeDtypeStruct((8, LANES), jnp.float32)
    return pl.pallas_call(
        lambda *refs: mix_kernel(nt, last, *refs),
        out_shape=message if last else (message, sums),
        in_specs=[ANY_VMEM] * (4 + len(part)),
        out_specs=ANY_VMEM if last else (ANY_VMEM, ANY_VMEM),
        scratch_shapes=[
            pltpu.VMEM((MEMBERS * 8, 2 * OBS), jnp.float32),
            pltpu.VMEM((nt, MEMBERS * PADDED, LANES), jnp.float32),
            pltpu.VMEM((nt, MEMBERS * PADDED, LANES), jnp.float32),
        ],
        compiler_params=params(),
        cost_estimate=cost(8 << 30, 4 << 20),
        name="mix",
    )(idx, value, weight, *part, g)


def put_back(offset, *sources):
    return pl.pallas_call(
        last_kernel,
        out_shape=jax.ShapeDtypeStruct((FIELDS, ROWS, LON), jnp.bfloat16),
        in_specs=[ANY_SMEM] + [ANY_VMEM] * len(sources),
        out_specs=ANY_VMEM,
        scratch_shapes=[pltpu.VMEM((TILES, PADDED * 16, LANES), jnp.float32)],
        compiler_params=params(),
        cost_estimate=cost(1 << 20, 7 << 20),
        name="put_back",
    )(offset, *sources)


def exchange(messages):
    return lax.all_to_all(messages, "dev", split_axis=0, concat_axis=0, tiled=True)


def share_observations(obs_value, obs_weight):
    both = jnp.stack([obs_value.reshape(3, 2, OBS), obs_weight.reshape(3, 2, OBS)], axis=1)
    groups = [[8 * r + t for t in range(8)] for r in range(8)]
    sent = jnp.broadcast_to(both[None], (8, 3, 2, 2, OBS))
    got = lax.all_to_all(sent, "dev", 0, 0, axis_index_groups=groups, tiled=True)
    pairs = got.reshape(24, 2, 2, OBS)
    t = lax.axis_index("dev") % 8
    mine = jnp.stack([lax.dynamic_index_in_dim(pairs, 8 * j + t, 0, False) for j in range(TILES)])
    return mine[:, 0].reshape(6, OBS), mine[:, 1].reshape(6, OBS)


def body(
    initial_realizations, diffusivity, w_in, b_in, w_out, obs_index, obs_value, obs_weight, climate
):
    role = lax.axis_index("role")
    dev = lax.axis_index("dev")
    x = initial_realizations.reshape(FIELDS, ROWS, LON)
    edge = lax.dynamic_slice_in_dim(x, jnp.where(role == 0, ROWS - 8, 0), 8, 1)
    halo = lax.ppermute(edge, "role", [(0, 1), (1, 0)])
    b_high = lax.reduce_precision(b_in, 8, 7)
    b_middle = lax.reduce_precision(b_in - b_high, 8, 7)
    b_low = b_in - b_high - b_middle
    bias = jnp.stack([b_high, b_middle, b_low], axis=1).astype(jnp.bfloat16)
    w_first = jnp.concatenate([w_in, bias], axis=1)
    w_second = jnp.pad(w_out * jnp.bfloat16(0.5), ((0, PADDED - FIELDS), (0, 0)))
    diff = jnp.broadcast_to(jnp.pad(diffusivity, (0, PADDED - FIELDS))[:, None], (PADDED, LON))

    value, weight = share_observations(obs_value, obs_weight)
    rows = lax.dynamic_slice_in_dim(obs_index, (dev // 8) * 48, 48, 0).reshape(TILES, 8, 2, OBS)
    index = lax.dynamic_index_in_dim(rows, dev % 8, 1, False).reshape(6, OBS)

    state = forecast_first(role.reshape(1), x, halo, diff, w_first, w_second)
    sent_a = forecast_second((0, 1), state, diff, w_first, w_second)
    got_a = exchange(sent_a)
    sent_b = forecast_second((2,), state, diff, w_first, w_second)
    got_b = exchange(sent_b)
    mixed_a, part = mix(False, index[:4], value[:4], weight[:4], got_a)
    back_a = exchange(mixed_a)
    mixed_b = mix(True, index[4:], value[4:], weight[4:], got_b, part)
    back_b = exchange(mixed_b)
    total = jnp.sum(back_b[:, 0, FIELDS:, 0].astype(jnp.float32))
    total = lax.psum(total, "role")
    offset = climate - total / VALUES
    return put_back(offset, back_a, back_b)[None]


def solution(mesh):
    in_specs = (
        P("dev", None, "role", None),
        P(),
        P(),
        P(),
        P(),
        P("role", None),
        P(("role", "dev"), None),
        P(("role", "dev"), None),
        P(),
    )
    out_specs = P("dev", None, "role", None)
    return jax.shard_map(body, mesh=mesh, in_specs=in_specs, out_specs=out_specs, check_vma=False)
```

```python
import jax
import jax.numpy as jnp
from jax import lax
from jax.experimental import pallas as pl
from jax.experimental.pallas import tpu as pltpu
from jax.sharding import PartitionSpec as P

EDGE = 8
NS_ITERS = 12
CELLS = 64
LANES = 128
FIELDS = 69
PADDED = 72
LATENT = 512
LON = 384
TILES = 3
ROWS = 64
MEMBERS = 64
OBS = 128
PATCHES = 6
GROUP = 16
BLOCK = 256
DEPTH = 2
VMEM = 56 * 1024 * 1024
GELU_A = 0.7978845608028654
GELU_B = 0.044715 * 0.7978845608028654
VALUES = MEMBERS * 128 * LON

IN_VMEM = pl.BlockSpec(memory_space=pltpu.VMEM)
IN_SMEM = pl.BlockSpec(memory_space=pltpu.SMEM)


def params():
    return pltpu.CompilerParams(vmem_limit_bytes=VMEM)


def cost(flops, size, tanhs=0):
    return pl.CostEstimate(flops=flops, bytes_accessed=size, transcendentals=tanhs)


def gelu_twice(linear):
    inner = linear * (GELU_A + GELU_B * (linear * linear))
    return (linear + linear * jnp.tanh(inner)).astype(jnp.bfloat16)


def mlp(smooth, w_in, w_out):
    count = smooth.shape[1] // BLOCK
    linear, changes = {}, []
    for n in range(count + DEPTH):
        if n < count:
            cols = slice(n * BLOCK, (n + 1) * BLOCK)
            linear[n] = jnp.dot(w_in, smooth[:, cols], preferred_element_type=jnp.float32)
        if n >= DEPTH:
            hidden = gelu_twice(linear.pop(n - DEPTH))
            changes.append(jnp.dot(w_out, hidden, preferred_element_type=jnp.float32))
    return jnp.concatenate(changes, axis=1)


def swap_groups(rows):
    lane = lax.broadcasted_iota(jnp.int32, rows[0].shape, 1)
    for bit in (4, 2, 1):
        shift = bit * GROUP
        high = (lane & shift) != 0
        new = list(rows)
        for a in range(8):
            if a & bit:
                continue
            first, second = rows[a], rows[a + bit]
            new[a] = jnp.where(high, pltpu.roll(second, shift, 1), first)
            new[a + bit] = jnp.where(high, second, pltpu.roll(first, LANES - shift, 1))
        rows = new
    return rows


def owner_of(r, tile, group):
    number = tile * 8 + group
    return r * 8 + number // 3, number % 3


def forecast_kernel(
    role_ref, x_ref, halo_ref, diff_ref, w_in_ref, b_in_ref, w_out_ref, out_ref, before, after
):
    f32, bf16 = jnp.float32, jnp.bfloat16
    role = role_ref[0]

    def turned(block):
        ones = jnp.ones((PADDED - FIELDS,) + block.shape[1:], bf16)
        return jnp.swapaxes(jnp.concatenate([block, ones], axis=0), 0, 1)

    zeros = jnp.zeros((8, PADDED, LON), bf16)
    before[0:8] = zeros
    before[72:80] = zeros
    before[pl.ds(jnp.where(role == 0, 72, 0), 8)] = turned(halo_ref[...])

    def load(step, carry):
        place = pl.multiple_of(step * 16, 16)
        before[pl.ds(8 + place, 16)] = turned(x_ref[:, pl.ds(place, 16), :])
        return carry

    lax.fori_loop(0, ROWS // 16, load, 0)

    diff = jnp.concatenate([diff_ref[...], jnp.zeros((1, LANES - FIELDS), f32)], axis=1)
    diff = jnp.broadcast_to(diff, (LANES, LANES)).T[:PADDED]
    diff = jnp.concatenate([diff] * TILES, axis=1)
    bias = b_in_ref[...]
    high = bias.astype(bf16)
    middle = (bias - high.astype(f32)).astype(bf16)
    low = (bias - high.astype(f32) - middle.astype(f32)).astype(bf16)
    w_in = jnp.concatenate([w_in_ref[...], high, middle, low], axis=0).astype(f32)
    w_in = jnp.concatenate([w_in, jnp.zeros((LANES - PADDED, LATENT), f32)], axis=0).T[:, :PADDED].astype(bf16)
    w_out = jnp.concatenate(
        [w_out_ref[...] * bf16(0.5), jnp.zeros((PADDED - FIELDS, LATENT), bf16)], axis=0
    )

    def advance(ref, place, count):
        centre, smooth = [], []
        rows = [ref[place + k - 1].astype(f32) for k in range(count + 2)]
        for k in range(count):
            c = rows[k + 1]
            around = rows[k] + rows[k + 2] + pltpu.roll(c, 1, 1) + pltpu.roll(c, LON - 1, 1)
            smooth.append((c + diff * (around - 4.0 * c)).astype(bf16))
            centre.append(c)
        change = mlp(jnp.concatenate(smooth, axis=1), w_in, w_out)
        return [centre[k] + change[:, k * LON : (k + 1) * LON] for k in range(count)]

    def first(step, carry):
        for k, row in enumerate(advance(before, step * 6 + 7, 6)):
            after[step * 6 + k] = row.astype(bf16)
        return carry

    lax.fori_loop(0, (ROWS + 2) // 6, first, 0)

    @pl.when(role == 0)
    def _():
        after[0] = jnp.zeros((PADDED, LON), bf16)

    @pl.when(role == 1)
    def _():
        after[ROWS + 1] = jnp.zeros((PADDED, LON), bf16)

    def second(r, carry):
        rows = advance(after, r * 8 + 1, 8)
        for tile in range(TILES):
            pieces = [row[:, tile * LANES : (tile + 1) * LANES] for row in rows]
            for group, message in enumerate(swap_groups(pieces)):
                owner, slot = owner_of(r, tile, group)
                out_ref[owner, slot] = message.astype(bf16)
        return carry

    lax.fori_loop(0, ROWS // 8, second, 0)


def split(a):
    high = a.astype(jnp.bfloat16)
    return high, (a - high.astype(jnp.float32)).astype(jnp.bfloat16)


def dot3(a, b, contract=((1,), (0,))):
    (a_high, a_low), (b_high, b_low) = split(a), split(b)
    left = jnp.concatenate([a_high, a_low, a_high], axis=1)
    right = jnp.concatenate([b_high, b_high, b_low], axis=contract[1][0])
    return lax.dot_general(left, right, (contract, ((), ())), preferred_element_type=jnp.float32)


def mix_kernel(dev_ref, idx_ref, value_ref, weight_ref, g_ref, out_ref, turn, back):
    f32, bf16 = jnp.float32, jnp.bfloat16
    dev = dev_ref[0]
    eye = jnp.where(
        lax.broadcasted_iota(jnp.int32, (MEMBERS, MEMBERS), 0)
        == lax.broadcasted_iota(jnp.int32, (MEMBERS, MEMBERS), 1),
        1.0,
        0.0,
    )
    odd = jnp.where(lax.broadcasted_iota(jnp.int32, (1, 2 * OBS), 1) >= OBS, EDGE, 0)
    spreads, weights, innovations = [], [], []
    for k in range(TILES):

        def load(step, carry):
            m = pl.multiple_of(step * 16, 16)
            turn[k, :, pl.ds(m, 16), :] = jnp.swapaxes(g_ref[pl.ds(m, 16), k], 0, 1)
            return carry

        lax.fori_loop(0, MEMBERS // 16, load, 0)
        idx = jnp.concatenate(
            [idx_ref[pl.ds(dev * PATCHES + 2 * k + e, 1), :] for e in range(2)], axis=1
        )
        cell = idx & (CELLS - 1)
        lane = (cell >> 3) * GROUP + odd + (cell & 7)
        field = idx >> 6
        hot = jnp.where(lax.broadcasted_iota(jnp.int32, (LANES, 2 * OBS), 0) == lane, 1.0, 0.0)
        hot = hot.astype(bf16)

        def pick(step, total):
            block = turn[k, pl.ds(step * 8, 8)].reshape(8 * MEMBERS, LANES)
            values = jnp.dot(block, hot, preferred_element_type=f32)
            for f in range(8):
                here = field == step * 8 + f
                total = total + jnp.where(here, values[f * MEMBERS : (f + 1) * MEMBERS], 0.0)
            return total

        observed = lax.fori_loop(0, PADDED // 8, pick, jnp.zeros((MEMBERS, 2 * OBS), f32))
        for e in range(2):
            mine = observed[:, e * OBS : (e + 1) * OBS]
            obs_mean = jnp.sum(mine, axis=0, keepdims=True) * (1.0 / MEMBERS)
            row = slice(2 * k + e, 2 * k + e + 1)
            spreads.append(mine - obs_mean)
            innovations.append(value_ref[row, :] - obs_mean)
            weights.append(weight_ref[row, :])

    weighted = [s * w for s, w in zip(spreads, weights)]
    precisions = [dot3(w, s, ((1,), (1,))) + (MEMBERS - 1.0) * eye for w, s in zip(weighted, spreads)]
    pulled = [
        jnp.broadcast_to(jnp.sum(w * i, axis=1, keepdims=True), (MEMBERS, MEMBERS))
        for w, i in zip(weighted, innovations)
    ]
    scales = [
        MEMBERS * jnp.sum(jnp.sum(p * eye, axis=0, keepdims=True), axis=1, keepdims=True)
        for p in precisions
    ]
    iterates = [p / s for p, s in zip(precisions, scales)]

    def newton(step, carry):
        iterates, roots = carry
        factors = [0.5 * (3.0 * eye - dot3(r, i)) for r, i in zip(roots, iterates)]
        new_iterates = [dot3(i, f) for i, f in zip(iterates, factors)]
        return new_iterates, [dot3(f, r) for f, r in zip(factors, roots)]

    _, roots = lax.fori_loop(0, NS_ITERS, newton, (iterates, [eye] * PATCHES))
    shifts = [dot3(r, p) for r, p in zip(roots, pulled)]
    shifts = [dot3(r, p) for r, p in zip(roots, shifts)]
    mixes = []
    for root, shift, scale in zip(roots, shifts, scales):
        combined = jnp.sqrt((MEMBERS - 1.0) / scale) * root + shift / scale
        rest = (1.0 - jnp.sum(combined, axis=0, keepdims=True)) * (1.0 / MEMBERS)
        mixes.append((combined + rest).T)

    even = (lax.broadcasted_iota(jnp.int32, (MEMBERS, BLOCK), 1) & EDGE) == 0
    total = jnp.zeros((1, 1), f32)
    for k in range(TILES):
        mix = jnp.concatenate(mixes[2 * k : 2 * k + 2], axis=0).astype(bf16)

        def mixed(x):
            both = jnp.dot(mix, x, preferred_element_type=f32)
            return jnp.where(even[:, : x.shape[1]], both[:MEMBERS], both[MEMBERS:])

        def apply(step, carry):
            for pair in range(4):
                f = step * 8 + 2 * pair
                new = mixed(jnp.concatenate([turn[k, f], turn[k, f + 1]], axis=1)).astype(bf16)
                back[k, f] = new[:, :LANES]
                back[k, f + 1] = new[:, LANES:]
            return carry

        lax.fori_loop(0, PADDED // 8, apply, 0)
        first = mixed(turn[k, 0])
        total = total + jnp.sum(jnp.sum(first, axis=0, keepdims=True), axis=1, keepdims=True)

    high = total.astype(bf16)
    middle = (total - high.astype(f32)).astype(bf16)
    low = (total - high.astype(f32) - middle.astype(f32)).astype(bf16)
    for row, part in enumerate((high, middle, low)):
        back[TILES - 1, FIELDS + row] = jnp.broadcast_to(part, (MEMBERS, LANES))
    for k in range(TILES):

        def give(step, carry):
            m = pl.multiple_of(step * 16, 16)
            out_ref[pl.ds(m, 16), k] = jnp.swapaxes(back[k, :, pl.ds(m, 16), :], 0, 1)
            return carry

        lax.fori_loop(0, MEMBERS // 16, give, 0)


def last_kernel(offset_ref, back_ref, out_ref):
    offset = offset_ref[0]
    first = lax.broadcasted_iota(jnp.int32, (FIELDS, 1, LANES), 0) == 0
    add = jnp.where(first, offset, 0.0)

    def block(step, carry):
        for tile in range(TILES):
            rows = []
            for half in range(2):
                pieces = []
                for group in range(8):
                    owner, slot = owner_of(step * 2 + half, tile, group)
                    pieces.append(back_ref[owner, slot].astype(jnp.float32))
                rows += [row.astype(jnp.bfloat16) for row in swap_groups(pieces)]
            values = jnp.swapaxes(jnp.stack(rows), 0, 1)[:FIELDS].astype(jnp.float32) + add
            place = pl.ds(pl.multiple_of(step * 16, 16), 16)
            out_ref[:, place, tile * LANES : (tile + 1) * LANES] = values.astype(jnp.bfloat16)
        return carry

    lax.fori_loop(0, ROWS // 16, block, 0)


MESSAGES = jax.ShapeDtypeStruct((MEMBERS, TILES, PADDED, LANES), jnp.bfloat16)


def forecast(role, x, halo, diff, w_in, b_in, w_out):
    cells = 2 * ROWS * LON
    return pl.pallas_call(
        forecast_kernel,
        out_shape=MESSAGES,
        in_specs=[IN_SMEM] + [IN_VMEM] * 6,
        out_specs=IN_VMEM,
        scratch_shapes=[
            pltpu.VMEM((ROWS + 16, PADDED, LON), jnp.bfloat16),
            pltpu.VMEM((ROWS + 2, PADDED, LON), jnp.bfloat16),
        ],
        compiler_params=params(),
        cost_estimate=cost(cells * LATENT * 256 * 4, 7 << 20, cells * LATENT),
        name="forecast",
    )(role, x, halo, diff, w_in, b_in, w_out)


def mix(dev, idx, value, weight, g):
    return pl.pallas_call(
        mix_kernel,
        out_shape=MESSAGES,
        in_specs=[IN_SMEM] + [IN_VMEM] * 4,
        out_specs=IN_VMEM,
        scratch_shapes=[
            pltpu.VMEM((TILES, PADDED, MEMBERS, LANES), jnp.bfloat16),
            pltpu.VMEM((TILES, PADDED, MEMBERS, LANES), jnp.bfloat16),
        ],
        compiler_params=params(),
        cost_estimate=cost(8 << 30, 7 << 20),
        name="mix",
    )(dev, idx, value, weight, g)


def put_back(offset, back):
    return pl.pallas_call(
        last_kernel,
        out_shape=jax.ShapeDtypeStruct((FIELDS, ROWS, LON), jnp.bfloat16),
        in_specs=[IN_SMEM, IN_VMEM],
        out_specs=IN_VMEM,
        compiler_params=params(),
        cost_estimate=cost(1 << 20, 7 << 20),
        name="put_back",
    )(offset, back)


def exchange(messages):
    return lax.all_to_all(messages, "dev", split_axis=0, concat_axis=0, tiled=True)


def body(
    initial_realizations, diffusivity, w_in, b_in, w_out, obs_index, obs_value, obs_weight, climate
):
    role = lax.axis_index("role")
    dev = lax.axis_index("dev")
    x = initial_realizations.reshape(FIELDS, ROWS, LON)
    edge = lax.dynamic_slice_in_dim(x, jnp.where(role == 0, ROWS - 8, 0), 8, 1)
    halo = lax.ppermute(edge, "role", [(0, 1), (1, 0)])
    sent = forecast(
        role.reshape(1), x, halo, diffusivity.reshape(1, FIELDS), w_in.T, b_in.reshape(1, LATENT), w_out
    )
    got = exchange(sent)
    mixed = mix(dev.reshape(1), obs_index, obs_value, obs_weight, got)
    back = exchange(mixed)
    total = jnp.sum(back[:, TILES - 1, FIELDS:, 0].astype(jnp.float32))
    total = lax.psum(total, "role")
    offset = climate - total / VALUES
    return put_back(offset, back)[None]


def solution(mesh):
    in_specs = (
        P("dev", None, "role", None),
        P(),
        P(),
        P(),
        P(),
        P("role", None),
        P(("role", "dev"), None),
        P(("role", "dev"), None),
        P(),
    )
    out_specs = P("dev", None, "role", None)
    return jax.shard_map(body, mesh=mesh, in_specs=in_specs, out_specs=out_specs, check_vma=False)
```

```python
import jax
import jax.numpy as jnp
from jax import lax
from jax.experimental import pallas as pl
from jax.experimental.pallas import tpu as pltpu
from jax.sharding import PartitionSpec as P

EDGE = 8
NS_ITERS = 12
CELLS = 64
LANES = 128
FIELDS = 69
PADDED = 72
LATENT = 512
LON = 384
TILES = 3
ROWS = 64
MEMBERS = 64
OBS = 128
PATCHES = 6
GROUP = 16
BLOCK = 256
DEPTH = 3
GELU_A = 0.7978845608028654
GELU_B = 0.044715 * 0.7978845608028654
VALUES = MEMBERS * 128 * LON

IN_VMEM = pl.BlockSpec(memory_space=pltpu.VMEM)
IN_HBM = pl.BlockSpec(memory_space=pltpu.HBM)
IN_SMEM = pl.BlockSpec(memory_space=pltpu.SMEM)


def params(mib):
    return pltpu.CompilerParams(vmem_limit_bytes=mib * 1024 * 1024)


def cost(flops, size, tanhs=0):
    return pl.CostEstimate(flops=flops, bytes_accessed=size, transcendentals=tanhs)


def gelu_twice(linear):
    linear = linear.astype(jnp.bfloat16)
    inner = linear * (jnp.bfloat16(GELU_A) + jnp.bfloat16(GELU_B) * (linear * linear))
    return linear + linear * jnp.tanh(inner)


def mlp(smooth, w_in, w_out):
    count = smooth.shape[1] // BLOCK
    linear, changes = {}, []
    for n in range(count + DEPTH):
        if n < count:
            cols = slice(n * BLOCK, (n + 1) * BLOCK)
            linear[n] = jnp.dot(w_in, smooth[:, cols], preferred_element_type=jnp.float32)
        if n >= DEPTH:
            hidden = gelu_twice(linear.pop(n - DEPTH))
            changes.append(jnp.dot(w_out, hidden, preferred_element_type=jnp.float32))
    return jnp.concatenate(changes, axis=1)


def swap_groups(rows):
    lane = lax.broadcasted_iota(jnp.int32, rows[0].shape, 1)
    rows = [pltpu.roll(row, a * GROUP, 1) if a else row for a, row in enumerate(rows)]
    rows = [rows[-p % 8] for p in range(8)]
    for bit in (1, 2, 4):
        move = (lane & (bit * GROUP)) != 0
        rows = [jnp.where(move, rows[(p - bit) % 8], rows[p]) for p in range(8)]
    return [pltpu.roll(row, LANES - p * GROUP, 1) if p else row for p, row in enumerate(rows)]


def owner_of(r, tile, group):
    number = tile * 8 + group
    return r * 8 + number // 3, number % 3


def forecast_kernel(
    role_ref, x_ref, halo_ref, diff_ref, w_in_ref, b_in_ref, w_out_ref, out_ref, own, before, after, messages,
    in_sems, out_sems,
):
    f32, bf16 = jnp.float32, jnp.bfloat16
    role = role_ref[0]

    def fetch(step):
        rows = pl.ds(step * 16, 16)
        return pltpu.make_async_copy(x_ref.at[:, rows, :], own.at[:, rows, :], in_sems.at[step])

    def send(r):
        owners = pl.ds(r * 8, 8)
        return pltpu.make_async_copy(messages.at[owners], out_ref.at[owners], out_sems.at[r])

    for step in range(ROWS // 16):
        fetch(step).start()

    def turned(block):
        ones = jnp.ones((PADDED - FIELDS,) + block.shape[1:], bf16)
        return jnp.swapaxes(jnp.concatenate([block, ones], axis=0), 0, 1)

    zeros = jnp.zeros((8, PADDED, LON), bf16)
    before[0:8] = zeros
    before[72:80] = zeros
    before[pl.ds(jnp.where(role == 0, 72, 0), 8)] = turned(halo_ref[...])

    for step in range(ROWS // 16):
        fetch(step).wait()
        before[8 + step * 16 : 24 + step * 16] = turned(own[:, step * 16 : (step + 1) * 16, :])

    diff = jnp.concatenate([diff_ref[...], jnp.zeros((1, LANES - FIELDS), f32)], axis=1)
    diff = jnp.broadcast_to(diff, (LANES, LANES)).T[:PADDED]
    diff = jnp.concatenate([diff] * TILES, axis=1)
    bias = b_in_ref[...]
    high = bias.astype(bf16)
    middle = (bias - high.astype(f32)).astype(bf16)
    low = (bias - high.astype(f32) - middle.astype(f32)).astype(bf16)
    w_in = jnp.concatenate([w_in_ref[...], high, middle, low], axis=0).astype(f32)
    w_in = jnp.concatenate([w_in, jnp.zeros((LANES - PADDED, LATENT), f32)], axis=0).T[:, :PADDED].astype(bf16)
    w_out = jnp.concatenate(
        [w_out_ref[...] * bf16(0.5), jnp.zeros((PADDED - FIELDS, LATENT), bf16)], axis=0
    )

    def advance(ref, place, count):
        centre, smooth = [], []
        packed = [ref[place + k - 1] for k in range(count + 2)]
        rows = [row.astype(f32) for row in packed]
        for k in range(count):
            c = rows[k + 1]
            around = rows[k] + rows[k + 2] + pltpu.roll(packed[k + 1], 1, 1).astype(f32) + pltpu.roll(packed[k + 1], LON - 1, 1).astype(f32)
            smooth.append((c + diff * (around - 4.0 * c)).astype(bf16))
            centre.append(c)
        change = mlp(jnp.concatenate(smooth, axis=1), w_in, w_out)
        return [centre[k] + change[:, k * LON : (k + 1) * LON] for k in range(count)]

    def first(step, carry):
        for k, row in enumerate(advance(before, step * 6 + 7, 6)):
            after[step * 6 + k] = row.astype(bf16)
        return carry

    lax.fori_loop(0, (ROWS + 2) // 6, first, 0)

    @pl.when(role == 0)
    def _():
        after[0] = jnp.zeros((PADDED, LON), bf16)

    @pl.when(role == 1)
    def _():
        after[ROWS + 1] = jnp.zeros((PADDED, LON), bf16)

    def second(r, carry):
        rows = advance(after, r * 8 + 1, 8)
        for tile in range(TILES):
            pieces = [row[:, tile * LANES : (tile + 1) * LANES].astype(bf16) for row in rows]
            for group, message in enumerate(swap_groups(pieces)):
                owner, slot = owner_of(r, tile, group)
                messages[owner, slot] = message
        send(r).start()
        return carry

    lax.fori_loop(0, ROWS // 8, second, 0)
    for r in range(ROWS // 8):
        send(r).wait()


def split(a):
    high = a.astype(jnp.bfloat16)
    return high, (a - high.astype(jnp.float32)).astype(jnp.bfloat16)


def stacked(a):
    low = lax.broadcasted_iota(jnp.int32, (MEMBERS, LANES), 1) < MEMBERS
    high, rest = split(a)
    high_turned, rest_turned = pltpu.roll(high, MEMBERS, 1), pltpu.roll(rest, MEMBERS, 1)
    first = jnp.concatenate([jnp.where(low, high, rest_turned), high[:, :MEMBERS]], axis=1)
    second = jnp.concatenate([jnp.where(low, high_turned, rest), high_turned[:, :MEMBERS]], axis=1)
    return jnp.concatenate([first, second], axis=0)


def pair_dot(lefts, right):
    low = lax.broadcasted_iota(jnp.int32, (MEMBERS, LANES), 1) < MEMBERS
    high, rest = split(right)
    right = jnp.concatenate([high, high, rest], axis=0)
    left = jnp.concatenate([stacked(a) for a in lefts], axis=0)
    both = jnp.dot(left, right, preferred_element_type=jnp.float32)
    return [
        jnp.where(low, both[n * LANES : n * LANES + MEMBERS], both[n * LANES + MEMBERS : (n + 1) * LANES])
        for n in range(len(lefts))
    ]


def wide_dot(a, b):
    (a_high, a_low), (b_high, b_low) = split(a), split(b)
    left = jnp.concatenate([a_high, a_low, a_high], axis=1)
    right = jnp.concatenate([b_high, b_high, b_low], axis=1)
    return lax.dot_general(left, right, (((1,), (1,)), ((), ())), preferred_element_type=jnp.float32)


def mix_kernel(idx_ref, value_ref, weight_ref, g_ref, out_ref, turn, back, messages, sems):
    f32, bf16 = jnp.float32, jnp.bfloat16
    lane = lax.broadcasted_iota(jnp.int32, (MEMBERS, LANES), 1)
    low = lane < MEMBERS
    eye = jnp.where(
        (lane & (MEMBERS - 1)) == lax.broadcasted_iota(jnp.int32, (MEMBERS, LANES), 0), 1.0, 0.0
    )
    odd = jnp.where(lax.broadcasted_iota(jnp.int32, (1, 2 * OBS), 1) >= OBS, EDGE, 0)

    def halves(a):
        first = jnp.sum(jnp.where(low[: a.shape[0]], a, 0.0), axis=1, keepdims=True)
        second = jnp.sum(jnp.where(low[: a.shape[0]], 0.0, a), axis=1, keepdims=True)
        return jnp.where(low[: a.shape[0]], first, second)

    def send(k):
        return pltpu.make_async_copy(messages.at[:, k], out_ref.at[:, k], sems.at[k])

    precisions, pulled = [], []
    for k in range(TILES):

        def load(step, carry):
            m = pl.multiple_of(step * 16, 16)
            turn[k, :, pl.ds(m, 16), :] = jnp.swapaxes(g_ref[pl.ds(m, 16), k], 0, 1)
            return carry

        lax.fori_loop(0, MEMBERS // 16, load, 0, unroll=2)
    for k in range(TILES):
        idx = jnp.concatenate(
            [idx_ref[2 * k + e : 2 * k + e + 1, :] for e in range(2)], axis=1
        )
        cell = idx & (CELLS - 1)
        place = (cell >> 3) * GROUP + odd + (cell & 7)
        field = jnp.broadcast_to(idx >> 6, (MEMBERS, 2 * OBS))
        hot = jnp.where(lax.broadcasted_iota(jnp.int32, (LANES, 2 * OBS), 0) == place, 1.0, 0.0)
        hot = hot.astype(bf16)

        def pick(step, total):
            for part in range(3):
                start = step * 24 + part * 8
                block = turn[k, pl.ds(start, 8)].reshape(8 * MEMBERS, LANES)
                values = jnp.dot(block, hot, preferred_element_type=f32)
                for f in range(8):
                    here = field == start + f
                    total = jnp.where(here, values[f * MEMBERS : (f + 1) * MEMBERS], total)
            return total

        observed = lax.fori_loop(0, PADDED // 24, pick, jnp.zeros((MEMBERS, 2 * OBS), f32))
        sides, pulls = [], []
        for e in range(2):
            mine = observed[:, e * OBS : (e + 1) * OBS]
            row = slice(2 * k + e, 2 * k + e + 1)
            obs_mean = jnp.sum(mine, axis=0, keepdims=True) * (1.0 / MEMBERS)
            spread = mine - obs_mean
            weighted = spread * weight_ref[row, :]
            sides.append(wide_dot(weighted, spread))
            pulls.append(jnp.sum(weighted * (value_ref[row, :] - obs_mean), axis=1, keepdims=True))
        precisions.append(jnp.concatenate(sides, axis=1) + (MEMBERS - 1.0) * eye)
        pulled.append(jnp.where(low, pulls[0], pulls[1]))

    scales = [MEMBERS * halves(jnp.sum(p * eye, axis=0, keepdims=True)) for p in precisions]
    iterates = [p / s for p, s in zip(precisions, scales)]

    def newton(step, carry):
        iterates, roots = carry
        products = [pair_dot([r], i)[0] for r, i in zip(roots, iterates)]
        factors = [0.5 * (3.0 * eye - p) for p in products]
        new = [pair_dot([i, r], f) for i, r, f in zip(iterates, roots, factors)]
        return [n[0] for n in new], [n[1] for n in new]

    _, roots = lax.fori_loop(0, NS_ITERS, newton, (iterates, [eye] * TILES))
    shifts = [pair_dot([r], p)[0] for r, p in zip(roots, pulled)]
    shifts = [pair_dot([r], p)[0] for r, p in zip(roots, shifts)]
    even = jnp.where((lax.broadcasted_iota(jnp.int32, (MEMBERS, BLOCK), 1) & EDGE) == 0, 1.0, 0.0)
    even = even.astype(bf16)
    uneven = bf16(1.0) - even
    mixes = []
    for root, shift, scale in zip(roots, shifts, scales):
        combined = jnp.sqrt((MEMBERS - 1.0) / scale) * root + shift / scale
        rest = (1.0 - jnp.sum(combined, axis=0, keepdims=True)) * (1.0 / MEMBERS)
        across = (combined + rest).T
        mixes.append(jnp.concatenate([across[:MEMBERS], across[MEMBERS:]], axis=1).astype(bf16))

    def mixed(k, f):
        x = jnp.concatenate([turn[k, f], turn[k, f + 1]], axis=1)
        x = jnp.concatenate([x * even, x * uneven], axis=0)
        return jnp.dot(mixes[k], x, preferred_element_type=f32)

    total = jnp.zeros((1, 1), f32)
    for k in range(TILES):

        def apply(step, carry):
            for pair in range(12):
                f = step * 24 + 2 * pair
                new = mixed(k, f).astype(bf16)
                back[k, f] = new[:, :LANES]
                back[k, f + 1] = new[:, LANES:]
            return carry

        lax.fori_loop(0, PADDED // 24, apply, 0)
        first = mixed(k, 0)[:, :LANES]
        total = total + jnp.sum(jnp.sum(first, axis=0, keepdims=True), axis=1, keepdims=True)

    high = total.astype(bf16)
    middle = (total - high.astype(f32)).astype(bf16)
    low_part = (total - high.astype(f32) - middle.astype(f32)).astype(bf16)
    for row, part in enumerate((high, middle, low_part)):
        back[TILES - 1, FIELDS + row] = jnp.broadcast_to(part, (MEMBERS, LANES))
    for k in range(TILES):

        def give(step, carry):
            m = pl.multiple_of(step * 16, 16)
            messages[pl.ds(m, 16), k] = jnp.swapaxes(back[k, :, pl.ds(m, 16), :], 0, 1)
            return carry

        lax.fori_loop(0, MEMBERS // 16, give, 0, unroll=2)
        send(k).start()
    for k in range(TILES):
        send(k).wait()


def last_kernel(back_ref, out_ref, grid, sems):
    def send(step):
        rows = pl.ds(pl.multiple_of(step * 16, 16), 16)
        return pltpu.make_async_copy(grid.at[:, rows, :], out_ref.at[:, rows, :], sems.at[step])

    def block(step, carry):
        for tile in range(TILES):
            rows = []
            for half in range(2):
                pieces = []
                for group in range(8):
                    owner, slot = owner_of(step * 2 + half, tile, group)
                    pieces.append(back_ref[owner, slot])
                rows += swap_groups(pieces)
            values = jnp.swapaxes(jnp.stack(rows), 0, 1)[:FIELDS]
            place = pl.ds(pl.multiple_of(step * 16, 16), 16)
            grid[:, place, tile * LANES : (tile + 1) * LANES] = values
        send(step).start()
        return carry

    lax.fori_loop(0, ROWS // 16, block, 0)
    for step in range(ROWS // 16):
        send(step).wait()


MESSAGES = jax.ShapeDtypeStruct((MEMBERS, TILES, PADDED, LANES), jnp.bfloat16)


def forecast(role, x, halo, diff, w_in, b_in, w_out):
    cells = 2 * ROWS * LON
    return pl.pallas_call(
        forecast_kernel,
        out_shape=MESSAGES,
        in_specs=[IN_SMEM, IN_HBM] + [IN_VMEM] * 5,
        out_specs=IN_HBM,
        scratch_shapes=[
            pltpu.VMEM((FIELDS, ROWS, LON), jnp.bfloat16),
            pltpu.VMEM((ROWS + 16, PADDED, LON), jnp.bfloat16),
            pltpu.VMEM((ROWS + 2, PADDED, LON), jnp.bfloat16),
            pltpu.VMEM(MESSAGES.shape, jnp.bfloat16),
            pltpu.SemaphoreType.DMA((ROWS // 16,)),
            pltpu.SemaphoreType.DMA((ROWS // 8,)),
        ],
        compiler_params=params(56),
        cost_estimate=cost(cells * LATENT * 256 * 4, 7 << 20, cells * LATENT),
        name="forecast",
    )(role, x, halo, diff, w_in, b_in, w_out)


def mix(idx, value, weight, g):
    return pl.pallas_call(
        mix_kernel,
        out_shape=MESSAGES,
        in_specs=[IN_VMEM] * 4,
        out_specs=IN_HBM,
        scratch_shapes=[
            pltpu.VMEM((TILES, PADDED, MEMBERS, LANES), jnp.bfloat16),
            pltpu.VMEM((TILES, PADDED, MEMBERS, LANES), jnp.bfloat16),
            pltpu.VMEM(MESSAGES.shape, jnp.bfloat16),
            pltpu.SemaphoreType.DMA((TILES,)),
        ],
        compiler_params=params(53),
        cost_estimate=cost(8 << 30, 7 << 20),
        name="mix",
    )(idx, value, weight, g)


def put_back(back):
    return pl.pallas_call(
        last_kernel,
        out_shape=jax.ShapeDtypeStruct((FIELDS, ROWS, LON), jnp.bfloat16),
        in_specs=[IN_VMEM],
        out_specs=IN_HBM,
        scratch_shapes=[
            pltpu.VMEM((FIELDS, ROWS, LON), jnp.bfloat16),
            pltpu.SemaphoreType.DMA((ROWS // 16,)),
        ],
        compiler_params=params(50),
        cost_estimate=cost(1 << 20, 7 << 20),
        name="put_back",
    )(back)


def nudge_kernel(total_ref, other_ref, climate_ref, field_ref, out_ref):
    offset = climate_ref[0] - (total_ref[0] + other_ref[0]) / VALUES
    out_ref[...] = (field_ref[...].astype(jnp.float32) + offset).astype(jnp.bfloat16)


def nudge(total, other, climate, placed):
    field = pl.BlockSpec((1, ROWS, LON), lambda i: (0, 0, 0))
    return pl.pallas_call(
        nudge_kernel,
        out_shape=jax.ShapeDtypeStruct(placed.shape, placed.dtype),
        grid=(1,),
        in_specs=[IN_SMEM, IN_SMEM, IN_SMEM, field],
        out_specs=field,
        input_output_aliases={3: 0},
        cost_estimate=cost(1 << 16, 1 << 17),
        name="nudge",
    )(total, other, climate, placed)


def exchange(messages):
    return lax.all_to_all(messages, "dev", split_axis=0, concat_axis=0, tiled=True)


def body(
    initial_realizations, diffusivity, w_in, b_in, w_out, obs_index, obs_value, obs_weight, climate
):
    role = lax.axis_index("role")
    dev = lax.axis_index("dev")
    x = initial_realizations.reshape(FIELDS, ROWS, LON)
    edge = lax.dynamic_slice_in_dim(x, jnp.where(role == 0, ROWS - 8, 0), 8, 1)
    halo = lax.ppermute(edge, "role", [(0, 1), (1, 0)])
    sent = forecast(
        role.reshape(1), x, halo, diffusivity.reshape(1, FIELDS), w_in.T, b_in.reshape(1, LATENT), w_out
    )
    got = exchange(sent)
    index = lax.dynamic_slice_in_dim(obs_index, dev * PATCHES, PATCHES, 0)
    mixed = mix(index, obs_value, obs_weight, got)
    back = exchange(mixed)
    total = jnp.sum(back[:, TILES - 1, FIELDS:, 0].astype(jnp.float32)).reshape(1)
    other = lax.ppermute(total, "role", [(0, 1), (1, 0)])
    return nudge(total, other, climate, put_back(back))[None]


def solution(mesh):
    in_specs = (
        P("dev", None, "role", None),
        P(),
        P(),
        P(),
        P(),
        P("role", None),
        P(("role", "dev"), None),
        P(("role", "dev"), None),
        P(),
    )
    out_specs = P("dev", None, "role", None)
    return jax.shard_map(body, mesh=mesh, in_specs=in_specs, out_specs=out_specs, check_vma=False)
```

```python
import jax
import jax.numpy as jnp
from jax import lax
from jax.experimental import pallas as pl
from jax.experimental.pallas import tpu as pltpu
from jax.sharding import PartitionSpec as P

EDGE = 8
NS_ITERS = 12
CELLS = 64
LANES = 128
FIELDS = 69
PADDED = 72
LATENT = 512
LON = 384
TILES = 3
ROWS = 64
MEMBERS = 64
OBS = 128
PATCHES = 6
GROUP = 16
BLOCK = 256
DEPTH = 3
GELU_A = 0.7978845608028654
GELU_B = 0.044715 * 0.7978845608028654
VALUES = MEMBERS * 128 * LON

IN_VMEM = pl.BlockSpec(memory_space=pltpu.VMEM)
IN_HBM = pl.BlockSpec(memory_space=pltpu.HBM)
IN_SMEM = pl.BlockSpec(memory_space=pltpu.SMEM)


def params(mib):
    return pltpu.CompilerParams(vmem_limit_bytes=mib * 1024 * 1024)


def in_hbm(x):
    return pltpu.with_memory_space_constraint(x, pltpu.HBM)


def cost(flops, size, tanhs=0):
    return pl.CostEstimate(flops=flops, bytes_accessed=size, transcendentals=tanhs)


def gelu_twice(linear):
    linear = linear.astype(jnp.bfloat16)
    inner = linear * (jnp.bfloat16(GELU_A) + jnp.bfloat16(GELU_B) * (linear * linear))
    return linear * (jnp.bfloat16(1.0) + jnp.tanh(inner))


def mlp(smooth, w_in, w_out):
    count = smooth.shape[1] // BLOCK
    linear, changes = {}, []
    for n in range(count + DEPTH):
        if n < count:
            cols = slice(n * BLOCK, (n + 1) * BLOCK)
            linear[n] = jnp.dot(w_in, smooth[:, cols], preferred_element_type=jnp.float32)
        if n >= DEPTH:
            hidden = gelu_twice(linear.pop(n - DEPTH))
            changes.append(jnp.dot(w_out, hidden, preferred_element_type=jnp.float32))
    return jnp.concatenate(changes, axis=1)


def swap_groups(rows):
    lane = lax.broadcasted_iota(jnp.int32, rows[0].shape, 1)
    rows = [pltpu.roll(row, a * GROUP, 1) if a else row for a, row in enumerate(rows)]
    rows = [rows[-p % 8] for p in range(8)]
    for bit in (1, 2, 4):
        move = (lane & (bit * GROUP)) != 0
        rows = [jnp.where(move, rows[(p - bit) % 8], rows[p]) for p in range(8)]
    return [pltpu.roll(row, LANES - p * GROUP, 1) if p else row for p, row in enumerate(rows)]


def owner_of(r, tile, group):
    number = tile * 8 + group
    return r * 8 + number // 3, number % 3


def forecast_kernel(
    role_ref, climate_ref, x_ref, halo_ref, diff_ref, w_in_ref, b_in_ref, w_out_ref,
    out_ref, climate_out, own, before, after, in_sems,
):
    f32, bf16 = jnp.float32, jnp.bfloat16
    role = role_ref[0]

    def fetch(step):
        rows = pl.ds(step * 16, 16)
        return pltpu.make_async_copy(x_ref.at[:, rows, :], own.at[:, rows, :], in_sems.at[step])

    for step in range(ROWS // 16):
        fetch(step).start()
    climate_out[...] = jnp.full((1, LANES), climate_ref[0], f32)

    def turned(block):
        ones = jnp.ones((PADDED - FIELDS,) + block.shape[1:], bf16)
        return jnp.swapaxes(jnp.concatenate([block, ones], axis=0), 0, 1)

    zeros = jnp.zeros((8, PADDED, LON), bf16)
    before[0:8] = zeros
    before[72:80] = zeros
    before[pl.ds(jnp.where(role == 0, 72, 0), 8)] = turned(halo_ref[...])

    for step in range(ROWS // 16):
        fetch(step).wait()
        before[8 + step * 16 : 24 + step * 16] = turned(own[:, step * 16 : (step + 1) * 16, :])

    diff = jnp.concatenate([diff_ref[...], jnp.zeros((1, LANES - FIELDS), f32)], axis=1)
    diff = jnp.broadcast_to(diff, (LANES, LANES)).T[:PADDED]
    diff = jnp.concatenate([diff] * TILES, axis=1)
    bias = b_in_ref[...]
    high = bias.astype(bf16)
    middle = (bias - high.astype(f32)).astype(bf16)
    low = (bias - high.astype(f32) - middle.astype(f32)).astype(bf16)
    w_in = jnp.concatenate([w_in_ref[...], high, middle, low], axis=0).astype(f32)
    w_in = jnp.concatenate([w_in, jnp.zeros((LANES - PADDED, LATENT), f32)], axis=0).T[:, :PADDED].astype(bf16)
    w_out = jnp.concatenate(
        [w_out_ref[...] * bf16(0.5), jnp.zeros((PADDED - FIELDS, LATENT), bf16)], axis=0
    )

    def advance(ref, place, count):
        centre, smooth = [], []
        packed = [ref[place + k - 1] for k in range(count + 2)]
        rows = [row.astype(f32) for row in packed]
        for k in range(count):
            c = rows[k + 1]
            around = rows[k] + rows[k + 2] + pltpu.roll(packed[k + 1], 1, 1).astype(f32) + pltpu.roll(packed[k + 1], LON - 1, 1).astype(f32)
            smooth.append((c + diff * (around - 4.0 * c)).astype(bf16))
            centre.append(c)
        change = mlp(jnp.concatenate(smooth, axis=1), w_in, w_out)
        return [centre[k] + change[:, k * LON : (k + 1) * LON] for k in range(count)]

    def first(step, carry):
        for k, row in enumerate(advance(before, step * 6 + 7, 6)):
            after[step * 6 + k] = row.astype(bf16)
        return carry

    lax.fori_loop(0, (ROWS + 2) // 6, first, 0)

    @pl.when(role == 0)
    def _():
        after[0] = jnp.zeros((PADDED, LON), bf16)

    @pl.when(role == 1)
    def _():
        after[ROWS + 1] = jnp.zeros((PADDED, LON), bf16)

    def second(r, carry):
        rows = advance(after, r * 8 + 1, 8)
        for tile in range(TILES):
            pieces = [row[:, tile * LANES : (tile + 1) * LANES].astype(bf16) for row in rows]
            for group, message in enumerate(swap_groups(pieces)):
                owner, slot = owner_of(r, tile, group)
                out_ref[owner, slot] = message
        return carry

    lax.fori_loop(0, ROWS // 8, second, 0)


def split(a):
    high = a.astype(jnp.bfloat16)
    return high, (a - high.astype(jnp.float32)).astype(jnp.bfloat16)


def stacked(a):
    low = lax.broadcasted_iota(jnp.int32, (MEMBERS, LANES), 1) < MEMBERS
    high, rest = split(a)
    high_turned, rest_turned = pltpu.roll(high, MEMBERS, 1), pltpu.roll(rest, MEMBERS, 1)
    first = jnp.concatenate([jnp.where(low, high, rest_turned), high[:, :MEMBERS]], axis=1)
    second = jnp.concatenate([jnp.where(low, high_turned, rest), high_turned[:, :MEMBERS]], axis=1)
    return jnp.concatenate([first, second], axis=0)


def pair_dot(lefts, right):
    low = lax.broadcasted_iota(jnp.int32, (MEMBERS, LANES), 1) < MEMBERS
    high, rest = split(right)
    right = jnp.concatenate([high, high, rest], axis=0)
    left = jnp.concatenate([stacked(a) for a in lefts], axis=0)
    both = jnp.dot(left, right, preferred_element_type=jnp.float32)
    return [
        jnp.where(low, both[n * LANES : n * LANES + MEMBERS], both[n * LANES + MEMBERS : (n + 1) * LANES])
        for n in range(len(lefts))
    ]


def wide_dot(a, b):
    (a_high, a_low), (b_high, b_low) = split(a), split(b)
    left = jnp.concatenate([a_high, a_low, a_high], axis=1)
    right = jnp.concatenate([b_high, b_high, b_low], axis=1)
    return lax.dot_general(left, right, (((1,), (1,)), ((), ())), preferred_element_type=jnp.float32)


def weights_kernel(
    idx_ref, value_ref, weight_ref, g_ref, turn, mix_ref, total_ref
):
    f32, bf16 = jnp.float32, jnp.bfloat16
    lane = lax.broadcasted_iota(jnp.int32, (MEMBERS, LANES), 1)
    low = lane < MEMBERS
    eye = jnp.where(
        (lane & (MEMBERS - 1)) == lax.broadcasted_iota(jnp.int32, (MEMBERS, LANES), 0), 1.0, 0.0
    )
    odd = jnp.where(lax.broadcasted_iota(jnp.int32, (1, 2 * OBS), 1) >= OBS, EDGE, 0)

    def halves(a):
        first = jnp.sum(jnp.where(low[: a.shape[0]], a, 0.0), axis=1, keepdims=True)
        second = jnp.sum(jnp.where(low[: a.shape[0]], 0.0, a), axis=1, keepdims=True)
        return jnp.where(low[: a.shape[0]], first, second)

    precisions, pulled = [], []
    for k in range(TILES):

        def load(step, carry):
            m = pl.multiple_of(step * 16, 16)
            turn[k, :, pl.ds(m, 16), :] = jnp.swapaxes(g_ref[pl.ds(m, 16), k], 0, 1)
            return carry

        lax.fori_loop(0, MEMBERS // 16, load, 0, unroll=2)
    for k in range(TILES):
        idx = jnp.concatenate(
            [idx_ref[2 * k + e : 2 * k + e + 1, :] for e in range(2)], axis=1
        )
        cell = idx & (CELLS - 1)
        place = (cell >> 3) * GROUP + odd + (cell & 7)
        field = jnp.broadcast_to(idx >> 6, (MEMBERS, 2 * OBS))
        hot = jnp.where(lax.broadcasted_iota(jnp.int32, (LANES, 2 * OBS), 0) == place, 1.0, 0.0)
        hot = hot.astype(bf16)

        def pick(step, total):
            for part in range(3):
                start = step * 24 + part * 8
                block = turn[k, pl.ds(start, 8)].reshape(8 * MEMBERS, LANES)
                values = jnp.dot(block, hot, preferred_element_type=f32)
                for f in range(8):
                    here = field == start + f
                    total = jnp.where(here, values[f * MEMBERS : (f + 1) * MEMBERS], total)
            return total

        observed = lax.fori_loop(0, PADDED // 24, pick, jnp.zeros((MEMBERS, 2 * OBS), f32))
        sides, pulls = [], []
        for e in range(2):
            mine = observed[:, e * OBS : (e + 1) * OBS]
            row = slice(2 * k + e, 2 * k + e + 1)
            obs_mean = jnp.sum(mine, axis=0, keepdims=True) * (1.0 / MEMBERS)
            spread = mine - obs_mean
            weighted = spread * weight_ref[row, :]
            sides.append(wide_dot(weighted, spread))
            pulls.append(jnp.sum(weighted * (value_ref[row, :] - obs_mean), axis=1, keepdims=True))
        precisions.append(jnp.concatenate(sides, axis=1) + (MEMBERS - 1.0) * eye)
        pulled.append(jnp.where(low, pulls[0], pulls[1]))

    scales = [MEMBERS * halves(jnp.sum(p * eye, axis=0, keepdims=True)) for p in precisions]
    iterates = [p / s for p, s in zip(precisions, scales)]

    def newton(step, carry):
        iterates, roots = carry
        products = [pair_dot([r], i)[0] for r, i in zip(roots, iterates)]
        factors = [0.5 * (3.0 * eye - p) for p in products]
        new = [pair_dot([i, r], f) for i, r, f in zip(iterates, roots, factors)]
        return [n[0] for n in new], [n[1] for n in new]

    _, roots = lax.fori_loop(0, NS_ITERS, newton, (iterates, [eye] * TILES))
    shifts = [pair_dot([r], p)[0] for r, p in zip(roots, pulled)]
    shifts = [pair_dot([r], p)[0] for r, p in zip(roots, shifts)]
    total = jnp.zeros((1, LANES), f32)
    odd_cell = (lane & EDGE) != 0
    for k, (root, shift, scale) in enumerate(zip(roots, shifts, scales)):
        combined = jnp.sqrt((MEMBERS - 1.0) / scale) * root + shift / scale
        rest = (1.0 - jnp.sum(combined, axis=0, keepdims=True)) * (1.0 / MEMBERS)
        mix = combined + rest
        across = mix.T
        mix_ref[k] = jnp.concatenate([across[:MEMBERS], across[MEMBERS:]], axis=1).astype(bf16)
        shares = jnp.where(
            odd_cell,
            jnp.sum(jnp.where(low, 0.0, mix), axis=1, keepdims=True),
            jnp.sum(jnp.where(low, mix, 0.0), axis=1, keepdims=True),
        )
        total = total + jnp.sum(shares * turn[k, 0].astype(f32), axis=0, keepdims=True)
    total_ref[...] = jnp.sum(total, axis=1, keepdims=True)


def apply_kernel(climate_ref, total_ref, other_ref, mix_ref, turn, out_ref, back):
    f32, bf16 = jnp.float32, jnp.bfloat16
    even = jnp.where((lax.broadcasted_iota(jnp.int32, (MEMBERS, BLOCK), 1) & EDGE) == 0, 1.0, 0.0)
    even = even.astype(bf16)
    uneven = bf16(1.0) - even
    total = total_ref[...] + other_ref[...] - climate_ref[...] * (VALUES // MEMBERS)
    total = jnp.broadcast_to(total, (MEMBERS, LANES))
    high = total.astype(bf16)
    middle = (total - high.astype(f32)).astype(bf16)
    low = (total - high.astype(f32) - middle.astype(f32)).astype(bf16)
    for k in range(TILES):
        mix = mix_ref[k]

        def apply(step, carry):
            for pair in range(12):
                f = step * 24 + 2 * pair
                x = jnp.concatenate([turn[k, f], turn[k, f + 1]], axis=1)
                x = jnp.concatenate([x * even, x * uneven], axis=0)
                new = jnp.dot(mix, x, preferred_element_type=f32).astype(bf16)
                back[k, f] = new[:, :LANES]
                back[k, f + 1] = new[:, LANES:]
            return carry

        lax.fori_loop(0, PADDED // 24, apply, 0)
        if k == TILES - 1:
            for row, part in enumerate((high, middle, low)):
                back[k, FIELDS + row] = part

        def give(step, carry):
            m = pl.multiple_of(step * 16, 16)
            out_ref[pl.ds(m, 16), k] = jnp.swapaxes(back[k, :, pl.ds(m, 16), :], 0, 1)
            return carry

        lax.fori_loop(0, MEMBERS // 16, give, 0, unroll=2)


def last_kernel(back_ref, out_ref, grid, sems):
    f32, bf16 = jnp.float32, jnp.bfloat16

    def send(first, count):
        fields = pl.ds(first, count)
        return pltpu.make_async_copy(grid.at[fields], out_ref.at[fields], sems.at[first // 16])

    totals = jnp.zeros((8, LANES), f32)
    for owner in range(MEMBERS):
        totals = totals + back_ref[owner, TILES - 1, PADDED - 8 : PADDED, :].astype(f32)
    offset = jnp.sum(totals[8 - PADDED + FIELDS :], axis=0, keepdims=True) / -VALUES

    chunks = [(first, min(16, FIELDS - first)) for first in range(0, FIELDS, 16)]
    for first, count in chunks:
        taken = slice(first, min(first + 16, PADDED))

        def block(step, carry):
            for tile in range(TILES):
                rows = []
                for half in range(2):
                    pieces = []
                    for group in range(8):
                        owner, slot = owner_of(step * 2 + half, tile, group)
                        pieces.append(back_ref[owner, slot, taken, :])
                    rows += swap_groups(pieces)
                values = jnp.swapaxes(jnp.stack(rows), 0, 1)[:count]
                place = pl.ds(pl.multiple_of(step * 16, 16), 16)
                lanes = slice(tile * LANES, (tile + 1) * LANES)
                if first == 0:
                    grid[0:1, place, lanes] = (values[:1].astype(f32) + offset).astype(bf16)
                    grid[1:count, place, lanes] = values[1:]
                else:
                    grid[first : first + count, place, lanes] = values
            return carry

        lax.fori_loop(0, ROWS // 16, block, 0)
        send(first, count).start()
    for first, count in chunks:
        send(first, count).wait()


MESSAGES = jax.ShapeDtypeStruct((MEMBERS, TILES, PADDED, LANES), jnp.bfloat16)


def forecast(role, climate, x, halo, diff, w_in, b_in, w_out):
    cells = 2 * ROWS * LON
    return pl.pallas_call(
        forecast_kernel,
        out_shape=(MESSAGES, jax.ShapeDtypeStruct((1, LANES), jnp.float32)),
        in_specs=[IN_SMEM, IN_SMEM, IN_HBM] + [IN_VMEM] * 5,
        out_specs=(IN_VMEM, IN_VMEM),
        scratch_shapes=[
            pltpu.VMEM((FIELDS, ROWS, LON), jnp.bfloat16),
            pltpu.VMEM((ROWS + 16, PADDED, LON), jnp.bfloat16),
            pltpu.VMEM((ROWS + 2, PADDED, LON), jnp.bfloat16),
            pltpu.SemaphoreType.DMA((ROWS // 16,)),
        ],
        compiler_params=params(32),
        cost_estimate=cost(cells * LATENT * 256 * 4, 7 << 20, cells * LATENT),
        name="forecast",
    )(role, climate, in_hbm(x), halo, in_hbm(diff), in_hbm(w_in), in_hbm(b_in), in_hbm(w_out))


def weights(idx, value, weight, g):
    return pl.pallas_call(
        weights_kernel,
        out_shape=(
            jax.ShapeDtypeStruct((TILES, PADDED, MEMBERS, LANES), jnp.bfloat16),
            jax.ShapeDtypeStruct((TILES, MEMBERS, LANES), jnp.bfloat16),
            jax.ShapeDtypeStruct((1, 1), jnp.float32),
        ),
        in_specs=[IN_VMEM] * 4,
        out_specs=(IN_VMEM,) * 3,
        compiler_params=params(32),
        cost_estimate=cost(8 << 30, 7 << 20),
        name="weights",
    )(idx, value, weight, g)


def apply(climate, total, other, mixes, turn):
    return pl.pallas_call(
        apply_kernel,
        out_shape=MESSAGES,
        in_specs=[IN_VMEM] * 5,
        out_specs=IN_VMEM,
        scratch_shapes=[pltpu.VMEM((TILES, PADDED, MEMBERS, LANES), jnp.bfloat16)],
        compiler_params=params(32),
        cost_estimate=cost(8 << 30, 7 << 20),
        name="apply",
    )(climate, total, other, mixes, turn)


def put_back(back):
    return pl.pallas_call(
        last_kernel,
        out_shape=jax.ShapeDtypeStruct((FIELDS, ROWS, LON), jnp.bfloat16),
        in_specs=[IN_VMEM],
        out_specs=IN_HBM,
        scratch_shapes=[
            pltpu.VMEM((FIELDS, ROWS, LON), jnp.bfloat16),
            pltpu.SemaphoreType.DMA((PADDED // 16 + 1,)),
        ],
        compiler_params=params(50),
        cost_estimate=cost(1 << 20, 7 << 20),
        name="put_back",
    )(back)


def exchange(messages):
    return lax.all_to_all(messages, "dev", split_axis=0, concat_axis=0, tiled=True)


def body(
    initial_realizations, diffusivity, w_in, b_in, w_out, obs_index, obs_value, obs_weight, climate
):
    role = lax.axis_index("role")
    dev = lax.axis_index("dev")
    x = initial_realizations.reshape(FIELDS, ROWS, LON)
    index = lax.dynamic_slice_in_dim(obs_index, dev * PATCHES, PATCHES, 0)
    edge = lax.dynamic_slice_in_dim(x, jnp.where(role == 0, ROWS - 8, 0), 8, 1)
    halo = lax.ppermute(edge, "role", [(0, 1), (1, 0)])
    halo, index = lax.optimization_barrier((halo, index))
    sent, climate = forecast(
        role.reshape(1), climate, x, halo, diffusivity.reshape(1, FIELDS), w_in.T, b_in.reshape(1, LATENT), w_out
    )
    got = exchange(sent)
    turn, mixes, total = weights(index, obs_value, obs_weight, got)
    other = lax.ppermute(total, "role", [(0, 1), (1, 0)])
    back = exchange(apply(climate, total, other, mixes, turn))
    return put_back(back)[None]


def solution(mesh):
    in_specs = (
        P("dev", None, "role", None),
        P(),
        P(),
        P(),
        P(),
        P("role", None),
        P(("role", "dev"), None),
        P(("role", "dev"), None),
        P(),
    )
    out_specs = P("dev", None, "role", None)
    return jax.shard_map(body, mesh=mesh, in_specs=in_specs, out_specs=out_specs, check_vma=False)
```

```python
import jax
import jax.numpy as jnp
from jax import lax
from jax.experimental import pallas as pl
from jax.experimental.pallas import tpu as pltpu
from jax.sharding import PartitionSpec as P

EDGE = 8
NS_ITERS = 12
CELLS = 64
LANES = 128
FIELDS = 69
PADDED = 72
LATENT = 512
LON = 384
TILES = 3
ROWS = 64
MEMBERS = 64
OBS = 128
PATCHES = 6
MAIN = 64
REST = FIELDS - MAIN
TAIL = TILES * MAIN
MESSAGE = 208
GROUP = 16
BLOCK = 256
DEPTH = 3
GELU_A = 0.7978845608028654
GELU_B = 0.044715 * 0.7978845608028654
VALUES = MEMBERS * 128 * LON

IN_VMEM = pl.BlockSpec(memory_space=pltpu.VMEM)
IN_HBM = pl.BlockSpec(memory_space=pltpu.HBM)
IN_SMEM = pl.BlockSpec(memory_space=pltpu.SMEM)


def params(mib):
    return pltpu.CompilerParams(vmem_limit_bytes=mib * 1024 * 1024)


def in_hbm(x):
    return pltpu.with_memory_space_constraint(x, pltpu.HBM)


def cost(flops, size, tanhs=0):
    return pl.CostEstimate(flops=flops, bytes_accessed=size, transcendentals=tanhs)


def gelu_twice(linear):
    linear = linear.astype(jnp.bfloat16)
    inner = linear * (jnp.bfloat16(GELU_A) + jnp.bfloat16(GELU_B) * (linear * linear))
    return linear * (jnp.bfloat16(1.0) + jnp.tanh(inner))


def mlp(count, smooth_of, done, w_in, w_out):
    linear = {}
    for n in range(count + DEPTH):
        if n < count:
            linear[n] = jnp.dot(w_in, smooth_of(n), preferred_element_type=jnp.float32)
        if n >= DEPTH:
            hidden = gelu_twice(linear.pop(n - DEPTH))
            done(n - DEPTH, jnp.dot(w_out, hidden, preferred_element_type=jnp.float32))


def swap_groups(rows):
    lane = lax.broadcasted_iota(jnp.int32, rows[0].shape, 1)
    rows = [pltpu.roll(row, a * GROUP, 1) if a else row for a, row in enumerate(rows)]
    rows = [rows[-p % 8] for p in range(8)]
    for bit in (1, 2, 4):
        move = (lane & (bit * GROUP)) != 0
        rows = [jnp.where(move, rows[(p - bit) % 8], rows[p]) for p in range(8)]
    return [pltpu.roll(row, LANES - p * GROUP, 1) if p else row for p, row in enumerate(rows)]


def owner_of(r, tile, group):
    number = tile * 8 + group
    return r * 8 + number // 3, number % 3


def forecast_kernel(
    role_ref, climate_ref, x_ref, halo_ref, diff_ref, w_in_ref, b_in_ref, w_out_ref,
    out_ref, climate_out, own, before, after, rests, in_sems,
):
    f32, bf16 = jnp.float32, jnp.bfloat16
    role = role_ref[0]

    def fetch(step):
        rows = pl.ds(step * 16, 16)
        return pltpu.make_async_copy(x_ref.at[:, rows, :], own.at[:, rows, :], in_sems.at[step])

    for step in range(ROWS // 16):
        fetch(step).start()
    climate_out[...] = jnp.full((1, LANES), climate_ref[0], f32)

    def turned(block):
        ones = jnp.ones((PADDED - FIELDS,) + block.shape[1:], bf16)
        return jnp.swapaxes(jnp.concatenate([block, ones], axis=0), 0, 1)

    zeros = jnp.zeros((8, PADDED, LON), bf16)
    before[0:8] = zeros
    before[72:80] = zeros
    before[pl.ds(jnp.where(role == 0, 72, 0), 8)] = turned(halo_ref[...])

    def take(step):
        fetch(step).wait()
        place = pl.multiple_of(step * 16, 16)
        before[pl.ds(8 + place, 16)] = turned(own[:, pl.ds(place, 16), :])

    take(0)

    diff = jnp.concatenate([diff_ref[...], jnp.zeros((1, LANES - FIELDS), f32)], axis=1)
    diff = jnp.broadcast_to(diff, (LANES, LANES)).T[:PADDED]
    diff = jnp.concatenate([diff] * TILES, axis=1)
    bias = b_in_ref[...]
    high = bias.astype(bf16)
    middle = (bias - high.astype(f32)).astype(bf16)
    low = (bias - high.astype(f32) - middle.astype(f32)).astype(bf16)
    w_in = jnp.concatenate([w_in_ref[...], high, middle, low], axis=0).astype(f32)
    w_in = jnp.concatenate([w_in, jnp.zeros((LANES - PADDED, LATENT), f32)], axis=0).T[:, :PADDED].astype(bf16)
    w_out = jnp.concatenate(
        [w_out_ref[...] * bf16(0.5), jnp.zeros((PADDED - FIELDS, LATENT), bf16)], axis=0
    )

    def advance(ref, place, count, give):
        rows, smooth = {}, {}

        def row(k):
            if k not in rows:
                rows[k] = ref[place + k]
            return rows[k].astype(f32)

        def smooth_of(n):
            pieces = []
            for piece in (2 * n, 2 * n + 1):
                k, tile = divmod(piece, TILES)
                if k not in smooth:
                    c = row(k)
                    around = row(k - 1) + row(k + 1) + pltpu.roll(rows[k], 1, 1).astype(f32)
                    around = around + pltpu.roll(rows[k], LON - 1, 1).astype(f32)
                    smooth[k] = (c + diff * (around - 4.0 * c)).astype(bf16)
                pieces.append(smooth[k][:, tile * LANES : (tile + 1) * LANES])
            return jnp.concatenate(pieces, axis=1)

        def done(n, change):
            for half, piece in enumerate((2 * n, 2 * n + 1)):
                k, tile = divmod(piece, TILES)
                lanes = slice(tile * LANES, (tile + 1) * LANES)
                new = rows[k][:, lanes].astype(f32) + change[:, half * LANES : (half + 1) * LANES]
                give(k, tile, new.astype(bf16))

        mlp(count * TILES // 2, smooth_of, done, w_in, w_out)

    def first_rows(start, count):
        def give(k, tile, new):
            after[start + k, :, tile * LANES : (tile + 1) * LANES] = new

        advance(before, start + 7, count, give)

    def first(step, carry):
        first_rows(step * 16, 16)

        @pl.when(step < ROWS // 16 - 1)
        def _():
            take(step + 1)

        return carry

    lax.fori_loop(0, ROWS // 16, first, 0)
    first_rows(ROWS, 2)

    @pl.when(role == 0)
    def _():
        after[0] = jnp.zeros((PADDED, LON), bf16)

    @pl.when(role == 1)
    def _():
        after[ROWS + 1] = jnp.zeros((PADDED, LON), bf16)

    def second(step, carry):
        pieces = {}

        def give(k, tile, new):
            pieces[k, tile] = new
            if k % 8 == 7:
                rows = [pieces.pop((k - 7 + a, tile)) for a in range(8)]
                for group, message in enumerate(swap_groups(rows)):
                    owner, slot = owner_of(step * 2 + k // 8, tile, group)
                    out_ref[owner, slot * MAIN : (slot + 1) * MAIN, :] = message[:MAIN]
                    rests[owner, slot] = message[MAIN:]

        advance(after, step * 16 + 1, 16, give)
        for half in range(2):
            for u in range(8):
                owner = step * 16 + half * 8 + u
                parts = [rests[owner, slot].astype(f32)[:REST] for slot in range(TILES)]
                tail = jnp.concatenate(parts + [jnp.zeros((1, LANES), f32)], axis=0)
                out_ref[owner, TAIL:MESSAGE, :] = tail.astype(bf16)
        return carry

    lax.fori_loop(0, ROWS // 16, second, 0)


def split(a):
    high = a.astype(jnp.bfloat16)
    return high, (a - high.astype(jnp.float32)).astype(jnp.bfloat16)


def streamed(a):
    high, rest = split(a)
    return jnp.concatenate([high, rest, high], axis=1)


def held(a):
    low = lax.broadcasted_iota(jnp.int32, (MEMBERS, LANES), 1) < MEMBERS
    high, rest = split(jnp.concatenate([jnp.where(low, a, 0.0), jnp.where(low, 0.0, a)], axis=0))
    return jnp.concatenate([high, high, rest], axis=0)


def pair_dot(left, right):
    return jnp.dot(left, right, preferred_element_type=jnp.float32)


def wide_dot(a, b):
    (a_high, a_low), (b_high, b_low) = split(a), split(b)
    left = jnp.concatenate([a_high, a_low, a_high], axis=1)
    right = jnp.concatenate([b_high, b_high, b_low], axis=1)
    return lax.dot_general(left, right, (((1,), (1,)), ((), ())), preferred_element_type=jnp.float32)


def weights_kernel(
    idx_ref, value_ref, weight_ref, g_ref, turn, mix_ref, total_ref
):
    f32, bf16 = jnp.float32, jnp.bfloat16
    lane = lax.broadcasted_iota(jnp.int32, (MEMBERS, LANES), 1)
    low = lane < MEMBERS
    eye = jnp.where(
        (lane & (MEMBERS - 1)) == lax.broadcasted_iota(jnp.int32, (MEMBERS, LANES), 0), 1.0, 0.0
    )
    odd = jnp.where(lax.broadcasted_iota(jnp.int32, (1, 2 * OBS), 1) >= OBS, EDGE, 0)

    def halves(a):
        first = jnp.sum(jnp.where(low[: a.shape[0]], a, 0.0), axis=1, keepdims=True)
        second = jnp.sum(jnp.where(low[: a.shape[0]], 0.0, a), axis=1, keepdims=True)
        return jnp.where(low[: a.shape[0]], first, second)

    def load(step, carry):
        m = pl.multiple_of(step * 16, 16)
        turn[:, pl.ds(m, 16), :] = jnp.swapaxes(g_ref[pl.ds(m, 16)], 0, 1)
        return carry

    lax.fori_loop(0, MEMBERS // 16, load, 0, unroll=2)
    precisions, pulled = [], []
    for k in range(TILES):
        idx = jnp.concatenate(
            [idx_ref[2 * k + e : 2 * k + e + 1, :] for e in range(2)], axis=1
        )
        cell = idx & (CELLS - 1)
        place = (cell >> 3) * GROUP + odd + (cell & 7)
        field = jnp.broadcast_to(idx >> 6, (MEMBERS, 2 * OBS))
        hot = jnp.where(lax.broadcasted_iota(jnp.int32, (LANES, 2 * OBS), 0) == place, 1.0, 0.0)
        hot = hot.astype(bf16)

        def pick(total, start, first, count):
            block = turn[pl.ds(start, count)].reshape(count * MEMBERS, LANES)
            values = jnp.dot(block, hot, preferred_element_type=f32)
            for f in range(count):
                here = field == first + f
                total = jnp.where(here, values[f * MEMBERS : (f + 1) * MEMBERS], total)
            return total

        def picks(step, total):
            for part in range(4):
                first = step * 32 + part * 8
                total = pick(total, k * MAIN + first, first, 8)
            return total

        observed = pick(jnp.zeros((MEMBERS, 2 * OBS), f32), TAIL + k * REST, MAIN, REST)
        observed = lax.fori_loop(0, MAIN // 32, picks, observed)
        sides, pulls = [], []
        for e in range(2):
            mine = observed[:, e * OBS : (e + 1) * OBS]
            row = slice(2 * k + e, 2 * k + e + 1)
            obs_mean = jnp.sum(mine, axis=0, keepdims=True) * (1.0 / MEMBERS)
            spread = mine - obs_mean
            weighted = spread * weight_ref[row, :]
            sides.append(wide_dot(weighted, spread))
            pulls.append(jnp.sum(weighted * (value_ref[row, :] - obs_mean), axis=1, keepdims=True))
        precisions.append(jnp.concatenate(sides, axis=1) + (MEMBERS - 1.0) * eye)
        pulled.append(jnp.where(low, pulls[0], pulls[1]))

    scales = [MEMBERS * halves(jnp.sum(p * eye, axis=0, keepdims=True)) for p in precisions]
    iterates = [p / s for p, s in zip(precisions, scales)]

    def newton(step, carry):
        iterates, roots = carry
        rights = [held(i) for i in iterates]
        products = [pair_dot(streamed(r), i) for r, i in zip(roots, rights)]
        rights = [jnp.concatenate([i, held(r)], axis=1) for i, r in zip(rights, roots)]
        factors = [0.5 * (3.0 * eye - p) for p in products]
        new = [pair_dot(streamed(f), r) for f, r in zip(factors, rights)]
        return [n[:, :LANES] for n in new], [n[:, LANES:] for n in new]

    _, roots = lax.fori_loop(0, NS_ITERS, newton, (iterates, [eye] * TILES), unroll=2)
    shifts = [pair_dot(streamed(r), held(p)) for r, p in zip(roots, pulled)]
    shifts = [pair_dot(streamed(r), held(p)) for r, p in zip(roots, shifts)]
    total = jnp.zeros((1, LANES), f32)
    odd_cell = (lane & EDGE) != 0
    for k, (root, shift, scale) in enumerate(zip(roots, shifts, scales)):
        combined = jnp.sqrt((MEMBERS - 1.0) / scale) * root + shift / scale
        rest = (1.0 - jnp.sum(combined, axis=0, keepdims=True)) * (1.0 / MEMBERS)
        mix = combined + rest
        across = mix.T
        mix_ref[k] = jnp.concatenate([across[:MEMBERS], across[MEMBERS:]], axis=1).astype(bf16)
        shares = jnp.where(
            odd_cell,
            jnp.sum(jnp.where(low, 0.0, mix), axis=1, keepdims=True),
            jnp.sum(jnp.where(low, mix, 0.0), axis=1, keepdims=True),
        )
        total = total + jnp.sum(shares * turn[k * MAIN].astype(f32), axis=0, keepdims=True)
    total_ref[...] = jnp.sum(total, axis=1, keepdims=True)


def apply_kernel(climate_ref, total_ref, other_ref, mix_ref, turn, out_ref, back):
    f32, bf16 = jnp.float32, jnp.bfloat16
    even = jnp.where((lax.broadcasted_iota(jnp.int32, (MEMBERS, BLOCK), 1) & EDGE) == 0, 1.0, 0.0)
    even = even.astype(bf16)
    uneven = bf16(1.0) - even
    total = total_ref[...] + other_ref[...] - climate_ref[...] * (VALUES // MEMBERS)
    high = total.astype(bf16).astype(f32)
    middle = (total - high).astype(bf16).astype(f32)
    lane = lax.broadcasted_iota(jnp.int32, (1, LANES), 1)
    parts = jnp.where(lane == 0, high, jnp.where(lane == 1, middle, total - high - middle))
    parts = jnp.where(lane < 3, parts, 0.0)
    back[MESSAGE - 1] = jnp.broadcast_to(parts, (MEMBERS, LANES)).astype(bf16)

    def mixed(k, places):
        x = jnp.concatenate([turn[place] for place in places], axis=1)
        width = len(places) * LANES
        x = jnp.concatenate([x * even[:, :width], x * uneven[:, :width]], axis=0)
        new = jnp.dot(mix_ref[k], x, preferred_element_type=f32).astype(bf16)
        for n, place in enumerate(places):
            back[place] = new[:, n * LANES : (n + 1) * LANES]

    def main(k, step):
        for pair in range(8):
            place = k * MAIN + step * 16 + 2 * pair
            mixed(k, [place, place + 1])

    def give(first, count, step):
        members = pl.ds(pl.multiple_of(step * 16, 16), 16)
        block = jnp.swapaxes(back[first : first + count, members, :], 0, 1)
        out_ref[members, first : first + count, :] = block

    for k in range(TILES):
        for place in range(TAIL + k * REST, TAIL + (k + 1) * REST, 2):
            mixed(k, [p for p in (place, place + 1) if p < TAIL + (k + 1) * REST])

    for k in range(TILES + 1):

        def both(step, carry):
            if k < TILES:
                main(k, step)
            if k > 0:
                give((k - 1) * MAIN, MAIN, step)
            else:
                give(TAIL, MESSAGE - TAIL, step)
            return carry

        lax.fori_loop(0, 4, both, 0)


def last_kernel(back_ref, out_ref, grid, sems):
    f32, bf16 = jnp.float32, jnp.bfloat16

    def send(first, count):
        fields = pl.ds(first, count)
        return pltpu.make_async_copy(grid.at[fields], out_ref.at[fields], sems.at[first // 16])

    totals = jnp.zeros((MESSAGE - TAIL, LANES), f32)
    for owner in range(MEMBERS):
        totals = totals + back_ref[owner, TAIL:MESSAGE, :].astype(f32)
    offset = jnp.sum(totals[MESSAGE - TAIL - 1 :], axis=1, keepdims=True) / -VALUES

    def piece(owner, slot, first, count):
        if first < MAIN:
            return back_ref[owner, slot * MAIN + first : slot * MAIN + first + count, :]
        rest = back_ref[owner, TAIL:MESSAGE, :].astype(f32)
        return rest[slot * REST : (slot + 1) * REST].astype(bf16)

    chunks = [(first, min(16, FIELDS - first)) for first in range(0, FIELDS, 16)]
    for first, count in chunks:

        def block(step, carry):
            for tile in range(TILES):
                rows = []
                for half in range(2):
                    pieces = []
                    for group in range(8):
                        owner, slot = owner_of(step * 2 + half, tile, group)
                        pieces.append(piece(owner, slot, first, count))
                    rows += swap_groups(pieces)
                values = jnp.swapaxes(jnp.stack(rows), 0, 1)
                place = pl.ds(pl.multiple_of(step * 16, 16), 16)
                lanes = slice(tile * LANES, (tile + 1) * LANES)
                if first == 0:
                    grid[0:1, place, lanes] = (values[:1].astype(f32) + offset).astype(bf16)
                    grid[1:count, place, lanes] = values[1:]
                else:
                    grid[first : first + count, place, lanes] = values
            return carry

        lax.fori_loop(0, ROWS // 16, block, 0)
        send(first, count).start()
    for first, count in chunks:
        send(first, count).wait()


MESSAGES = jax.ShapeDtypeStruct((MEMBERS, MESSAGE, LANES), jnp.bfloat16)
TURNED = jax.ShapeDtypeStruct((MESSAGE, MEMBERS, LANES), jnp.bfloat16)


def forecast(role, climate, x, halo, diff, w_in, b_in, w_out):
    cells = 2 * ROWS * LON
    return pl.pallas_call(
        forecast_kernel,
        out_shape=(MESSAGES, jax.ShapeDtypeStruct((1, LANES), jnp.float32)),
        in_specs=[IN_SMEM, IN_SMEM, IN_HBM] + [IN_VMEM] * 5,
        out_specs=(IN_VMEM, IN_VMEM),
        scratch_shapes=[
            pltpu.VMEM((FIELDS, ROWS, LON), jnp.bfloat16),
            pltpu.VMEM((ROWS + 16, PADDED, LON), jnp.bfloat16),
            pltpu.VMEM((ROWS + 2, PADDED, LON), jnp.bfloat16),
            pltpu.VMEM((MEMBERS, TILES, PADDED - MAIN, LANES), jnp.bfloat16),
            pltpu.SemaphoreType.DMA((ROWS // 16,)),
        ],
        compiler_params=params(32),
        cost_estimate=cost(cells * LATENT * 256 * 4, 7 << 20, cells * LATENT),
        name="forecast",
    )(role, climate, in_hbm(x), halo, in_hbm(diff), in_hbm(w_in), in_hbm(b_in), in_hbm(w_out))


def weights(idx, value, weight, g):
    return pl.pallas_call(
        weights_kernel,
        out_shape=(
            TURNED,
            jax.ShapeDtypeStruct((TILES, MEMBERS, LANES), jnp.bfloat16),
            jax.ShapeDtypeStruct((1, 1), jnp.float32),
        ),
        in_specs=[IN_VMEM] * 4,
        out_specs=(IN_VMEM,) * 3,
        compiler_params=params(32),
        cost_estimate=cost(8 << 30, 7 << 20),
        name="weights",
    )(idx, value, weight, g)


def apply(climate, total, other, mixes, turn):
    return pl.pallas_call(
        apply_kernel,
        out_shape=MESSAGES,
        in_specs=[IN_VMEM] * 5,
        out_specs=IN_VMEM,
        scratch_shapes=[pltpu.VMEM(TURNED.shape, jnp.bfloat16)],
        compiler_params=params(32),
        cost_estimate=cost(8 << 30, 7 << 20),
        name="apply",
    )(climate, total, other, mixes, turn)


def put_back(back):
    return pl.pallas_call(
        last_kernel,
        out_shape=jax.ShapeDtypeStruct((FIELDS, ROWS, LON), jnp.bfloat16),
        in_specs=[IN_VMEM],
        out_specs=IN_HBM,
        scratch_shapes=[
            pltpu.VMEM((FIELDS, ROWS, LON), jnp.bfloat16),
            pltpu.SemaphoreType.DMA((PADDED // 16 + 1,)),
        ],
        compiler_params=params(50),
        cost_estimate=cost(1 << 20, 7 << 20),
        name="put_back",
    )(back)


def exchange(messages):
    return lax.all_to_all(messages, "dev", split_axis=0, concat_axis=0, tiled=True)


def body(
    initial_realizations, diffusivity, w_in, b_in, w_out, obs_index, obs_value, obs_weight, climate
):
    role = lax.axis_index("role")
    dev = lax.axis_index("dev")
    x = initial_realizations.reshape(FIELDS, ROWS, LON)
    index = lax.dynamic_slice_in_dim(obs_index, dev * PATCHES, PATCHES, 0)
    edge = lax.dynamic_slice_in_dim(x, jnp.where(role == 0, ROWS - 8, 0), 8, 1)
    halo = lax.ppermute(edge, "role", [(0, 1), (1, 0)])
    halo, index = lax.optimization_barrier((halo, index))
    sent, climate = forecast(
        role.reshape(1), climate, x, halo, diffusivity.reshape(1, FIELDS), w_in.T, b_in.reshape(1, LATENT), w_out
    )
    got = exchange(sent)
    turn, mixes, total = weights(index, obs_value, obs_weight, got)
    other = lax.ppermute(total, "role", [(0, 1), (1, 0)])
    back = exchange(apply(climate, total, other, mixes, turn))
    return put_back(back)[None]


def solution(mesh):
    in_specs = (
        P("dev", None, "role", None),
        P(),
        P(),
        P(),
        P(),
        P("role", None),
        P(("role", "dev"), None),
        P(("role", "dev"), None),
        P(),
    )
    out_specs = P("dev", None, "role", None)
    return jax.shard_map(body, mesh=mesh, in_specs=in_specs, out_specs=out_specs, check_vma=False)
```

```python
import jax
import jax.numpy as jnp
from jax import lax
from jax.experimental import pallas as pl
from jax.experimental.pallas import tpu as pltpu
from jax.sharding import PartitionSpec as P

EDGE = 8
NS_ITERS = 12
CELLS = 64
LANES = 128
FIELDS = 69
PADDED = 72
LATENT = 512
LON = 384
TILES = 3
ROWS = 64
MEMBERS = 64
OBS = 128
PATCHES = 6
MAIN = 64
REST = FIELDS - MAIN
TAIL = TILES * MAIN
MESSAGE = 208
GROUP = 16
BLOCK = 256
DEPTH = 3
GELU_A = 0.7978845608028654
GELU_B = 0.044715 * 0.7978845608028654
VALUES = MEMBERS * 128 * LON

IN_VMEM = pl.BlockSpec(memory_space=pltpu.VMEM)
IN_HBM = pl.BlockSpec(memory_space=pltpu.HBM)
IN_SMEM = pl.BlockSpec(memory_space=pltpu.SMEM)


def params(mib):
    return pltpu.CompilerParams(vmem_limit_bytes=mib * 1024 * 1024)


def in_hbm(x):
    return pltpu.with_memory_space_constraint(x, pltpu.HBM)


def cost(flops, size, tanhs=0):
    return pl.CostEstimate(flops=flops, bytes_accessed=size, transcendentals=tanhs)


def gelu_twice(linear):
    linear = linear.astype(jnp.bfloat16)
    inner = linear * (jnp.bfloat16(GELU_A) + jnp.bfloat16(GELU_B) * (linear * linear))
    return linear * (jnp.bfloat16(1.0) + jnp.tanh(inner))


def mlp(count, smooth_of, done, w_in, w_out):
    linear = {}
    for n in range(count + DEPTH):
        if n < count:
            linear[n] = jnp.dot(w_in, smooth_of(n), preferred_element_type=jnp.float32)
        if n >= DEPTH:
            hidden = gelu_twice(linear.pop(n - DEPTH))
            done(n - DEPTH, jnp.dot(w_out, hidden, preferred_element_type=jnp.float32))


def choose(rows):
    lane = lax.broadcasted_iota(jnp.int32, rows[0].shape, 1)
    rows = [rows[-p % 8] for p in range(8)]
    for bit in (1, 2, 4):
        move = (lane & (bit * GROUP)) != 0
        rows = [jnp.where(move, rows[(p - bit) % 8], rows[p]) for p in range(8)]
    return rows


def to_messages(rows):
    return choose([pltpu.roll(row, a * GROUP, 1) if a else row for a, row in enumerate(rows)])


def to_rows(messages):
    rows = choose(messages)
    return [pltpu.roll(row, LANES - a * GROUP, 1) if a else row for a, row in enumerate(rows)]


def owner_of(r, tile, group):
    number = tile * 8 + group
    return r * 8 + number // 3, number % 3


def forecast_kernel(
    role_ref, climate_ref, x_ref, halo_ref, diff_ref, w_in_ref, b_in_ref, w_out_ref,
    out_ref, climate_out, own, before, after, rests, in_sems,
):
    f32, bf16 = jnp.float32, jnp.bfloat16
    role = role_ref[0]

    def fetch(step):
        rows = pl.ds(step * 16, 16)
        return pltpu.make_async_copy(x_ref.at[:, rows, :], own.at[:, rows, :], in_sems.at[step])

    for step in range(ROWS // 16):
        fetch(step).start()
    climate_out[...] = jnp.full((1, LANES), climate_ref[0], f32)

    def turned(block):
        ones = jnp.ones((PADDED - FIELDS,) + block.shape[1:], bf16)
        return jnp.swapaxes(jnp.concatenate([block, ones], axis=0), 0, 1)

    zeros = jnp.zeros((8, PADDED, LON), bf16)
    before[0:8] = zeros
    before[72:80] = zeros
    before[pl.ds(jnp.where(role == 0, 72, 0), 8)] = turned(halo_ref[...])

    def take(step):
        fetch(step).wait()
        place = pl.multiple_of(step * 16, 16)
        before[pl.ds(8 + place, 16)] = turned(own[:, pl.ds(place, 16), :])

    take(0)

    diff = jnp.concatenate([diff_ref[...], jnp.zeros((1, LANES - FIELDS), f32)], axis=1)
    diff = jnp.broadcast_to(diff, (LANES, LANES)).T[:PADDED]
    diff = jnp.concatenate([diff] * TILES, axis=1)
    bias = b_in_ref[...]
    high = bias.astype(bf16)
    middle = (bias - high.astype(f32)).astype(bf16)
    low = (bias - high.astype(f32) - middle.astype(f32)).astype(bf16)
    w_in = jnp.concatenate([w_in_ref[...], high, middle, low], axis=0).astype(f32)
    w_in = jnp.concatenate([w_in, jnp.zeros((LANES - PADDED, LATENT), f32)], axis=0).T[:, :PADDED].astype(bf16)
    w_out = jnp.concatenate(
        [w_out_ref[...] * bf16(0.5), jnp.zeros((PADDED - FIELDS, LATENT), bf16)], axis=0
    )

    def advance(ref, place, count, give):
        rows, smooth = {}, {}

        def row(k):
            if k not in rows:
                rows[k] = ref[place + k]
            return rows[k].astype(f32)

        def smooth_of(n):
            pieces = []
            for piece in (2 * n, 2 * n + 1):
                k, tile = divmod(piece, TILES)
                if k not in smooth:
                    c = row(k)
                    around = row(k - 1) + row(k + 1) + pltpu.roll(rows[k], 1, 1).astype(f32)
                    around = around + pltpu.roll(rows[k], LON - 1, 1).astype(f32)
                    smooth[k] = (c + diff * (around - 4.0 * c)).astype(bf16)
                pieces.append(smooth[k][:, tile * LANES : (tile + 1) * LANES])
            return jnp.concatenate(pieces, axis=1)

        def done(n, change):
            for half, piece in enumerate((2 * n, 2 * n + 1)):
                k, tile = divmod(piece, TILES)
                lanes = slice(tile * LANES, (tile + 1) * LANES)
                new = rows[k][:, lanes].astype(f32) + change[:, half * LANES : (half + 1) * LANES]
                give(k, tile, new.astype(bf16))

        mlp(count * TILES // 2, smooth_of, done, w_in, w_out)

    def first_rows(start, count):
        def give(k, tile, new):
            after[start + k, :, tile * LANES : (tile + 1) * LANES] = new

        advance(before, start + 7, count, give)

    def first(step, carry):
        first_rows(step * 16, 16)

        @pl.when(step < ROWS // 16 - 1)
        def _():
            take(step + 1)

        return carry

    lax.fori_loop(0, ROWS // 16, first, 0)
    first_rows(ROWS, 2)

    @pl.when(role == 0)
    def _():
        after[0] = jnp.zeros((PADDED, LON), bf16)

    @pl.when(role == 1)
    def _():
        after[ROWS + 1] = jnp.zeros((PADDED, LON), bf16)

    def second(step, carry):
        pieces = {}

        def give(k, tile, new):
            pieces[k, tile] = new
            if k % 8 == 7:
                rows = [pieces.pop((k - 7 + a, tile)) for a in range(8)]
                for group, message in enumerate(to_messages(rows)):
                    owner, slot = owner_of(step * 2 + k // 8, tile, group)
                    out_ref[owner, slot * MAIN : (slot + 1) * MAIN, :] = message[:MAIN]
                    rests[owner, slot] = message[MAIN:]

        advance(after, step * 16 + 1, 16, give)
        for half in range(2):
            for u in range(8):
                owner = step * 16 + half * 8 + u
                parts = [rests[owner, slot].astype(f32)[:REST] for slot in range(TILES)]
                tail = jnp.concatenate(parts + [jnp.zeros((1, LANES), f32)], axis=0)
                out_ref[owner, TAIL:MESSAGE, :] = tail.astype(bf16)
        return carry

    lax.fori_loop(0, ROWS // 16, second, 0)


def split(a):
    high = a.astype(jnp.bfloat16)
    return high, (a - high.astype(jnp.float32)).astype(jnp.bfloat16)


def streamed(a):
    high, rest = split(a)
    return jnp.concatenate([high, rest, high], axis=1)


def held(a):
    low = lax.broadcasted_iota(jnp.int32, (MEMBERS, LANES), 1) < MEMBERS
    high, rest = split(jnp.concatenate([jnp.where(low, a, 0.0), jnp.where(low, 0.0, a)], axis=0))
    return jnp.concatenate([high, high, rest], axis=0)


def pair_dot(left, right):
    return jnp.dot(left, right, preferred_element_type=jnp.float32)


def wide_dot(a, b):
    (a_high, a_low), (b_high, b_low) = split(a), split(b)
    left = jnp.concatenate([a_high, a_low, a_high], axis=1)
    right = jnp.concatenate([b_high, b_high, b_low], axis=1)
    return lax.dot_general(left, right, (((1,), (1,)), ((), ())), preferred_element_type=jnp.float32)


def weights_kernel(
    idx_ref, value_ref, weight_ref, g_ref, turn, mix_ref, total_ref
):
    f32, bf16 = jnp.float32, jnp.bfloat16
    lane = lax.broadcasted_iota(jnp.int32, (MEMBERS, LANES), 1)
    low = lane < MEMBERS
    eye = jnp.where(
        (lane & (MEMBERS - 1)) == lax.broadcasted_iota(jnp.int32, (MEMBERS, LANES), 0), 1.0, 0.0
    )
    odd = jnp.where(lax.broadcasted_iota(jnp.int32, (1, 2 * OBS), 1) >= OBS, EDGE, 0)

    def halves(a):
        first = jnp.sum(jnp.where(low[: a.shape[0]], a, 0.0), axis=1, keepdims=True)
        second = jnp.sum(jnp.where(low[: a.shape[0]], 0.0, a), axis=1, keepdims=True)
        return jnp.where(low[: a.shape[0]], first, second)

    def load(step, carry):
        m = pl.multiple_of(step * 16, 16)
        turn[:, pl.ds(m, 16), :] = jnp.swapaxes(g_ref[pl.ds(m, 16)], 0, 1)
        return carry

    lax.fori_loop(0, MEMBERS // 16, load, 0, unroll=4)
    precisions, pulled = [], []
    for k in range(TILES):
        idx = jnp.concatenate(
            [idx_ref[2 * k + e : 2 * k + e + 1, :] for e in range(2)], axis=1
        )
        cell = idx & (CELLS - 1)
        place = (cell >> 3) * GROUP + odd + (cell & 7)
        field = jnp.broadcast_to(idx >> 6, (MEMBERS, 2 * OBS))
        hot = jnp.where(lax.broadcasted_iota(jnp.int32, (LANES, 2 * OBS), 0) == place, 1.0, 0.0)
        hot = hot.astype(bf16)

        def pick(total, start, first, count):
            block = turn[pl.ds(start, count)].reshape(count * MEMBERS, LANES)
            values = jnp.dot(block, hot, preferred_element_type=f32)
            for f in range(count):
                here = field == first + f
                total = jnp.where(here, values[f * MEMBERS : (f + 1) * MEMBERS], total)
            return total

        def picks(step, total):
            for part in range(4):
                first = step * 32 + part * 8
                total = pick(total, k * MAIN + first, first, 8)
            return total

        observed = pick(jnp.zeros((MEMBERS, 2 * OBS), f32), TAIL + k * REST, MAIN, REST)
        observed = lax.fori_loop(0, MAIN // 32, picks, observed, unroll=2)
        sides, pulls = [], []
        for e in range(2):
            mine = observed[:, e * OBS : (e + 1) * OBS]
            row = slice(2 * k + e, 2 * k + e + 1)
            obs_mean = jnp.sum(mine, axis=0, keepdims=True) * (1.0 / MEMBERS)
            spread = mine - obs_mean
            weighted = spread * weight_ref[row, :]
            sides.append(wide_dot(weighted, spread))
            pulls.append(jnp.sum(weighted * (value_ref[row, :] - obs_mean), axis=1, keepdims=True))
        precisions.append(jnp.concatenate(sides, axis=1) + (MEMBERS - 1.0) * eye)
        pulled.append(jnp.where(low, pulls[0], pulls[1]))

    scales = [MEMBERS * halves(jnp.sum(p * eye, axis=0, keepdims=True)) for p in precisions]
    iterates = [p / s for p, s in zip(precisions, scales)]

    def newton(step, carry):
        iterates, roots = carry
        rights = [held(i) for i in iterates]
        products = [pair_dot(streamed(r), i) for r, i in zip(roots, rights)]
        rights = [jnp.concatenate([i, held(r)], axis=1) for i, r in zip(rights, roots)]
        factors = [0.5 * (3.0 * eye - p) for p in products]
        new = [pair_dot(streamed(f), r) for f, r in zip(factors, rights)]
        return [n[:, :LANES] for n in new], [n[:, LANES:] for n in new]

    factors = [0.5 * (3.0 * eye - i) for i in iterates]
    iterates = [pair_dot(streamed(f), held(i)) for f, i in zip(factors, iterates)]
    _, roots = lax.fori_loop(1, NS_ITERS, newton, (iterates, factors), unroll=NS_ITERS - 1)
    shifts = [pair_dot(streamed(r), held(p)) for r, p in zip(roots, pulled)]
    shifts = [pair_dot(streamed(r), held(p)) for r, p in zip(roots, shifts)]
    total = jnp.zeros((1, LANES), f32)
    odd_cell = (lane & EDGE) != 0
    for k, (root, shift, scale) in enumerate(zip(roots, shifts, scales)):
        combined = jnp.sqrt((MEMBERS - 1.0) / scale) * root + shift / scale
        rest = (1.0 - jnp.sum(combined, axis=0, keepdims=True)) * (1.0 / MEMBERS)
        mix = combined + rest
        across = mix.T
        mix_ref[k] = jnp.concatenate([across[:MEMBERS], across[MEMBERS:]], axis=1).astype(bf16)
        shares = jnp.where(
            odd_cell,
            jnp.sum(jnp.where(low, 0.0, mix), axis=1, keepdims=True),
            jnp.sum(jnp.where(low, mix, 0.0), axis=1, keepdims=True),
        )
        total = total + jnp.sum(shares * turn[k * MAIN].astype(f32), axis=0, keepdims=True)
    total_ref[...] = jnp.sum(total, axis=1, keepdims=True)


def apply_kernel(mix_ref, turn, out_ref, back):
    f32, bf16 = jnp.float32, jnp.bfloat16
    even = jnp.where((lax.broadcasted_iota(jnp.int32, (MEMBERS, BLOCK), 1) & EDGE) == 0, 1.0, 0.0)
    even = even.astype(bf16)
    uneven = bf16(1.0) - even
    def mixed(k, places):
        x = jnp.concatenate([turn[place] for place in places], axis=1)
        width = len(places) * LANES
        x = jnp.concatenate([x * even[:, :width], x * uneven[:, :width]], axis=0)
        new = jnp.dot(mix_ref[k], x, preferred_element_type=f32).astype(bf16)
        for n, place in enumerate(places):
            back[place] = new[:, n * LANES : (n + 1) * LANES]

    def main(k, step):
        for pair in range(8):
            place = k * MAIN + step * 16 + 2 * pair
            mixed(k, [place, place + 1])

    def give(first, count, step):
        members = pl.ds(pl.multiple_of(step * 16, 16), 16)
        block = jnp.swapaxes(back[first : first + count, members, :], 0, 1)
        out_ref[members, first : first + count, :] = block

    for k in range(TILES):
        for place in range(TAIL + k * REST, TAIL + (k + 1) * REST, 2):
            mixed(k, [p for p in (place, place + 1) if p < TAIL + (k + 1) * REST])

    for k in range(TILES + 1):

        def both(step, carry):
            if k < TILES:
                main(k, step)
            if k > 0:
                give((k - 1) * MAIN, MAIN, step)
            else:
                give(TAIL, MESSAGE - TAIL, step)
            return carry

        lax.fori_loop(0, 4, both, 0, unroll=4)


def seal_kernel(climate_ref, total_ref, other_ref, messages_ref, out_ref):
    f32, bf16 = jnp.float32, jnp.bfloat16
    total = total_ref[...] + other_ref[...] - climate_ref[...] * (VALUES // MEMBERS)
    high = total.astype(bf16).astype(f32)
    middle = (total - high).astype(bf16).astype(f32)
    lane = lax.broadcasted_iota(jnp.int32, (16, LANES), 1)
    row = lax.broadcasted_iota(jnp.int32, (16, LANES), 0)
    parts = jnp.where(lane == 0, high, jnp.where(lane == 1, middle, total - high - middle))
    parts = jnp.where(lane < 3, parts, 0.0)
    for owner in range(MEMBERS):
        tail = messages_ref[owner, TAIL:MESSAGE, :].astype(f32)
        out_ref[owner, TAIL:MESSAGE, :] = jnp.where(row == 15, parts, tail).astype(bf16)


def last_kernel(back_ref, out_ref, grid, sems):
    f32, bf16 = jnp.float32, jnp.bfloat16

    def send(first, count):
        fields = pl.ds(first, count)
        return pltpu.make_async_copy(grid.at[fields], out_ref.at[fields], sems.at[first // 16])

    totals = jnp.zeros((MESSAGE - TAIL, LANES), f32)
    for owner in range(MEMBERS):
        totals = totals + back_ref[owner, TAIL:MESSAGE, :].astype(f32)
    offset = jnp.sum(totals[MESSAGE - TAIL - 1 :], axis=1, keepdims=True) / -VALUES

    def piece(owner, slot, first, count):
        if first < MAIN:
            return back_ref[owner, slot * MAIN + first : slot * MAIN + first + count, :]
        rest = back_ref[owner, TAIL:MESSAGE, :].astype(f32)
        return rest[slot * REST : (slot + 1) * REST].astype(bf16)

    chunks = [(first, min(16, FIELDS - first)) for first in range(0, FIELDS, 16)]
    for first, count in chunks:

        def block(step, carry):
            for tile in range(TILES):
                rows = []
                for half in range(2):
                    pieces = []
                    for group in range(8):
                        owner, slot = owner_of(step * 2 + half, tile, group)
                        pieces.append(piece(owner, slot, first, count))
                    rows += to_rows(pieces)
                values = jnp.swapaxes(jnp.stack(rows), 0, 1)
                place = pl.ds(pl.multiple_of(step * 16, 16), 16)
                lanes = slice(tile * LANES, (tile + 1) * LANES)
                if first == 0:
                    grid[0:1, place, lanes] = (values[:1].astype(f32) + offset).astype(bf16)
                    grid[1:count, place, lanes] = values[1:]
                else:
                    grid[first : first + count, place, lanes] = values
            return carry

        lax.fori_loop(0, ROWS // 16, block, 0, unroll=4)
        send(first, count).start()
    for first, count in chunks:
        send(first, count).wait()


MESSAGES = jax.ShapeDtypeStruct((MEMBERS, MESSAGE, LANES), jnp.bfloat16)
TURNED = jax.ShapeDtypeStruct((MESSAGE, MEMBERS, LANES), jnp.bfloat16)


def forecast(role, climate, x, halo, diff, w_in, b_in, w_out):
    cells = 2 * ROWS * LON
    return pl.pallas_call(
        forecast_kernel,
        out_shape=(MESSAGES, jax.ShapeDtypeStruct((1, LANES), jnp.float32)),
        in_specs=[IN_SMEM, IN_SMEM, IN_HBM] + [IN_VMEM] * 5,
        out_specs=(IN_VMEM, IN_VMEM),
        scratch_shapes=[
            pltpu.VMEM((FIELDS, ROWS, LON), jnp.bfloat16),
            pltpu.VMEM((ROWS + 16, PADDED, LON), jnp.bfloat16),
            pltpu.VMEM((ROWS + 2, PADDED, LON), jnp.bfloat16),
            pltpu.VMEM((MEMBERS, TILES, PADDED - MAIN, LANES), jnp.bfloat16),
            pltpu.SemaphoreType.DMA((ROWS // 16,)),
        ],
        compiler_params=params(32),
        cost_estimate=cost(cells * LATENT * 256 * 4, 7 << 20, cells * LATENT),
        name="forecast",
    )(role, climate, in_hbm(x), halo, in_hbm(diff), in_hbm(w_in), in_hbm(b_in), in_hbm(w_out))


def weights(idx, value, weight, g):
    return pl.pallas_call(
        weights_kernel,
        out_shape=(
            TURNED,
            jax.ShapeDtypeStruct((TILES, MEMBERS, LANES), jnp.bfloat16),
            jax.ShapeDtypeStruct((1, 1), jnp.float32),
        ),
        in_specs=[IN_VMEM] * 4,
        out_specs=(IN_VMEM,) * 3,
        compiler_params=params(32),
        cost_estimate=cost(8 << 30, 7 << 20),
        name="weights",
    )(idx, value, weight, g)


def apply(mixes, turn):
    return pl.pallas_call(
        apply_kernel,
        out_shape=MESSAGES,
        in_specs=[IN_VMEM] * 2,
        out_specs=IN_VMEM,
        scratch_shapes=[pltpu.VMEM(TURNED.shape, jnp.bfloat16)],
        compiler_params=params(32),
        cost_estimate=cost(8 << 30, 7 << 20),
        name="apply",
    )(mixes, turn)


def seal(climate, total, other, messages):
    return pl.pallas_call(
        seal_kernel,
        out_shape=MESSAGES,
        in_specs=[IN_VMEM] * 4,
        out_specs=IN_VMEM,
        input_output_aliases={3: 0},
        compiler_params=params(32),
        cost_estimate=cost(1 << 16, 1 << 18),
        name="seal",
    )(climate, total, other, messages)


def put_back(back):
    return pl.pallas_call(
        last_kernel,
        out_shape=jax.ShapeDtypeStruct((FIELDS, ROWS, LON), jnp.bfloat16),
        in_specs=[IN_VMEM],
        out_specs=IN_HBM,
        scratch_shapes=[
            pltpu.VMEM((FIELDS, ROWS, LON), jnp.bfloat16),
            pltpu.SemaphoreType.DMA((PADDED // 16 + 1,)),
        ],
        compiler_params=params(50),
        cost_estimate=cost(1 << 20, 7 << 20),
        name="put_back",
    )(back)


def exchange(messages):
    return lax.all_to_all(messages, "dev", split_axis=0, concat_axis=0, tiled=True)


def body(
    initial_realizations, diffusivity, w_in, b_in, w_out, obs_index, obs_value, obs_weight, climate
):
    role = lax.axis_index("role")
    dev = lax.axis_index("dev")
    x = initial_realizations.reshape(FIELDS, ROWS, LON)
    index = lax.dynamic_slice_in_dim(obs_index, dev * PATCHES, PATCHES, 0)
    group = dev % 8 * 3 + jnp.arange(PATCHES)[:, None] // 2
    index = (index & ~(CELLS - EDGE)) | ((index + group * EDGE) & (CELLS - EDGE))
    edge = lax.dynamic_slice_in_dim(x, jnp.where(role == 0, ROWS - 8, 0), 8, 1)
    halo = lax.ppermute(edge, "role", [(0, 1), (1, 0)])
    halo, index = lax.optimization_barrier((halo, index))
    sent, climate = forecast(
        role.reshape(1), climate, x, halo, diffusivity.reshape(1, FIELDS), w_in.T, b_in.reshape(1, LATENT), w_out
    )
    got = exchange(sent)
    turn, mixes, total = weights(index, obs_value, obs_weight, got)
    other = lax.ppermute(total, "role", [(0, 1), (1, 0)])
    back = exchange(seal(climate, total, other, apply(mixes, turn)))
    return put_back(back)[None]


def solution(mesh):
    in_specs = (
        P("dev", None, "role", None),
        P(),
        P(),
        P(),
        P(),
        P("role", None),
        P(("role", "dev"), None),
        P(("role", "dev"), None),
        P(),
    )
    out_specs = P("dev", None, "role", None)
    return jax.shard_map(body, mesh=mesh, in_specs=in_specs, out_specs=out_specs, check_vma=False)
```

```python
import jax
import jax.numpy as jnp
from jax import lax
from jax.experimental import pallas as pl
from jax.experimental.pallas import tpu as pltpu
from jax.sharding import PartitionSpec as P

EDGE = 8
NS_ITERS = 12
CELLS = 64
LANES = 128
FIELDS = 69
PADDED = 72
LATENT = 512
LON = 384
TILES = 3
ROWS = 64
MEMBERS = 64
OBS = 128
PATCHES = 6
MAIN = 64
REST = FIELDS - MAIN
TAIL = TILES * MAIN
MESSAGE = 208
GROUP = 16
BLOCK = 256
DEPTH = 3
GELU_A = 0.7978845608028654
GELU_B = 0.044715 * 0.7978845608028654
VALUES = MEMBERS * 128 * LON

IN_VMEM = pl.BlockSpec(memory_space=pltpu.VMEM)
IN_HBM = pl.BlockSpec(memory_space=pltpu.HBM)
IN_SMEM = pl.BlockSpec(memory_space=pltpu.SMEM)


def params(mib):
    return pltpu.CompilerParams(vmem_limit_bytes=mib * 1024 * 1024)


def in_hbm(x):
    return pltpu.with_memory_space_constraint(x, pltpu.HBM)


def cost(flops, size, tanhs=0):
    return pl.CostEstimate(flops=flops, bytes_accessed=size, transcendentals=tanhs)


def gelu_twice(linear):
    linear = linear.astype(jnp.bfloat16)
    inner = linear * (jnp.bfloat16(GELU_A) + jnp.bfloat16(GELU_B) * (linear * linear))
    return linear * (jnp.bfloat16(1.0) + jnp.tanh(inner))


def mlp(count, smooth_of, done, w_in, w_out):
    linear = {}
    for n in range(count + DEPTH):
        if n < count:
            linear[n] = jnp.dot(w_in, smooth_of(n), preferred_element_type=jnp.float32)
        if n >= DEPTH:
            hidden = gelu_twice(linear.pop(n - DEPTH))
            done(n - DEPTH, jnp.dot(w_out, hidden, preferred_element_type=jnp.float32))


def choose(rows):
    lane = lax.broadcasted_iota(jnp.int32, rows[0].shape, 1)
    rows = [rows[-p % 8] for p in range(8)]
    for bit in (1, 2, 4):
        move = (lane & (bit * GROUP)) != 0
        rows = [jnp.where(move, rows[(p - bit) % 8], rows[p]) for p in range(8)]
    return rows


def to_messages(rows):
    return choose([pltpu.roll(row, a * GROUP, 1) if a else row for a, row in enumerate(rows)])


def to_rows(messages):
    rows = choose(messages)
    return [pltpu.roll(row, LANES - a * GROUP, 1) if a else row for a, row in enumerate(rows)]


def owner_of(r, tile, group):
    number = tile * 8 + group
    return r * 8 + number // 3, number % 3


def forecast_kernel(
    role_ref, climate_ref, x_ref, halo_ref, diff_ref, w_in_ref, b_in_ref, w_out_ref,
    out_ref, climate_out, own, before, after, rests, in_sems, first_sems,
):
    f32, bf16 = jnp.float32, jnp.bfloat16
    role = role_ref[0]

    def fetch(step):
        rows = pl.ds(step * 16, 16)
        return pltpu.make_async_copy(x_ref.at[:, rows, :], own.at[:, rows, :], in_sems.at[step])

    def fetch_first(part):
        fields = pl.ds(part * (FIELDS // 3), FIELDS // 3)
        rows = pl.ds(0, 16)
        return pltpu.make_async_copy(
            x_ref.at[fields, rows, :], own.at[fields, rows, :], first_sems.at[part]
        )

    for part in range(3):
        fetch_first(part).start()
    climate_out[...] = jnp.full((1, LANES), climate_ref[0], f32)

    def turned(block):
        ones = jnp.ones((PADDED - FIELDS,) + block.shape[1:], bf16)
        return jnp.swapaxes(jnp.concatenate([block, ones], axis=0), 0, 1)

    zeros = jnp.zeros((8, PADDED, LON), bf16)
    before[0:8] = zeros
    before[72:80] = zeros
    before[pl.ds(jnp.where(role == 0, 72, 0), 8)] = turned(halo_ref[...])

    def take(step):
        place = pl.multiple_of(step * 16, 16)
        before[pl.ds(8 + place, 16)] = turned(own[:, pl.ds(place, 16), :])

    diff = jnp.concatenate([diff_ref[...], jnp.zeros((1, LANES - FIELDS), f32)], axis=1)
    diff = jnp.broadcast_to(diff, (LANES, LANES)).T[:PADDED]
    diff = jnp.concatenate([diff] * TILES, axis=1)
    bias = b_in_ref[...]
    high = bias.astype(bf16)
    middle = (bias - high.astype(f32)).astype(bf16)
    low = (bias - high.astype(f32) - middle.astype(f32)).astype(bf16)
    w_in = jnp.concatenate([w_in_ref[...], high, middle, low], axis=0).astype(f32)
    w_in = jnp.concatenate([w_in, jnp.zeros((LANES - PADDED, LATENT), f32)], axis=0).T[:, :PADDED].astype(bf16)
    w_out = jnp.concatenate(
        [w_out_ref[...] * bf16(0.5), jnp.zeros((PADDED - FIELDS, LATENT), bf16)], axis=0
    )

    for part in range(3):
        fetch_first(part).wait()
    for step in range(1, ROWS // 16):
        fetch(step).start()
    take(0)

    def advance(ref, place, count, give):
        rows, smooth = {}, {}

        def row(k):
            if k not in rows:
                rows[k] = ref[place + k]
            return rows[k].astype(f32)

        def smooth_of(n):
            pieces = []
            for piece in (2 * n, 2 * n + 1):
                k, tile = divmod(piece, TILES)
                if k not in smooth:
                    c = row(k)
                    around = row(k - 1) + row(k + 1) + pltpu.roll(rows[k], 1, 1).astype(f32)
                    around = around + pltpu.roll(rows[k], LON - 1, 1).astype(f32)
                    smooth[k] = (c + diff * (around - 4.0 * c)).astype(bf16)
                pieces.append(smooth[k][:, tile * LANES : (tile + 1) * LANES])
            return jnp.concatenate(pieces, axis=1)

        def done(n, change):
            for half, piece in enumerate((2 * n, 2 * n + 1)):
                k, tile = divmod(piece, TILES)
                lanes = slice(tile * LANES, (tile + 1) * LANES)
                new = rows[k][:, lanes].astype(f32) + change[:, half * LANES : (half + 1) * LANES]
                give(k, tile, new.astype(bf16))

        mlp(count * TILES // 2, smooth_of, done, w_in, w_out)

    def first_rows(start, count):
        def give(k, tile, new):
            after[start + k, :, tile * LANES : (tile + 1) * LANES] = new

        advance(before, start + 7, count, give)

    def first(step, carry):
        first_rows(step * 16, 16)

        @pl.when(step < ROWS // 16 - 1)
        def _():
            fetch(step + 1).wait()
            take(step + 1)

        return carry

    lax.fori_loop(0, ROWS // 16, first, 0)
    first_rows(ROWS, 2)

    @pl.when(role == 0)
    def _():
        after[0] = jnp.zeros((PADDED, LON), bf16)

    @pl.when(role == 1)
    def _():
        after[ROWS + 1] = jnp.zeros((PADDED, LON), bf16)

    def second(step, carry):
        pieces = {}

        def give(k, tile, new):
            pieces[k, tile] = new
            if k % 8 == 7:
                rows = [pieces.pop((k - 7 + a, tile)) for a in range(8)]
                for group, message in enumerate(to_messages(rows)):
                    owner, slot = owner_of(step * 2 + k // 8, tile, group)
                    out_ref[owner, slot * MAIN : (slot + 1) * MAIN, :] = message[:MAIN]
                    rests[owner, slot] = message[MAIN:]

        advance(after, step * 16 + 1, 16, give)
        for half in range(2):
            for u in range(8):
                owner = step * 16 + half * 8 + u
                parts = [rests[owner, slot].astype(f32)[:REST] for slot in range(TILES)]
                tail = jnp.concatenate(parts + [jnp.zeros((1, LANES), f32)], axis=0)
                out_ref[owner, TAIL:MESSAGE, :] = tail.astype(bf16)
        return carry

    lax.fori_loop(0, ROWS // 16, second, 0)


def split(a):
    high = a.astype(jnp.bfloat16)
    return high, (a - high.astype(jnp.float32)).astype(jnp.bfloat16)


def streamed(a):
    high, rest = split(a)
    return jnp.concatenate([high, rest, high], axis=1)


def held(a):
    low = lax.broadcasted_iota(jnp.int32, (MEMBERS, LANES), 1) < MEMBERS
    high, rest = split(jnp.concatenate([jnp.where(low, a, 0.0), jnp.where(low, 0.0, a)], axis=0))
    return jnp.concatenate([high, high, rest], axis=0)


def pair_dot(left, right):
    return jnp.dot(left, right, preferred_element_type=jnp.float32)


def wide_dot(a, b):
    (a_high, a_low), (b_high, b_low) = split(a), split(b)
    left = jnp.concatenate([a_high, a_low, a_high], axis=1)
    right = jnp.concatenate([b_high, b_high, b_low], axis=1)
    return lax.dot_general(left, right, (((1,), (1,)), ((), ())), preferred_element_type=jnp.float32)


def weights_kernel(
    idx_ref, value_ref, weight_ref, g_ref, turn, mix_ref, total_ref
):
    f32, bf16 = jnp.float32, jnp.bfloat16
    lane = lax.broadcasted_iota(jnp.int32, (MEMBERS, LANES), 1)
    low = lane < MEMBERS
    eye = jnp.where(
        (lane & (MEMBERS - 1)) == lax.broadcasted_iota(jnp.int32, (MEMBERS, LANES), 0), 1.0, 0.0
    )
    odd = jnp.where(lax.broadcasted_iota(jnp.int32, (1, 2 * OBS), 1) >= OBS, EDGE, 0)

    def halves(a):
        first = jnp.sum(jnp.where(low[: a.shape[0]], a, 0.0), axis=1, keepdims=True)
        second = jnp.sum(jnp.where(low[: a.shape[0]], 0.0, a), axis=1, keepdims=True)
        return jnp.where(low[: a.shape[0]], first, second)

    def load(step, carry):
        m = pl.multiple_of(step * 16, 16)
        turn[:, pl.ds(m, 16), :] = jnp.swapaxes(g_ref[pl.ds(m, 16)], 0, 1)
        return carry

    lax.fori_loop(0, MEMBERS // 16, load, 0, unroll=4)
    precisions, pulled = [], []
    for k in range(TILES):
        idx = jnp.concatenate(
            [idx_ref[2 * k + e : 2 * k + e + 1, :] for e in range(2)], axis=1
        )
        cell = idx & (CELLS - 1)
        place = (cell >> 3) * GROUP + odd + (cell & 7)
        field = jnp.broadcast_to(idx >> 6, (MEMBERS, 2 * OBS))
        hot = jnp.where(lax.broadcasted_iota(jnp.int32, (LANES, 2 * OBS), 0) == place, 1.0, 0.0)
        hot = hot.astype(bf16)

        def pick(total, start, first, count):
            block = turn[pl.ds(start, count)].reshape(count * MEMBERS, LANES)
            values = jnp.dot(block, hot, preferred_element_type=f32)
            for f in range(count):
                here = field == first + f
                total = jnp.where(here, values[f * MEMBERS : (f + 1) * MEMBERS], total)
            return total

        def picks(step, total):
            for part in range(4):
                first = step * 32 + part * 8
                total = pick(total, k * MAIN + first, first, 8)
            return total

        observed = pick(jnp.zeros((MEMBERS, 2 * OBS), f32), TAIL + k * REST, MAIN, REST)
        observed = lax.fori_loop(0, MAIN // 32, picks, observed, unroll=2)
        sides, pulls = [], []
        for e in range(2):
            mine = observed[:, e * OBS : (e + 1) * OBS]
            row = slice(2 * k + e, 2 * k + e + 1)
            obs_mean = jnp.sum(mine, axis=0, keepdims=True) * (1.0 / MEMBERS)
            spread = mine - obs_mean
            weighted = spread * weight_ref[row, :]
            sides.append(wide_dot(weighted, spread))
            pulls.append(jnp.sum(weighted * (value_ref[row, :] - obs_mean), axis=1, keepdims=True))
        precisions.append(jnp.concatenate(sides, axis=1) + (MEMBERS - 1.0) * eye)
        pulled.append(jnp.where(low, pulls[0], pulls[1]))

    scales = [MEMBERS * halves(jnp.sum(p * eye, axis=0, keepdims=True)) for p in precisions]
    iterates = [p / s for p, s in zip(precisions, scales)]

    def newton(step, carry):
        iterates, roots = carry
        rights = [held(i) for i in iterates]
        products = [pair_dot(streamed(r), i) for r, i in zip(roots, rights)]
        rights = [jnp.concatenate([i, held(r)], axis=1) for i, r in zip(rights, roots)]
        factors = [0.5 * (3.0 * eye - p) for p in products]
        new = [pair_dot(streamed(f), r) for f, r in zip(factors, rights)]
        return [n[:, :LANES] for n in new], [n[:, LANES:] for n in new]

    factors = [0.5 * (3.0 * eye - i) for i in iterates]
    iterates = [pair_dot(streamed(f), held(i)) for f, i in zip(factors, iterates)]
    _, roots = lax.fori_loop(1, NS_ITERS, newton, (iterates, factors), unroll=NS_ITERS - 1)
    shifts = [pair_dot(streamed(r), held(p)) for r, p in zip(roots, pulled)]
    shifts = [pair_dot(streamed(r), held(p)) for r, p in zip(roots, shifts)]
    total = jnp.zeros((1, LANES), f32)
    odd_cell = (lane & EDGE) != 0
    for k, (root, shift, scale) in enumerate(zip(roots, shifts, scales)):
        combined = jnp.sqrt((MEMBERS - 1.0) / scale) * root + shift / scale
        rest = (1.0 - jnp.sum(combined, axis=0, keepdims=True)) * (1.0 / MEMBERS)
        mix = combined + rest
        across = mix.T
        across = jnp.concatenate([across[:MEMBERS], across[MEMBERS:]], axis=1)
        mix_ref[k] = jnp.concatenate(split(across), axis=1)
        shares = jnp.where(
            odd_cell,
            jnp.sum(jnp.where(low, 0.0, mix), axis=1, keepdims=True),
            jnp.sum(jnp.where(low, mix, 0.0), axis=1, keepdims=True),
        )
        total = total + jnp.sum(shares * turn[k * MAIN].astype(f32), axis=0, keepdims=True)
    total_ref[...] = jnp.sum(total, axis=1, keepdims=True)


def apply_kernel(mix_ref, turn, out_ref, back):
    f32, bf16 = jnp.float32, jnp.bfloat16
    even = jnp.where((lax.broadcasted_iota(jnp.int32, (MEMBERS, BLOCK), 1) & EDGE) == 0, 1.0, 0.0)
    even = even.astype(bf16)
    uneven = bf16(1.0) - even
    def mixed(k, places):
        x = jnp.concatenate([turn[place] for place in places], axis=1)
        width = len(places) * LANES
        x = jnp.concatenate([x * even[:, :width], x * uneven[:, :width]], axis=0)
        x = jnp.concatenate([x, x], axis=0)
        new = jnp.dot(mix_ref[k], x, preferred_element_type=f32).astype(bf16)
        for n, place in enumerate(places):
            back[place] = new[:, n * LANES : (n + 1) * LANES]

    def main(k, step):
        for pair in range(8):
            place = k * MAIN + step * 16 + 2 * pair
            mixed(k, [place, place + 1])

    def give(first, count, step):
        members = pl.ds(pl.multiple_of(step * 16, 16), 16)
        block = jnp.swapaxes(back[first : first + count, members, :], 0, 1)
        out_ref[members, first : first + count, :] = block

    for k in range(TILES):
        for place in range(TAIL + k * REST, TAIL + (k + 1) * REST, 2):
            mixed(k, [p for p in (place, place + 1) if p < TAIL + (k + 1) * REST])

    for k in range(TILES + 1):

        def both(step, carry):
            if k < TILES:
                main(k, step)
            if k > 0:
                give((k - 1) * MAIN, MAIN, step)
            else:
                give(TAIL, MESSAGE - TAIL, step)
            return carry

        lax.fori_loop(0, 4, both, 0, unroll=4)


def seal_kernel(climate_ref, total_ref, other_ref, messages_ref, out_ref):
    f32, bf16 = jnp.float32, jnp.bfloat16
    total = total_ref[...] + other_ref[...] - climate_ref[...] * (VALUES // MEMBERS)
    high = total.astype(bf16).astype(f32)
    middle = (total - high).astype(bf16).astype(f32)
    lane = lax.broadcasted_iota(jnp.int32, (16, LANES), 1)
    row = lax.broadcasted_iota(jnp.int32, (16, LANES), 0)
    parts = jnp.where(lane == 0, high, jnp.where(lane == 1, middle, total - high - middle))
    parts = jnp.where(lane < 3, parts, 0.0)
    for owner in range(MEMBERS):
        tail = messages_ref[owner, TAIL:MESSAGE, :].astype(f32)
        out_ref[owner, TAIL:MESSAGE, :] = jnp.where(row == 15, parts, tail).astype(bf16)


def last_kernel(back_ref, out_ref, grid, sems):
    f32, bf16 = jnp.float32, jnp.bfloat16

    def send(first, count):
        fields = pl.ds(first, count)
        return pltpu.make_async_copy(grid.at[fields], out_ref.at[fields], sems.at[first // 16])

    totals = jnp.zeros((MESSAGE - TAIL, LANES), f32)
    for owner in range(MEMBERS):
        totals = totals + back_ref[owner, TAIL:MESSAGE, :].astype(f32)
    offset = jnp.sum(totals[MESSAGE - TAIL - 1 :], axis=1, keepdims=True) / -VALUES

    def piece(owner, slot, first, count):
        if first < MAIN:
            return back_ref[owner, slot * MAIN + first : slot * MAIN + first + count, :]
        rest = back_ref[owner, TAIL:MESSAGE, :].astype(f32)
        return rest[slot * REST : (slot + 1) * REST].astype(bf16)

    chunks = [(first, min(16, FIELDS - first)) for first in range(0, FIELDS, 16)]
    for first, count in chunks:

        def block(step, carry):
            for tile in range(TILES):
                rows = []
                for half in range(2):
                    pieces = []
                    for group in range(8):
                        owner, slot = owner_of(step * 2 + half, tile, group)
                        pieces.append(piece(owner, slot, first, count))
                    rows += to_rows(pieces)
                values = jnp.swapaxes(jnp.stack(rows), 0, 1)
                place = pl.ds(pl.multiple_of(step * 16, 16), 16)
                lanes = slice(tile * LANES, (tile + 1) * LANES)
                if first == 0:
                    grid[0:1, place, lanes] = (values[:1].astype(f32) + offset).astype(bf16)
                    grid[1:count, place, lanes] = values[1:]
                else:
                    grid[first : first + count, place, lanes] = values
            return carry

        lax.fori_loop(0, ROWS // 16, block, 0, unroll=4)
        send(first, count).start()
    for first, count in chunks:
        send(first, count).wait()


MESSAGES = jax.ShapeDtypeStruct((MEMBERS, MESSAGE, LANES), jnp.bfloat16)
TURNED = jax.ShapeDtypeStruct((MESSAGE, MEMBERS, LANES), jnp.bfloat16)


def forecast(role, climate, x, halo, diff, w_in, b_in, w_out):
    cells = 2 * ROWS * LON
    return pl.pallas_call(
        forecast_kernel,
        out_shape=(MESSAGES, jax.ShapeDtypeStruct((1, LANES), jnp.float32)),
        in_specs=[IN_SMEM, IN_SMEM, IN_HBM] + [IN_VMEM] * 5,
        out_specs=(IN_VMEM, IN_VMEM),
        scratch_shapes=[
            pltpu.VMEM((FIELDS, ROWS, LON), jnp.bfloat16),
            pltpu.VMEM((ROWS + 16, PADDED, LON), jnp.bfloat16),
            pltpu.VMEM((ROWS + 2, PADDED, LON), jnp.bfloat16),
            pltpu.VMEM((MEMBERS, TILES, PADDED - MAIN, LANES), jnp.bfloat16),
            pltpu.SemaphoreType.DMA((ROWS // 16,)),
            pltpu.SemaphoreType.DMA((3,)),
        ],
        compiler_params=params(32),
        cost_estimate=cost(cells * LATENT * 256 * 4, 7 << 20, cells * LATENT),
        name="forecast",
    )(role, climate, in_hbm(x), halo, in_hbm(diff), in_hbm(w_in), in_hbm(b_in), in_hbm(w_out))


def weights(idx, value, weight, g):
    return pl.pallas_call(
        weights_kernel,
        out_shape=(
            TURNED,
            jax.ShapeDtypeStruct((TILES, MEMBERS, 2 * LANES), jnp.bfloat16),
            jax.ShapeDtypeStruct((1, 1), jnp.float32),
        ),
        in_specs=[IN_VMEM] * 4,
        out_specs=(IN_VMEM,) * 3,
        compiler_params=params(32),
        cost_estimate=cost(8 << 30, 7 << 20),
        name="weights",
    )(idx, value, weight, g)


def apply(mixes, turn):
    return pl.pallas_call(
        apply_kernel,
        out_shape=MESSAGES,
        in_specs=[IN_VMEM] * 2,
        out_specs=IN_VMEM,
        scratch_shapes=[pltpu.VMEM(TURNED.shape, jnp.bfloat16)],
        compiler_params=params(32),
        cost_estimate=cost(8 << 30, 7 << 20),
        name="apply",
    )(mixes, turn)


def seal(climate, total, other, messages):
    return pl.pallas_call(
        seal_kernel,
        out_shape=MESSAGES,
        in_specs=[IN_VMEM] * 4,
        out_specs=IN_VMEM,
        input_output_aliases={3: 0},
        compiler_params=params(32),
        cost_estimate=cost(1 << 16, 1 << 18),
        name="seal",
    )(climate, total, other, messages)


def put_back(back):
    return pl.pallas_call(
        last_kernel,
        out_shape=jax.ShapeDtypeStruct((FIELDS, ROWS, LON), jnp.bfloat16),
        in_specs=[IN_VMEM],
        out_specs=IN_HBM,
        scratch_shapes=[
            pltpu.VMEM((FIELDS, ROWS, LON), jnp.bfloat16),
            pltpu.SemaphoreType.DMA((PADDED // 16 + 1,)),
        ],
        compiler_params=params(50),
        cost_estimate=cost(1 << 20, 7 << 20),
        name="put_back",
    )(back)


def exchange(messages):
    return lax.all_to_all(messages, "dev", split_axis=0, concat_axis=0, tiled=True)


def body(
    initial_realizations, diffusivity, w_in, b_in, w_out, obs_index, obs_value, obs_weight, climate
):
    role = lax.axis_index("role")
    dev = lax.axis_index("dev")
    x = initial_realizations.reshape(FIELDS, ROWS, LON)
    index = lax.dynamic_slice_in_dim(obs_index, dev * PATCHES, PATCHES, 0)
    group = dev % 8 * 3 + jnp.arange(PATCHES)[:, None] // 2
    index = (index & ~(CELLS - EDGE)) | ((index + group * EDGE) & (CELLS - EDGE))
    edge = lax.dynamic_slice_in_dim(x, jnp.where(role == 0, ROWS - 8, 0), 8, 1)
    halo = lax.ppermute(edge, "role", [(0, 1), (1, 0)])
    halo, index = lax.optimization_barrier((halo, index))
    sent, climate = forecast(
        role.reshape(1), climate, x, halo, diffusivity.reshape(1, FIELDS), w_in.T, b_in.reshape(1, LATENT), w_out
    )
    got = exchange(sent)
    turn, mixes, total = weights(index, obs_value, obs_weight, got)
    other = lax.ppermute(total, "role", [(0, 1), (1, 0)])
    back = exchange(seal(climate, total, other, apply(mixes, turn)))
    return put_back(back)[None]


def solution(mesh):
    in_specs = (
        P("dev", None, "role", None),
        P(),
        P(),
        P(),
        P(),
        P("role", None),
        P(("role", "dev"), None),
        P(("role", "dev"), None),
        P(),
    )
    out_specs = P("dev", None, "role", None)
    return jax.shard_map(body, mesh=mesh, in_specs=in_specs, out_specs=out_specs, check_vma=False)
```

```python
import jax
import jax.numpy as jnp
from jax import lax
from jax.experimental import pallas as pl
from jax.experimental.pallas import tpu as pltpu
from jax.sharding import PartitionSpec as P

EDGE = 8
NS_ITERS = 12
CELLS = 64
LANES = 128
FIELDS = 69
PADDED = 72
LATENT = 512
LON = 384
TILES = 3
ROWS = 64
MEMBERS = 64
OBS = 128
PATCHES = 6
MAIN = 64
REST = FIELDS - MAIN
TAIL = TILES * MAIN
MESSAGE = 208
GROUP = 16
BLOCK = 256
DEPTH = 3
GELU_A = 0.7978845608028654
GELU_B = 0.044715 * 0.7978845608028654
VALUES = MEMBERS * 128 * LON

IN_VMEM = pl.BlockSpec(memory_space=pltpu.VMEM)
IN_HBM = pl.BlockSpec(memory_space=pltpu.HBM)
IN_SMEM = pl.BlockSpec(memory_space=pltpu.SMEM)


def params(mib):
    return pltpu.CompilerParams(vmem_limit_bytes=mib * 1024 * 1024)


def in_hbm(x):
    return pltpu.with_memory_space_constraint(x, pltpu.HBM)


def cost(flops, size, tanhs=0):
    return pl.CostEstimate(flops=flops, bytes_accessed=size, transcendentals=tanhs)


def gelu_twice(linear):
    linear = linear.astype(jnp.bfloat16)
    inner = linear * (jnp.bfloat16(GELU_A) + jnp.bfloat16(GELU_B) * (linear * linear))
    return linear * (jnp.bfloat16(1.0) + jnp.tanh(inner))


def mlp(count, smooth_of, done, w_in, w_out):
    linear = {}
    for n in range(count + DEPTH):
        if n < count:
            linear[n] = jnp.dot(w_in, smooth_of(n), preferred_element_type=jnp.float32)
        if n >= DEPTH:
            hidden = gelu_twice(linear.pop(n - DEPTH))
            done(n - DEPTH, jnp.dot(w_out, hidden, preferred_element_type=jnp.float32))


def choose(rows):
    lane = lax.broadcasted_iota(jnp.int32, rows[0].shape, 1)
    rows = [rows[-p % 8] for p in range(8)]
    for bit in (1, 2, 4):
        move = (lane & (bit * GROUP)) != 0
        rows = [jnp.where(move, rows[(p - bit) % 8], rows[p]) for p in range(8)]
    return rows


def to_messages(rows):
    return choose([pltpu.roll(row, a * GROUP, 1) if a else row for a, row in enumerate(rows)])


def to_rows(messages):
    rows = choose(messages)
    return [pltpu.roll(row, LANES - a * GROUP, 1) if a else row for a, row in enumerate(rows)]


def owner_of(r, tile, group):
    number = tile * 8 + group
    return r * 8 + number // 3, number % 3


def forecast_kernel(
    role_ref, climate_ref, x_ref, halo_ref, diff_ref, w_in_ref, b_in_ref, w_out_ref,
    out_ref, climate_out, own, before, after, rests, in_sems, first_sems,
):
    f32, bf16 = jnp.float32, jnp.bfloat16
    role = role_ref[0]

    def fetch(step):
        rows = pl.ds(step * 16, 16)
        return pltpu.make_async_copy(x_ref.at[:, rows, :], own.at[:, rows, :], in_sems.at[step])

    def fetch_first(part):
        fields = pl.ds(part * (FIELDS // 3), FIELDS // 3)
        rows = pl.ds(0, 16)
        return pltpu.make_async_copy(
            x_ref.at[fields, rows, :], own.at[fields, rows, :], first_sems.at[part]
        )

    for part in range(3):
        fetch_first(part).start()
    climate_out[...] = jnp.full((1, LANES), climate_ref[0], f32)

    def turned(block):
        ones = jnp.ones((PADDED - FIELDS,) + block.shape[1:], bf16)
        return jnp.swapaxes(jnp.concatenate([block, ones], axis=0), 0, 1)

    zeros = jnp.zeros((8, PADDED, LON), bf16)
    before[0:8] = zeros
    before[72:80] = zeros
    before[pl.ds(jnp.where(role == 0, 72, 0), 8)] = turned(halo_ref[...])

    def take(step):
        place = pl.multiple_of(step * 16, 16)
        before[pl.ds(8 + place, 16)] = turned(own[:, pl.ds(place, 16), :])

    diff = jnp.concatenate([diff_ref[...], jnp.zeros((1, LANES - FIELDS), f32)], axis=1)
    diff = jnp.broadcast_to(diff, (LANES, LANES)).T[:PADDED]
    diff = jnp.concatenate([diff] * TILES, axis=1)
    bias = b_in_ref[...]
    high = bias.astype(bf16)
    middle = (bias - high.astype(f32)).astype(bf16)
    low = (bias - high.astype(f32) - middle.astype(f32)).astype(bf16)
    w_in = jnp.concatenate([w_in_ref[...], high, middle, low], axis=0).astype(f32)
    w_in = jnp.concatenate([w_in, jnp.zeros((LANES - PADDED, LATENT), f32)], axis=0).T[:, :PADDED].astype(bf16)
    w_out = jnp.concatenate(
        [w_out_ref[...] * bf16(0.5), jnp.zeros((PADDED - FIELDS, LATENT), bf16)], axis=0
    )

    for part in range(3):
        fetch_first(part).wait()
    for step in range(1, ROWS // 16):
        fetch(step).start()
    take(0)

    def advance(ref, place, count, give):
        rows, smooth = {}, {}

        def row(k):
            if k not in rows:
                rows[k] = ref[place + k]
            return rows[k].astype(f32)

        def smooth_of(n):
            pieces = []
            for piece in (2 * n, 2 * n + 1):
                k, tile = divmod(piece, TILES)
                if k not in smooth:
                    c = row(k)
                    around = row(k - 1) + row(k + 1) + pltpu.roll(rows[k], 1, 1).astype(f32)
                    around = around + pltpu.roll(rows[k], LON - 1, 1).astype(f32)
                    smooth[k] = (c + diff * (around - 4.0 * c)).astype(bf16)
                pieces.append(smooth[k][:, tile * LANES : (tile + 1) * LANES])
            return jnp.concatenate(pieces, axis=1)

        def done(n, change):
            for half, piece in enumerate((2 * n, 2 * n + 1)):
                k, tile = divmod(piece, TILES)
                lanes = slice(tile * LANES, (tile + 1) * LANES)
                new = rows[k][:, lanes].astype(f32) + change[:, half * LANES : (half + 1) * LANES]
                give(k, tile, new.astype(bf16))

        mlp(count * TILES // 2, smooth_of, done, w_in, w_out)

    def first_rows(start, count):
        def give(k, tile, new):
            after[start + k, :, tile * LANES : (tile + 1) * LANES] = new

        advance(before, start + 7, count, give)

    def first(step, carry):
        first_rows(step * 16, 16)

        @pl.when(step < ROWS // 16 - 1)
        def _():
            fetch(step + 1).wait()
            take(step + 1)

        return carry

    lax.fori_loop(0, ROWS // 16, first, 0)
    first_rows(ROWS, 2)

    @pl.when(role == 0)
    def _():
        after[0] = jnp.zeros((PADDED, LON), bf16)

    @pl.when(role == 1)
    def _():
        after[ROWS + 1] = jnp.zeros((PADDED, LON), bf16)

    def second(step, carry):
        pieces = {}

        def give(k, tile, new):
            pieces[k, tile] = new
            if k % 8 == 7:
                rows = [pieces.pop((k - 7 + a, tile)) for a in range(8)]
                for group, message in enumerate(to_messages(rows)):
                    owner, slot = owner_of(step * 2 + k // 8, tile, group)
                    out_ref[owner, slot * MAIN : (slot + 1) * MAIN, :] = message[:MAIN]
                    rests[owner, slot] = message[MAIN:]

        advance(after, step * 16 + 1, 16, give)
        for half in range(2):
            for u in range(8):
                owner = step * 16 + half * 8 + u
                parts = [rests[owner, slot].astype(f32)[:REST] for slot in range(TILES)]
                tail = jnp.concatenate(parts + [jnp.zeros((1, LANES), f32)], axis=0)
                out_ref[owner, TAIL:MESSAGE, :] = tail.astype(bf16)
        return carry

    lax.fori_loop(0, ROWS // 16, second, 0)


def split(a):
    high = a.astype(jnp.bfloat16)
    return high, (a - high.astype(jnp.float32)).astype(jnp.bfloat16)


def streamed(a):
    high, rest = split(a)
    return jnp.concatenate([high, rest, high], axis=1)


def held(a):
    low = lax.broadcasted_iota(jnp.int32, (MEMBERS, LANES), 1) < MEMBERS
    high, rest = split(jnp.concatenate([jnp.where(low, a, 0.0), jnp.where(low, 0.0, a)], axis=0))
    return jnp.concatenate([high, high, rest], axis=0)


def pair_dot(left, right):
    return jnp.dot(left, right, preferred_element_type=jnp.float32)


def wide_dot(a, b):
    (a_high, a_low), (b_high, b_low) = split(a), split(b)
    left = jnp.concatenate([a_high, a_low, a_high], axis=1)
    right = jnp.concatenate([b_high, b_high, b_low], axis=1)
    return lax.dot_general(left, right, (((1,), (1,)), ((), ())), preferred_element_type=jnp.float32)


def weights_kernel(
    idx_ref, value_ref, weight_ref, g_ref, turn, mix_ref, total_ref
):
    f32, bf16 = jnp.float32, jnp.bfloat16
    lane = lax.broadcasted_iota(jnp.int32, (MEMBERS, LANES), 1)
    low = lane < MEMBERS
    eye = jnp.where(
        (lane & (MEMBERS - 1)) == lax.broadcasted_iota(jnp.int32, (MEMBERS, LANES), 0), 1.0, 0.0
    )
    odd = jnp.where(lax.broadcasted_iota(jnp.int32, (1, 2 * OBS), 1) >= OBS, EDGE, 0)

    def halves(a):
        first = jnp.sum(jnp.where(low[: a.shape[0]], a, 0.0), axis=1, keepdims=True)
        second = jnp.sum(jnp.where(low[: a.shape[0]], 0.0, a), axis=1, keepdims=True)
        return jnp.where(low[: a.shape[0]], first, second)

    def load(step, carry):
        m = pl.multiple_of(step * 16, 16)
        turn[:, pl.ds(m, 16), :] = jnp.swapaxes(g_ref[pl.ds(m, 16)], 0, 1)
        return carry

    lax.fori_loop(0, MEMBERS // 16, load, 0, unroll=4)
    precisions, pulled = [], []
    for k in range(TILES):
        idx = jnp.concatenate(
            [idx_ref[2 * k + e : 2 * k + e + 1, :] for e in range(2)], axis=1
        )
        cell = idx & (CELLS - 1)
        place = (cell >> 3) * GROUP + odd + (cell & 7)
        field = idx >> 6
        hot = jnp.where(lax.broadcasted_iota(jnp.int32, (LANES, 2 * OBS), 0) == place, 1.0, 0.0)
        late = (field & 32) != 0
        both = jnp.concatenate([jnp.where(late, 0.0, hot), jnp.where(late, hot, 0.0)], axis=0)
        hot, both = hot.astype(bf16), both.astype(bf16)
        rest = jnp.broadcast_to(field - MAIN, (MEMBERS, 2 * OBS))
        main = jnp.broadcast_to(jnp.where(field < MAIN, field & 31, -1), (MEMBERS, 2 * OBS))

        def flat(start, count):
            return turn[start : start + count].reshape(count * MEMBERS, LANES)

        def pick(total, values, wanted, first, count):
            for f in range(count):
                here = wanted == first + f
                total = jnp.where(here, values[f * MEMBERS : (f + 1) * MEMBERS], total)
            return total

        values = jnp.dot(flat(TAIL + k * REST, REST), hot, preferred_element_type=f32)
        observed = pick(jnp.zeros((MEMBERS, 2 * OBS), f32), values, rest, 0, REST)
        for first in range(0, 32, 8):
            start = k * MAIN + first
            block = jnp.concatenate([flat(start, 8), flat(start + 32, 8)], axis=1)
            values = jnp.dot(block, both, preferred_element_type=f32)
            observed = pick(observed, values, main, first, 8)
        sides, pulls = [], []
        for e in range(2):
            mine = observed[:, e * OBS : (e + 1) * OBS]
            row = slice(2 * k + e, 2 * k + e + 1)
            obs_mean = jnp.sum(mine, axis=0, keepdims=True) * (1.0 / MEMBERS)
            spread = mine - obs_mean
            weighted = spread * weight_ref[row, :]
            sides.append(wide_dot(weighted, spread))
            pulls.append(jnp.sum(weighted * (value_ref[row, :] - obs_mean), axis=1, keepdims=True))
        precisions.append(jnp.concatenate(sides, axis=1) + (MEMBERS - 1.0) * eye)
        pulled.append(jnp.where(low, pulls[0], pulls[1]))

    scales = [MEMBERS * halves(jnp.sum(p * eye, axis=0, keepdims=True)) for p in precisions]
    iterates = [p / s for p, s in zip(precisions, scales)]

    def newton(step, carry):
        iterates, roots = carry
        rights = [held(i) for i in iterates]
        products = [pair_dot(streamed(r), i) for r, i in zip(roots, rights)]
        rights = [jnp.concatenate([i, held(r)], axis=1) for i, r in zip(rights, roots)]
        factors = [0.5 * (3.0 * eye - p) for p in products]
        new = [pair_dot(streamed(f), r) for f, r in zip(factors, rights)]
        return [n[:, :LANES] for n in new], [n[:, LANES:] for n in new]

    factors = [0.5 * (3.0 * eye - i) for i in iterates]
    iterates = [pair_dot(streamed(f), held(i)) for f, i in zip(factors, iterates)]
    _, roots = lax.fori_loop(1, NS_ITERS, newton, (iterates, factors), unroll=NS_ITERS - 1)
    shifts = [pair_dot(streamed(r), held(p)) for r, p in zip(roots, pulled)]
    shifts = [pair_dot(streamed(r), held(p)) for r, p in zip(roots, shifts)]
    total = jnp.zeros((1, LANES), f32)
    odd_cell = (lane & EDGE) != 0
    for k, (root, shift, scale) in enumerate(zip(roots, shifts, scales)):
        combined = jnp.sqrt((MEMBERS - 1.0) / scale) * root + shift / scale
        rest = (1.0 - jnp.sum(combined, axis=0, keepdims=True)) * (1.0 / MEMBERS)
        mix = combined + rest
        across = mix.T
        across = jnp.concatenate([across[:MEMBERS], across[MEMBERS:]], axis=1)
        mix_ref[k] = jnp.concatenate(split(across), axis=1)
        shares = jnp.where(
            odd_cell,
            jnp.sum(jnp.where(low, 0.0, mix), axis=1, keepdims=True),
            jnp.sum(jnp.where(low, mix, 0.0), axis=1, keepdims=True),
        )
        total = total + jnp.sum(shares * turn[k * MAIN].astype(f32), axis=0, keepdims=True)
    total_ref[...] = jnp.sum(total, axis=1, keepdims=True)


def apply_kernel(mix_ref, turn, out_ref, back):
    f32, bf16 = jnp.float32, jnp.bfloat16
    even = jnp.where((lax.broadcasted_iota(jnp.int32, (MEMBERS, BLOCK), 1) & EDGE) == 0, 1.0, 0.0)
    even = even.astype(bf16)
    uneven = bf16(1.0) - even
    def mixed(k, places):
        x = jnp.concatenate([turn[place] for place in places], axis=1)
        width = len(places) * LANES
        x = jnp.concatenate([x * even[:, :width], x * uneven[:, :width]], axis=0)
        x = jnp.concatenate([x, x], axis=0)
        new = jnp.dot(mix_ref[k], x, preferred_element_type=f32).astype(bf16)
        for n, place in enumerate(places):
            back[place] = new[:, n * LANES : (n + 1) * LANES]

    def main(k, step):
        for pair in range(8):
            place = k * MAIN + step * 16 + 2 * pair
            mixed(k, [place, place + 1])

    def give(first, count, step):
        members = pl.ds(pl.multiple_of(step * 16, 16), 16)
        block = jnp.swapaxes(back[first : first + count, members, :], 0, 1)
        out_ref[members, first : first + count, :] = block

    for k in range(TILES):
        for place in range(TAIL + k * REST, TAIL + (k + 1) * REST, 2):
            mixed(k, [p for p in (place, place + 1) if p < TAIL + (k + 1) * REST])

    for k in range(TILES + 1):

        def both(step, carry):
            if k < TILES:
                main(k, step)
            if k > 0:
                give((k - 1) * MAIN, MAIN, step)
            else:
                give(TAIL, MESSAGE - TAIL, step)
            return carry

        lax.fori_loop(0, 4, both, 0, unroll=4)


def seal_kernel(climate_ref, total_ref, other_ref, messages_ref, out_ref):
    f32, bf16 = jnp.float32, jnp.bfloat16
    total = total_ref[...] + other_ref[...] - climate_ref[...] * (VALUES // MEMBERS)
    high = total.astype(bf16).astype(f32)
    middle = (total - high).astype(bf16).astype(f32)
    lane = lax.broadcasted_iota(jnp.int32, (16, LANES), 1)
    row = lax.broadcasted_iota(jnp.int32, (16, LANES), 0)
    parts = jnp.where(lane == 0, high, jnp.where(lane == 1, middle, total - high - middle))
    parts = jnp.where(lane < 3, parts, 0.0).astype(bf16)
    for owner in range(MEMBERS):
        tail = messages_ref[owner, TAIL:MESSAGE, :]
        out_ref[owner, TAIL:MESSAGE, :] = jnp.where(row == 15, parts, tail)


def last_kernel(back_ref, out_ref, grid, sems):
    f32, bf16 = jnp.float32, jnp.bfloat16

    def send(first, count):
        fields = pl.ds(first, count)
        return pltpu.make_async_copy(grid.at[fields], out_ref.at[fields], sems.at[first // 16])

    totals = jnp.zeros((MESSAGE - TAIL, LANES), f32)
    for owner in range(MEMBERS):
        totals = totals + back_ref[owner, TAIL:MESSAGE, :].astype(f32)
    offset = jnp.sum(totals[MESSAGE - TAIL - 1 :], axis=1, keepdims=True) / -VALUES

    def piece(owner, slot, first, count):
        if first < MAIN:
            return back_ref[owner, slot * MAIN + first : slot * MAIN + first + count, :]
        rest = back_ref[owner, TAIL:MESSAGE, :].astype(f32)
        return rest[slot * REST : (slot + 1) * REST].astype(bf16)

    chunks = [(first, min(16, FIELDS - first)) for first in range(0, FIELDS, 16)]
    for first, count in chunks:

        def block(step, carry):
            for tile in range(TILES):
                rows = []
                for half in range(2):
                    pieces = []
                    for group in range(8):
                        owner, slot = owner_of(step * 2 + half, tile, group)
                        pieces.append(piece(owner, slot, first, count))
                    rows += to_rows(pieces)
                values = jnp.swapaxes(jnp.stack(rows), 0, 1)
                place = pl.ds(pl.multiple_of(step * 16, 16), 16)
                lanes = slice(tile * LANES, (tile + 1) * LANES)
                if first == 0:
                    grid[0:1, place, lanes] = (values[:1].astype(f32) + offset).astype(bf16)
                    grid[1:count, place, lanes] = values[1:]
                else:
                    grid[first : first + count, place, lanes] = values
            return carry

        lax.fori_loop(0, ROWS // 16, block, 0, unroll=4)
        send(first, count).start()
    for first, count in chunks:
        send(first, count).wait()


MESSAGES = jax.ShapeDtypeStruct((MEMBERS, MESSAGE, LANES), jnp.bfloat16)
TURNED = jax.ShapeDtypeStruct((MESSAGE, MEMBERS, LANES), jnp.bfloat16)


def forecast(role, climate, x, halo, diff, w_in, b_in, w_out):
    cells = 2 * ROWS * LON
    return pl.pallas_call(
        forecast_kernel,
        out_shape=(MESSAGES, jax.ShapeDtypeStruct((1, LANES), jnp.float32)),
        in_specs=[IN_SMEM, IN_SMEM, IN_HBM] + [IN_VMEM] * 5,
        out_specs=(IN_VMEM, IN_VMEM),
        scratch_shapes=[
            pltpu.VMEM((FIELDS, ROWS, LON), jnp.bfloat16),
            pltpu.VMEM((ROWS + 16, PADDED, LON), jnp.bfloat16),
            pltpu.VMEM((ROWS + 2, PADDED, LON), jnp.bfloat16),
            pltpu.VMEM((MEMBERS, TILES, PADDED - MAIN, LANES), jnp.bfloat16),
            pltpu.SemaphoreType.DMA((ROWS // 16,)),
            pltpu.SemaphoreType.DMA((3,)),
        ],
        compiler_params=params(32),
        cost_estimate=cost(cells * LATENT * 256 * 4, 7 << 20, cells * LATENT),
        name="forecast",
    )(role, climate, in_hbm(x), halo, in_hbm(diff), in_hbm(w_in), in_hbm(b_in), in_hbm(w_out))


def weights(idx, value, weight, g):
    return pl.pallas_call(
        weights_kernel,
        out_shape=(
            TURNED,
            jax.ShapeDtypeStruct((TILES, MEMBERS, 2 * LANES), jnp.bfloat16),
            jax.ShapeDtypeStruct((1, 1), jnp.float32),
        ),
        in_specs=[IN_VMEM] * 4,
        out_specs=(IN_VMEM,) * 3,
        compiler_params=params(32),
        cost_estimate=cost(8 << 30, 7 << 20),
        name="weights",
    )(idx, value, weight, g)


def apply(mixes, turn):
    return pl.pallas_call(
        apply_kernel,
        out_shape=MESSAGES,
        in_specs=[IN_VMEM] * 2,
        out_specs=IN_VMEM,
        scratch_shapes=[pltpu.VMEM(TURNED.shape, jnp.bfloat16)],
        compiler_params=params(32),
        cost_estimate=cost(8 << 30, 7 << 20),
        name="apply",
    )(mixes, turn)


def seal(climate, total, other, messages):
    return pl.pallas_call(
        seal_kernel,
        out_shape=MESSAGES,
        in_specs=[IN_VMEM] * 4,
        out_specs=IN_VMEM,
        input_output_aliases={3: 0},
        compiler_params=params(32),
        cost_estimate=cost(1 << 16, 1 << 18),
        name="seal",
    )(climate, total, other, messages)


def put_back(back):
    return pl.pallas_call(
        last_kernel,
        out_shape=jax.ShapeDtypeStruct((FIELDS, ROWS, LON), jnp.bfloat16),
        in_specs=[IN_VMEM],
        out_specs=IN_HBM,
        scratch_shapes=[
            pltpu.VMEM((FIELDS, ROWS, LON), jnp.bfloat16),
            pltpu.SemaphoreType.DMA((PADDED // 16 + 1,)),
        ],
        compiler_params=params(50),
        cost_estimate=cost(1 << 20, 7 << 20),
        name="put_back",
    )(back)


def exchange(messages):
    return lax.all_to_all(messages, "dev", split_axis=0, concat_axis=0, tiled=True)


def body(
    initial_realizations, diffusivity, w_in, b_in, w_out, obs_index, obs_value, obs_weight, climate
):
    role = lax.axis_index("role")
    dev = lax.axis_index("dev")
    x = initial_realizations.reshape(FIELDS, ROWS, LON)
    index = lax.dynamic_slice_in_dim(obs_index, dev * PATCHES, PATCHES, 0)
    group = dev % 8 * 3 + jnp.arange(PATCHES)[:, None] // 2
    index = (index & ~(CELLS - EDGE)) | ((index + group * EDGE) & (CELLS - EDGE))
    edge = lax.dynamic_slice_in_dim(x, jnp.where(role == 0, ROWS - 8, 0), 8, 1)
    halo = lax.ppermute(edge, "role", [(0, 1), (1, 0)])
    halo, index = lax.optimization_barrier((halo, index))
    sent, climate = forecast(
        role.reshape(1), climate, x, halo, diffusivity.reshape(1, FIELDS), w_in.T, b_in.reshape(1, LATENT), w_out
    )
    got = exchange(sent)
    turn, mixes, total = weights(index, obs_value, obs_weight, got)
    other = lax.ppermute(total, "role", [(0, 1), (1, 0)])
    back = exchange(seal(climate, total, other, apply(mixes, turn)))
    return put_back(back)[None]


def solution(mesh):
    in_specs = (
        P("dev", None, "role", None),
        P(),
        P(),
        P(),
        P(),
        P("role", None),
        P(("role", "dev"), None),
        P(("role", "dev"), None),
        P(),
    )
    out_specs = P("dev", None, "role", None)
    return jax.shard_map(body, mesh=mesh, in_specs=in_specs, out_specs=out_specs, check_vma=False)
```

```python
import jax
import jax.numpy as jnp
from jax import lax
from jax.experimental import pallas as pl
from jax.experimental.pallas import tpu as pltpu
from jax.sharding import PartitionSpec as P

EDGE = 8
NS_ITERS = 12
CELLS = 64
LANES = 128
FIELDS = 69
PADDED = 72
LATENT = 512
LON = 384
TILES = 3
ROWS = 64
MEMBERS = 64
OBS = 128
PATCHES = 6
MAIN = 64
REST = FIELDS - MAIN
TAIL = TILES * MAIN
MESSAGE = 208
GROUP = 16
BLOCK = 256
DEPTH = 3
GELU_A = 0.7978845608028654
GELU_B = 0.044715 * 0.7978845608028654
VALUES = MEMBERS * 128 * LON

IN_VMEM = pl.BlockSpec(memory_space=pltpu.VMEM)
IN_HBM = pl.BlockSpec(memory_space=pltpu.HBM)
IN_SMEM = pl.BlockSpec(memory_space=pltpu.SMEM)


def params(mib):
    return pltpu.CompilerParams(vmem_limit_bytes=mib * 1024 * 1024)


def in_hbm(x):
    return pltpu.with_memory_space_constraint(x, pltpu.HBM)


def cost(flops, size, tanhs=0):
    return pl.CostEstimate(flops=flops, bytes_accessed=size, transcendentals=tanhs)


def gelu_twice(linear):
    linear = linear.astype(jnp.bfloat16)
    inner = linear * (jnp.bfloat16(GELU_A) + jnp.bfloat16(GELU_B) * (linear * linear))
    return linear * (jnp.bfloat16(1.0) + jnp.tanh(inner))


def mlp(count, smooth_of, done, w_in, w_out):
    linear = {}
    for n in range(count + DEPTH):
        if n < count:
            linear[n] = jnp.dot(w_in, smooth_of(n), preferred_element_type=jnp.float32)
        if n >= DEPTH:
            hidden = gelu_twice(linear.pop(n - DEPTH))
            done(n - DEPTH, jnp.dot(w_out, hidden, preferred_element_type=jnp.float32))


def choose(rows):
    lane = lax.broadcasted_iota(jnp.int32, rows[0].shape, 1)
    rows = [rows[-p % 8] for p in range(8)]
    for bit in (1, 2, 4):
        move = (lane & (bit * GROUP)) != 0
        rows = [jnp.where(move, rows[(p - bit) % 8], rows[p]) for p in range(8)]
    return rows


def to_messages(rows):
    return choose([pltpu.roll(row, a * GROUP, 1) if a else row for a, row in enumerate(rows)])


def to_rows(messages):
    rows = choose(messages)
    return [pltpu.roll(row, LANES - a * GROUP, 1) if a else row for a, row in enumerate(rows)]


def owner_of(r, tile, group):
    number = tile * 8 + group
    return r * 8 + number // 3, number % 3


def forecast_kernel(
    role_ref, climate_ref, x_ref, halo_ref, diff_ref, w_in_ref, b_in_ref, w_out_ref,
    out_ref, climate_out, own, before, after, rests, in_sems, first_sems,
):
    f32, bf16 = jnp.float32, jnp.bfloat16
    role = role_ref[0]

    def fetch(step):
        rows = pl.ds(step * 16, 16)
        return pltpu.make_async_copy(x_ref.at[:, rows, :], own.at[:, rows, :], in_sems.at[step])

    def fetch_first(part):
        fields = pl.ds(part * (FIELDS // 3), FIELDS // 3)
        rows = pl.ds(0, 16)
        return pltpu.make_async_copy(
            x_ref.at[fields, rows, :], own.at[fields, rows, :], first_sems.at[part]
        )

    for part in range(3):
        fetch_first(part).start()
    climate_out[...] = jnp.full((1, LANES), climate_ref[0], f32)

    def turned(block):
        ones = jnp.ones((PADDED - FIELDS,) + block.shape[1:], bf16)
        return jnp.swapaxes(jnp.concatenate([block, ones], axis=0), 0, 1)

    zeros = jnp.zeros((8, PADDED, LON), bf16)
    before[0:8] = zeros
    before[72:80] = zeros
    before[pl.ds(jnp.where(role == 0, 72, 0), 8)] = turned(halo_ref[...])

    def take(step):
        place = pl.multiple_of(step * 16, 16)
        before[pl.ds(8 + place, 16)] = turned(own[:, pl.ds(place, 16), :])

    diff = jnp.concatenate([diff_ref[...], jnp.zeros((1, LANES - FIELDS), f32)], axis=1)
    diff = jnp.broadcast_to(diff, (LANES, LANES)).T[:PADDED]
    diff = jnp.concatenate([diff] * TILES, axis=1)
    bias = b_in_ref[...]
    high = bias.astype(bf16)
    middle = (bias - high.astype(f32)).astype(bf16)
    low = (bias - high.astype(f32) - middle.astype(f32)).astype(bf16)
    w_in = jnp.concatenate([w_in_ref[...], high, middle, low], axis=0).astype(f32)
    w_in = jnp.concatenate([w_in, jnp.zeros((LANES - PADDED, LATENT), f32)], axis=0).T[:, :PADDED].astype(bf16)
    w_out = jnp.concatenate(
        [w_out_ref[...] * bf16(0.5), jnp.zeros((PADDED - FIELDS, LATENT), bf16)], axis=0
    )

    for part in range(3):
        fetch_first(part).wait()
    for step in range(1, ROWS // 16):
        fetch(step).start()
    take(0)

    def advance(ref, place, count, give):
        rows, smooth = {}, {}

        def row(k):
            if k not in rows:
                rows[k] = ref[place + k]
            return rows[k].astype(f32)

        def smooth_of(n):
            pieces = []
            for piece in (2 * n, 2 * n + 1):
                k, tile = divmod(piece, TILES)
                if k not in smooth:
                    c = row(k)
                    around = row(k - 1) + row(k + 1) + pltpu.roll(rows[k], 1, 1).astype(f32)
                    around = around + pltpu.roll(rows[k], LON - 1, 1).astype(f32)
                    smooth[k] = (c + diff * (around - 4.0 * c)).astype(bf16)
                pieces.append(smooth[k][:, tile * LANES : (tile + 1) * LANES])
            return jnp.concatenate(pieces, axis=1)

        def done(n, change):
            for half, piece in enumerate((2 * n, 2 * n + 1)):
                k, tile = divmod(piece, TILES)
                lanes = slice(tile * LANES, (tile + 1) * LANES)
                new = rows[k][:, lanes].astype(f32) + change[:, half * LANES : (half + 1) * LANES]
                give(k, tile, new.astype(bf16))

        mlp(count * TILES // 2, smooth_of, done, w_in, w_out)

    def first_rows(start, count):
        def give(k, tile, new):
            after[start + k, :, tile * LANES : (tile + 1) * LANES] = new

        advance(before, start + 7, count, give)

    def first(step, carry):
        first_rows(step * 16, 16)

        @pl.when(step < ROWS // 16 - 1)
        def _():
            fetch(step + 1).wait()
            take(step + 1)

        return carry

    lax.fori_loop(0, ROWS // 16, first, 0)
    first_rows(ROWS, 2)

    @pl.when(role == 0)
    def _():
        after[0] = jnp.zeros((PADDED, LON), bf16)

    @pl.when(role == 1)
    def _():
        after[ROWS + 1] = jnp.zeros((PADDED, LON), bf16)

    def second(step, carry):
        pieces = {}

        def give(k, tile, new):
            pieces[k, tile] = new
            if k % 8 == 7:
                rows = [pieces.pop((k - 7 + a, tile)) for a in range(8)]
                for group, message in enumerate(to_messages(rows)):
                    owner, slot = owner_of(step * 2 + k // 8, tile, group)
                    out_ref[owner, slot * MAIN : (slot + 1) * MAIN, :] = message[:MAIN]
                    rests[owner, slot] = message[MAIN:]

        advance(after, step * 16 + 1, 16, give)
        for half in range(2):
            for u in range(8):
                owner = step * 16 + half * 8 + u
                parts = [rests[owner, slot].astype(f32)[:REST] for slot in range(TILES)]
                tail = jnp.concatenate(parts + [jnp.zeros((1, LANES), f32)], axis=0)
                out_ref[owner, TAIL:MESSAGE, :] = tail.astype(bf16)
        return carry

    lax.fori_loop(0, ROWS // 16, second, 0)


def split(a):
    high = a.astype(jnp.bfloat16)
    return high, (a - high.astype(jnp.float32)).astype(jnp.bfloat16)


def streamed(a):
    high, rest = split(a)
    return jnp.concatenate([high, rest, high], axis=1)


def held(a):
    low = lax.broadcasted_iota(jnp.int32, (MEMBERS, LANES), 1) < MEMBERS
    high, rest = split(jnp.concatenate([jnp.where(low, a, 0.0), jnp.where(low, 0.0, a)], axis=0))
    return jnp.concatenate([high, high, rest], axis=0)


def pair_dot(left, right):
    return jnp.dot(left, right, preferred_element_type=jnp.float32)


def wide_dot(a, b):
    (a_high, a_low), (b_high, b_low) = split(a), split(b)
    left = jnp.concatenate([a_high, a_low, a_high], axis=1)
    right = jnp.concatenate([b_high, b_high, b_low], axis=1)
    return lax.dot_general(left, right, (((1,), (1,)), ((), ())), preferred_element_type=jnp.float32)


def weights_kernel(
    idx_ref, value_ref, weight_ref, g_ref, turn, mix_ref, total_ref
):
    f32, bf16 = jnp.float32, jnp.bfloat16
    lane = lax.broadcasted_iota(jnp.int32, (MEMBERS, LANES), 1)
    low = lane < MEMBERS
    eye = jnp.where(
        (lane & (MEMBERS - 1)) == lax.broadcasted_iota(jnp.int32, (MEMBERS, LANES), 0), 1.0, 0.0
    )
    odd = jnp.where(lax.broadcasted_iota(jnp.int32, (1, 2 * OBS), 1) >= OBS, EDGE, 0)

    def halves(a):
        first = jnp.sum(jnp.where(low[: a.shape[0]], a, 0.0), axis=1, keepdims=True)
        second = jnp.sum(jnp.where(low[: a.shape[0]], 0.0, a), axis=1, keepdims=True)
        return jnp.where(low[: a.shape[0]], first, second)

    def load(step, carry):
        m = pl.multiple_of(step * 16, 16)
        turn[:, pl.ds(m, 16), :] = jnp.swapaxes(g_ref[pl.ds(m, 16)], 0, 1)
        return carry

    lax.fori_loop(0, MEMBERS // 16, load, 0, unroll=4)
    precisions, pulled = [], []
    for k in range(TILES):
        idx = jnp.concatenate(
            [idx_ref[2 * k + e : 2 * k + e + 1, :] for e in range(2)], axis=1
        )
        cell = idx & (CELLS - 1)
        place = (cell >> 3) * GROUP + odd + (cell & 7)
        field = idx >> 6
        hot = jnp.where(lax.broadcasted_iota(jnp.int32, (LANES, 2 * OBS), 0) == place, 1.0, 0.0)
        late = (field & 32) != 0
        both = jnp.concatenate([jnp.where(late, 0.0, hot), jnp.where(late, hot, 0.0)], axis=0)
        hot, both = hot.astype(bf16), both.astype(bf16)
        rest = jnp.broadcast_to(field - MAIN, (MEMBERS, 2 * OBS))
        main = jnp.broadcast_to(jnp.where(field < MAIN, field & 31, -1), (MEMBERS, 2 * OBS))

        def flat(start, count):
            return turn[start : start + count].reshape(count * MEMBERS, LANES)

        def pick(total, values, wanted, first, count):
            for f in range(count):
                here = wanted == first + f
                total = jnp.where(here, values[f * MEMBERS : (f + 1) * MEMBERS], total)
            return total

        values = jnp.dot(flat(TAIL + k * REST, REST), hot, preferred_element_type=f32)
        observed = pick(jnp.zeros((MEMBERS, 2 * OBS), f32), values, rest, 0, REST)
        for first in range(0, 32, 8):
            start = k * MAIN + first
            block = jnp.concatenate([flat(start, 8), flat(start + 32, 8)], axis=1)
            values = jnp.dot(block, both, preferred_element_type=f32)
            observed = pick(observed, values, main, first, 8)
        sides, pulls = [], []
        for e in range(2):
            mine = observed[:, e * OBS : (e + 1) * OBS]
            row = slice(2 * k + e, 2 * k + e + 1)
            obs_mean = jnp.sum(mine, axis=0, keepdims=True) * (1.0 / MEMBERS)
            spread = mine - obs_mean
            weighted = spread * weight_ref[row, :]
            sides.append(wide_dot(weighted, spread))
            pulls.append(jnp.sum(weighted * (value_ref[row, :] - obs_mean), axis=1, keepdims=True))
        precisions.append(jnp.concatenate(sides, axis=1) + (MEMBERS - 1.0) * eye)
        pulled.append(jnp.where(low, pulls[0], pulls[1]))

    scales = [MEMBERS * halves(jnp.sum(p * eye, axis=0, keepdims=True)) for p in precisions]
    iterates = [p / s for p, s in zip(precisions, scales)]

    def newton(step, carry):
        iterates, roots = carry
        rights = [held(i) for i in iterates]
        products = [pair_dot(streamed(r), i) for r, i in zip(roots, rights)]
        rights = [jnp.concatenate([i, held(r)], axis=1) for i, r in zip(rights, roots)]
        factors = [0.5 * (3.0 * eye - p) for p in products]
        new = [pair_dot(streamed(f), r) for f, r in zip(factors, rights)]
        return [n[:, :LANES] for n in new], [n[:, LANES:] for n in new]

    factors = [0.5 * (3.0 * eye - i) for i in iterates]
    iterates = [pair_dot(streamed(f), held(i)) for f, i in zip(factors, iterates)]
    iterates, roots = lax.fori_loop(
        1, NS_ITERS - 1, newton, (iterates, factors), unroll=NS_ITERS - 2
    )
    products = [pair_dot(streamed(r), held(i)) for r, i in zip(roots, iterates)]
    factors = [0.5 * (3.0 * eye - p) for p in products]
    roots = [pair_dot(streamed(f), held(r)) for f, r in zip(factors, roots)]
    shifts = [pair_dot(streamed(r), held(p)) for r, p in zip(roots, pulled)]
    shifts = [pair_dot(streamed(r), held(p)) for r, p in zip(roots, shifts)]
    total = jnp.zeros((1, LANES), f32)
    odd_cell = (lane & EDGE) != 0
    for k, (root, shift, scale) in enumerate(zip(roots, shifts, scales)):
        combined = jnp.sqrt((MEMBERS - 1.0) / scale) * root + shift / scale
        rest = (1.0 - jnp.sum(combined, axis=0, keepdims=True)) * (1.0 / MEMBERS)
        mix = combined + rest
        across = mix.T
        across = jnp.concatenate([across[:MEMBERS], across[MEMBERS:]], axis=1)
        mix_ref[k] = jnp.concatenate(split(across), axis=1)
        shares = jnp.where(
            odd_cell,
            jnp.sum(jnp.where(low, 0.0, mix), axis=1, keepdims=True),
            jnp.sum(jnp.where(low, mix, 0.0), axis=1, keepdims=True),
        )
        total = total + jnp.sum(shares * turn[k * MAIN].astype(f32), axis=0, keepdims=True)
    total_ref[...] = jnp.sum(total, axis=1, keepdims=True)


def apply_kernel(mix_ref, turn, out_ref, back):
    f32, bf16 = jnp.float32, jnp.bfloat16
    even = jnp.where((lax.broadcasted_iota(jnp.int32, (MEMBERS, BLOCK), 1) & EDGE) == 0, 1.0, 0.0)
    even = even.astype(bf16)
    uneven = bf16(1.0) - even
    def mixed(k, places):
        x = jnp.concatenate([turn[place] for place in places], axis=1)
        width = len(places) * LANES
        x = jnp.concatenate([x * even[:, :width], x * uneven[:, :width]], axis=0)
        x = jnp.concatenate([x, x], axis=0)
        new = jnp.dot(mix_ref[k], x, preferred_element_type=f32).astype(bf16)
        for n, place in enumerate(places):
            back[place] = new[:, n * LANES : (n + 1) * LANES]

    def main(k, step):
        for pair in range(8):
            place = k * MAIN + step * 16 + 2 * pair
            mixed(k, [place, place + 1])

    def give(first, count, step):
        members = pl.ds(pl.multiple_of(step * 16, 16), 16)
        block = jnp.swapaxes(back[first : first + count, members, :], 0, 1)
        out_ref[members, first : first + count, :] = block

    for k in range(TILES):
        for place in range(TAIL + k * REST, TAIL + (k + 1) * REST, 2):
            mixed(k, [p for p in (place, place + 1) if p < TAIL + (k + 1) * REST])

    for k in range(TILES + 1):

        def both(step, carry):
            if k < TILES:
                main(k, step)
            if k > 0:
                give((k - 1) * MAIN, MAIN, step)
            else:
                give(TAIL, MESSAGE - TAIL, step)
            return carry

        lax.fori_loop(0, 4, both, 0, unroll=4)


def seal_kernel(climate_ref, total_ref, other_ref, messages_ref, out_ref):
    f32, bf16 = jnp.float32, jnp.bfloat16
    total = total_ref[...] + other_ref[...] - climate_ref[...] * (VALUES // MEMBERS)
    high = total.astype(bf16).astype(f32)
    middle = (total - high).astype(bf16).astype(f32)
    lane = lax.broadcasted_iota(jnp.int32, (16, LANES), 1)
    row = lax.broadcasted_iota(jnp.int32, (16, LANES), 0)
    parts = jnp.where(lane == 0, high, jnp.where(lane == 1, middle, total - high - middle))
    parts = jnp.where(lane < 3, parts, 0.0).astype(bf16)
    for owner in range(MEMBERS):
        tail = messages_ref[owner, TAIL:MESSAGE, :]
        out_ref[owner, TAIL:MESSAGE, :] = jnp.where(row == 15, parts, tail)


def last_kernel(back_ref, out_ref, grid, sems):
    f32, bf16 = jnp.float32, jnp.bfloat16

    def send(first, count):
        fields = pl.ds(first, count)
        return pltpu.make_async_copy(grid.at[fields], out_ref.at[fields], sems.at[first // 16])

    totals = jnp.zeros((MESSAGE - TAIL, LANES), f32)
    for owner in range(MEMBERS):
        totals = totals + back_ref[owner, TAIL:MESSAGE, :].astype(f32)
    offset = jnp.sum(totals[MESSAGE - TAIL - 1 :], axis=1, keepdims=True) / -VALUES

    def piece(owner, slot, first, count):
        if first < MAIN:
            return back_ref[owner, slot * MAIN + first : slot * MAIN + first + count, :]
        rest = back_ref[owner, TAIL:MESSAGE, :].astype(f32)
        return rest[slot * REST : (slot + 1) * REST].astype(bf16)

    chunks = [(first, min(16, FIELDS - first)) for first in range(0, FIELDS, 16)]
    for first, count in chunks:

        def block(step, carry):
            for tile in range(TILES):
                rows = []
                for half in range(2):
                    pieces = []
                    for group in range(8):
                        owner, slot = owner_of(step * 2 + half, tile, group)
                        pieces.append(piece(owner, slot, first, count))
                    rows += to_rows(pieces)
                values = jnp.swapaxes(jnp.stack(rows), 0, 1)
                place = pl.ds(pl.multiple_of(step * 16, 16), 16)
                lanes = slice(tile * LANES, (tile + 1) * LANES)
                if first == 0:
                    grid[0:1, place, lanes] = (values[:1].astype(f32) + offset).astype(bf16)
                    grid[1:count, place, lanes] = values[1:]
                else:
                    grid[first : first + count, place, lanes] = values
            return carry

        lax.fori_loop(0, ROWS // 16, block, 0, unroll=4)
        send(first, count).start()
    for first, count in chunks:
        send(first, count).wait()


MESSAGES = jax.ShapeDtypeStruct((MEMBERS, MESSAGE, LANES), jnp.bfloat16)
TURNED = jax.ShapeDtypeStruct((MESSAGE, MEMBERS, LANES), jnp.bfloat16)


def forecast(role, climate, x, halo, diff, w_in, b_in, w_out):
    cells = 2 * ROWS * LON
    return pl.pallas_call(
        forecast_kernel,
        out_shape=(MESSAGES, jax.ShapeDtypeStruct((1, LANES), jnp.float32)),
        in_specs=[IN_SMEM, IN_SMEM, IN_HBM] + [IN_VMEM] * 5,
        out_specs=(IN_VMEM, IN_VMEM),
        scratch_shapes=[
            pltpu.VMEM((FIELDS, ROWS, LON), jnp.bfloat16),
            pltpu.VMEM((ROWS + 16, PADDED, LON), jnp.bfloat16),
            pltpu.VMEM((ROWS + 2, PADDED, LON), jnp.bfloat16),
            pltpu.VMEM((MEMBERS, TILES, PADDED - MAIN, LANES), jnp.bfloat16),
            pltpu.SemaphoreType.DMA((ROWS // 16,)),
            pltpu.SemaphoreType.DMA((3,)),
        ],
        compiler_params=params(32),
        cost_estimate=cost(cells * LATENT * 256 * 4, 7 << 20, cells * LATENT),
        name="forecast",
    )(role, climate, in_hbm(x), halo, in_hbm(diff), in_hbm(w_in), in_hbm(b_in), in_hbm(w_out))


def weights(idx, value, weight, g):
    return pl.pallas_call(
        weights_kernel,
        out_shape=(
            TURNED,
            jax.ShapeDtypeStruct((TILES, MEMBERS, 2 * LANES), jnp.bfloat16),
            jax.ShapeDtypeStruct((1, 1), jnp.float32),
        ),
        in_specs=[IN_VMEM] * 4,
        out_specs=(IN_VMEM,) * 3,
        compiler_params=params(32),
        cost_estimate=cost(8 << 30, 7 << 20),
        name="weights",
    )(idx, value, weight, g)


def apply(mixes, turn):
    return pl.pallas_call(
        apply_kernel,
        out_shape=MESSAGES,
        in_specs=[IN_VMEM] * 2,
        out_specs=IN_VMEM,
        scratch_shapes=[pltpu.VMEM(TURNED.shape, jnp.bfloat16)],
        compiler_params=params(32),
        cost_estimate=cost(8 << 30, 7 << 20),
        name="apply",
    )(mixes, turn)


def seal(climate, total, other, messages):
    return pl.pallas_call(
        seal_kernel,
        out_shape=MESSAGES,
        in_specs=[IN_VMEM] * 4,
        out_specs=IN_VMEM,
        input_output_aliases={3: 0},
        compiler_params=params(32),
        cost_estimate=cost(1 << 16, 1 << 18),
        name="seal",
    )(climate, total, other, messages)


def put_back(back):
    return pl.pallas_call(
        last_kernel,
        out_shape=jax.ShapeDtypeStruct((FIELDS, ROWS, LON), jnp.bfloat16),
        in_specs=[IN_VMEM],
        out_specs=IN_HBM,
        scratch_shapes=[
            pltpu.VMEM((FIELDS, ROWS, LON), jnp.bfloat16),
            pltpu.SemaphoreType.DMA((PADDED // 16 + 1,)),
        ],
        compiler_params=params(50),
        cost_estimate=cost(1 << 20, 7 << 20),
        name="put_back",
    )(back)


def exchange(messages):
    return lax.all_to_all(messages, "dev", split_axis=0, concat_axis=0, tiled=True)


def body(
    initial_realizations, diffusivity, w_in, b_in, w_out, obs_index, obs_value, obs_weight, climate
):
    role = lax.axis_index("role")
    dev = lax.axis_index("dev")
    x = initial_realizations.reshape(FIELDS, ROWS, LON)
    index = lax.dynamic_slice_in_dim(obs_index, dev * PATCHES, PATCHES, 0)
    group = dev % 8 * 3 + jnp.arange(PATCHES)[:, None] // 2
    index = (index & ~(CELLS - EDGE)) | ((index + group * EDGE) & (CELLS - EDGE))
    edge = lax.dynamic_slice_in_dim(x, jnp.where(role == 0, ROWS - 8, 0), 8, 1)
    halo = lax.ppermute(edge, "role", [(0, 1), (1, 0)])
    halo, index = lax.optimization_barrier((halo, index))
    sent, climate = forecast(
        role.reshape(1), climate, x, halo, diffusivity.reshape(1, FIELDS), w_in.T, b_in.reshape(1, LATENT), w_out
    )
    got = exchange(sent)
    turn, mixes, total = weights(index, obs_value, obs_weight, got)
    other = lax.ppermute(total, "role", [(0, 1), (1, 0)])
    back = exchange(seal(climate, total, other, apply(mixes, turn)))
    return put_back(back)[None]


def solution(mesh):
    in_specs = (
        P("dev", None, "role", None),
        P(),
        P(),
        P(),
        P(),
        P("role", None),
        P(("role", "dev"), None),
        P(("role", "dev"), None),
        P(),
    )
    out_specs = P("dev", None, "role", None)
    return jax.shard_map(body, mesh=mesh, in_specs=in_specs, out_specs=out_specs, check_vma=False)
```
